32 devices in a mesh: section: 2 (over y), grp: 2 (over x), dp: 8 (over z, core).
Axes of the slice: x: 2, y: 2, z: 4, core: 2. Of those that a mesh axis runs over, the one named last changes fastest.
Arguments:
- embedded: bfloat16 [2, 16, 256, 768], P(None, ('grp', 'dp')), may hold values from -6 to 6
- lengths: int32 [2, 16], P(None, ('grp', 'dp')), may hold values from 64 to 256, as said below
- token_grads: bfloat16 [2, 16, 256, 768], P(None, ('grp', 'dp')), may hold values from -6 to 6
- score_grads: float32 [2, 16], P(None, ('grp', 'dp')), may hold values from -6 to 6
- w_qkv: bfloat16 [2, 768, 2304], P('section', 'dp'), may hold values from -0.21875 to 0.21875
- w_attn_out: bfloat16 [2, 768, 768], P('section', 'dp'), may hold values from -0.875 to 0.875
- w_up: bfloat16 [2, 768, 3072], P('section', 'dp'), may hold values from -0.21875 to 0.21875
- w_down: bfloat16 [2, 3072, 768], P('section', 'dp'), may hold values from -0.109375 to 0.109375
- biases: float32 [2, 7680], P('section'), may hold values from -1.5 to 1.5
- gains: float32 [2, 2, 768], P('section'), may hold values from 0.25 to 1.75
- head_weight: float32 [768], replicated, may hold values from -5 to 5
Outputs:
- section_out: bfloat16 [2, 2, 16, 256, 768], P('section', None, ('grp', 'dp'))
- grad_in: float32 [2, 2, 16, 256, 768], P('section', None, ('grp', 'dp'))
- grad_qkv: float32 [2, 768, 2304], P('section', 'dp')
- grad_attn_out: float32 [2, 768, 768], P('section', 'dp')
- grad_up: float32 [2, 768, 3072], P('section', 'dp')
- grad_down: float32 [2, 3072, 768], P('section', 'dp')
- grad_biases: float32 [2, 7680], P('section')
- grad_gains: float32 [2, 2, 768], P('section')
- grad_head: float32 [768], replicated
The draws below stay inside these ranges and needn't reach their ends.
Inputs may be any that keep to these rules, and one draw needn't show every extreme that they name: `lengths`: token count of each pair; some pair has exactly 256.
All inputs are finite; a program needn't handle non-finite values.
Results may differ from the reference program's by a relative error of at most 0.023.
Values may be sent and summed in bfloat16 or wider, within the bound.
A program may use at most 192 MiB of HBM per device.

```python
import math
import jax
import jax.numpy as jnp
from jax import lax

D = 768
FF = 3072
HEADS = 12
HEAD = 64
SEQ = 256
MICRO = 2
LAYERS_SECTION = 1
PAIRS_MB = 16
LAYERS = 2
BIAS_W = 7680
N_SECTION = 2


def draw_lengths(key, part):
    key = jax.random.fold_in(key, 7)
    first_key, second_key = jax.random.split(key)
    drawn_lengths = jax.random.randint(first_key, (MICRO * PAIRS_MB,), SEQ // 4, SEQ + 1)
    longest = jax.random.randint(second_key, (), 0, MICRO * PAIRS_MB)
    return drawn_lengths.at[longest].set(SEQ).reshape(MICRO, PAIRS_MB).astype(jnp.int32)


def block_scale(key, extent, cuts, smallest, top_value):
    def one(dim, blocks):
        steps = jax.random.uniform(jax.random.fold_in(jax.random.fold_in(key, 6), dim), (blocks,), jnp.float32, smallest / len(cuts), top_value / len(cuts))
        return jnp.repeat(jnp.exp(steps), extent[dim] // blocks).reshape((-1,) + (1,) * (len(extent) - dim - 1))

    gain = one(*cuts[0])
    for cut in cuts[1:]:
        gain = gain * one(*cut)
    return gain


def scatter_about(rng, shape, spread, bound, cuts=(), held_as=jnp.bfloat16):
    values = jax.random.normal(rng, shape, jnp.float32) * spread
    if len(cuts) > 0:
        values = block_scale(rng, shape, cuts, -0.22, 0.18) * values
    return jnp.clip(values, min=-bound, max=bound).astype(held_as)


def setup_inputs(seed: int = 0) -> dict:
    seeds = jax.random.split(jax.random.key(seed), 12)
    return {
        "embedded": scatter_about(seeds[0], (MICRO, PAIRS_MB, SEQ, D), 1.0, 6.0, ((1, 16),)),
        "lengths": draw_lengths(jax.random.fold_in(seeds[11], 71), 0),
        "token_grads": scatter_about(seeds[2], (MICRO, PAIRS_MB, SEQ, D), 1.0, 6.0, ((1, 16),)),
        "score_grads": scatter_about(seeds[3], (MICRO, PAIRS_MB), 1.0, 6.0, ((1, 16),), jnp.float32),
        "w_qkv": scatter_about(seeds[4], (LAYERS, D, 3 * D), D ** -0.5, 0.21875, ((0, 2), (1, 8))),
        "w_attn_out": scatter_about(seeds[5], (LAYERS, D, D), (D // 16) ** -0.5, 0.875, ((0, 2), (1, 8))),
        "w_up": scatter_about(seeds[6], (LAYERS, D, FF), D ** -0.5, 0.21875, ((0, 2), (1, 8))),
        "w_down": scatter_about(seeds[7], (LAYERS, FF, D), FF ** -0.5, 0.109375, ((0, 2), (1, 8))),
        "biases": scatter_about(seeds[8], (LAYERS, BIAS_W), 0.3, 1.5, ((0, 2),), jnp.float32),
        "gains": jnp.clip(1.0 + 0.15 * jax.random.normal(seeds[9], (LAYERS, 2, D), jnp.float32), 0.25, 1.75),
        "head_weight": scatter_about(seeds[10], (D,), 1.0, 5.0, (), jnp.float32),
    }


PRECISE = lax.Precision.HIGHEST
EPSILON = 1e-06

@jax.custom_vjp
def low(v):
    return lax.optimization_barrier(v.astype(jnp.bfloat16)).astype(jnp.float32)

@jax.custom_vjp
def low_back(v):
    return v

def low_keep(v):
    return (low(v), None)

def low_pass(kept, grad):
    return (grad,)

def back_keep(v):
    return (v, None)

def back_low(kept, grad):
    return (low(grad),)
low.defvjp(low_keep, low_pass)
low_back.defvjp(back_keep, back_low)

def norm_rows(row_vals, gain_row, shift_row):
    row_mean = lax.optimization_barrier(jnp.mean(row_vals, -1, keepdims=True))
    centred = row_vals - row_mean
    row_var = lax.optimization_barrier(jnp.mean(centred * centred, -1, keepdims=True))
    return centred * lax.rsqrt(row_var + EPSILON) * gain_row + shift_row

def split_bias(bias_row):
    bounds_list = [0, D, 2 * D, 3 * D, 3 * D + FF, 4 * D + FF, 5 * D + FF, 6 * D + FF]
    return [bias_row[bounds_list[piece_num]:bounds_list[piece_num + 1]] for piece_num in range(7)]

def layer(hidden, valid_mask, w_qkv, w_attn, w_up, w_down, bias_row, gain_row):
    pair_count, seq_len = (hidden.shape[0], hidden.shape[1])
    q_bias, v_bias, o_bias, up_bias, down_bias, shift_one, shift_two = split_bias(bias_row)
    joint_bias = jnp.concatenate([q_bias, jnp.zeros((D,), jnp.float32), v_bias])
    qkv_vals = low_back(low(jnp.einsum('bsd,de->bse', low(hidden), w_qkv, precision=PRECISE) + joint_bias))
    query_heads = qkv_vals[..., 0:D].reshape(pair_count, seq_len, HEADS, HEAD)
    key_heads = qkv_vals[..., D:2 * D].reshape(pair_count, seq_len, HEADS, HEAD)
    value_heads = qkv_vals[..., 2 * D:3 * D].reshape(pair_count, seq_len, HEADS, HEAD)
    raw_scores = low_back(jnp.einsum('bqhd,bkhd->bhqk', query_heads, key_heads, precision=PRECISE) * (1.0 / math.sqrt(HEAD)))
    masked = jnp.where(valid_mask[:, None, None, :], raw_scores, -1e+30)
    row_top = lax.optimization_barrier(jnp.max(masked, -1, keepdims=True))
    exp_scores = jnp.exp(masked - row_top)
    prob_rows = exp_scores / lax.optimization_barrier(jnp.sum(exp_scores, -1, keepdims=True))
    mixed_heads = jnp.einsum('bhqk,bkhd->bqhd', low(prob_rows), value_heads, precision=PRECISE).reshape(pair_count, seq_len, D)
    attn_out = low_back(jnp.einsum('bsd,de->bse', low_back(low(mixed_heads)), w_attn, precision=PRECISE) + o_bias)
    first_norm = norm_rows(hidden + attn_out, gain_row[0], shift_one)
    inner_pre = low_back(jnp.einsum('bsd,df->bsf', low(first_norm), w_up, precision=PRECISE) + up_bias)
    act_vals = low(jax.nn.gelu(inner_pre, approximate=False))
    ff_out = low_back(jnp.einsum('bsf,fd->bsd', act_vals, w_down, precision=PRECISE) + down_bias)
    return norm_rows(first_norm + ff_out, gain_row[1], shift_two)

def group_forward(params, embedded, probes, valid_mask):
    w_qkv, w_attn, w_up, w_down, biases, gains, head_weight = params
    hidden = embedded
    section_vals = []
    for section_num in range(N_SECTION):
        for inner_num in range(LAYERS_SECTION):
            layer_num = section_num * LAYERS_SECTION + inner_num
            hidden = layer(hidden, valid_mask, w_qkv[layer_num], w_attn[layer_num], w_up[layer_num], w_down[layer_num], biases[layer_num], gains[layer_num])
        if section_num + 1 < N_SECTION:
            hidden = low_back(low(hidden))
            section_vals.append(hidden)
            hidden = hidden + probes[section_num]
        else:
            section_vals.append(hidden)
    pair_scores = jnp.einsum('gd,d->g', hidden[:, 0, :], head_weight, precision=PRECISE)
    return (jnp.stack(section_vals, 0), pair_scores)

def reference(embedded, lengths, token_grads, score_grads, w_qkv, w_attn_out, w_up, w_down, biases, gains, head_weight):
    pair_total = MICRO * PAIRS_MB
    group_size = math.gcd(pair_total, max(1, 4096 // SEQ))
    group_count = pair_total // group_size
    positions = jnp.arange(SEQ, dtype=jnp.int32)
    valid_mask = (positions[None, :] < lengths.reshape(pair_total, 1).astype(jnp.int32)).reshape(group_count, group_size, SEQ)
    flat_in = embedded.astype(jnp.float32).reshape(group_count, group_size, SEQ, D)
    probes = jnp.zeros((group_count, N_SECTION - 1, group_size, SEQ, D), jnp.float32)
    params = (w_qkv.astype(jnp.float32), w_attn_out.astype(jnp.float32), w_up.astype(jnp.float32), w_down.astype(jnp.float32), biases, gains, head_weight)
    checked = jax.checkpoint(group_forward)

    def whole(params, flat_in, probes):

        def scan_step(scan_carry, group_data):
            return (scan_carry, checked(params, group_data[0], group_data[1], group_data[2]))
        return lax.scan(scan_step, jnp.zeros((), jnp.float32), (flat_in, probes, valid_mask))[1]
    (section_vals, pair_scores), pullback = jax.vjp(whole, params, flat_in, probes)
    row_mask = valid_mask[..., None].astype(jnp.float32)
    final_cot = token_grads.astype(jnp.float32).reshape(group_count, group_size, SEQ, D) * row_mask
    section_cot = jnp.zeros_like(section_vals).at[:, N_SECTION - 1].set(final_cot)
    score_cot = score_grads.reshape(group_count, group_size)
    d_params, d_in, d_probes = pullback((section_cot, score_cot))
    section_out = jnp.moveaxis(section_vals, 1, 0).reshape(N_SECTION, MICRO, PAIRS_MB, SEQ, D).astype(jnp.bfloat16)
    grads_joined = jnp.concatenate([d_in[:, None], d_probes], 1)
    grad_in = jnp.moveaxis(grads_joined, 1, 0).reshape(N_SECTION, MICRO, PAIRS_MB, SEQ, D)
    return (section_out, grad_in, d_params[0], d_params[1], d_params[2], d_params[3], d_params[4], d_params[5], d_params[6])
```

```python
import functools
import math

import jax
import jax.numpy as jnp
from jax import lax
from jax.experimental import pallas as pl
from jax.experimental.pallas import tpu as pltpu
from jax.sharding import PartitionSpec as P

D = 768
FF = 3072
HEADS = 12
HEAD = 64
EPSILON = 1e-06
CHUNKS = 12
HALF = D // 2
DOWN = 8 * D
DOWN_GRAD = 12 * D
SCALE = 1.0 / math.sqrt(HEAD)
F32 = jnp.float32
BF = jnp.bfloat16
MESH = pl.DeviceIdType.MESH
BQ, BV, BO, BU, BD, BETA1, BETA2, GAIN1, GAIN2, HEAD_ROW = 0, 1, 2, 3, 7, 8, 9, 10, 11, 12
SMALL = 16


def dot(a, b):
    return lax.dot_general(a, b, (((1,), (0,)), ((), ())), preferred_element_type=F32)


def dot_t(a, b):
    return lax.dot_general(a, b, (((1,), (1,)), ((), ())), preferred_element_type=F32)


def dot_c(a, b):
    return lax.dot_general(a, b, (((0,), (0,)), ((), ())), preferred_element_type=F32)


def span(i, width):
    return pl.ds(pl.multiple_of(i * width, width), width)


def row_sum(x):
    return jnp.sum(x, 0, keepdims=True)


def gelu_parts(x):
    t = 1.0 / (1.0 + (0.3275911 * math.sqrt(0.5)) * jnp.abs(x))
    e = jnp.exp(-0.5 * x * x)
    tail = t * (0.127414796 + t * (-0.142248368 + t * (0.7107068705 + t * (-0.7265760135 + t * 0.5307027145)))) * e
    phi = jnp.where(x >= 0, 1.0 - tail, tail)
    return x * phi, phi + x * (e * (1.0 / math.sqrt(2.0 * math.pi)))


def normed(x):
    centred = x - jnp.mean(x, -1, keepdims=True)
    scale = lax.rsqrt(jnp.mean(centred * centred, -1, keepdims=True) + EPSILON)
    return centred * scale, scale


def norm_back(grad, n, scale, gain):
    gg = gain * grad
    return (gg - jnp.mean(gg, -1, keepdims=True) - n * jnp.mean(gg * n, -1, keepdims=True)) * scale


def kernel(sizes, *refs):
    groups, depth, rs, seq = sizes
    (emb, token_grads, wq_in, wo_in, wu_in, wd_in, lens, scores, bias, gains, head_w,
     out_sec, out_gin, out_q, out_o, out_u, out_d, out_small,
     big, s1, xr, zr, fin, peers,
     hbuf, qkv, probs, mixed, n1, r1, first_low, act, gp, n2, r2, outb, gbuf, high, dd, da, dm, dqkv,
     small, sm_sib, sm_grp, sm_dp, sm_sec,
     local_sem, io_sem, g_zr, g_xr, g_sr, g_send, y_send, y_recv,
     r_send, r_sib, r_x, r_z, r_fin, r_peer, sm_send, sm_recv) = refs
    pairs = 2
    sec = lax.axis_index("section")
    g = lax.axis_index("grp")
    d = lax.axis_index("dp")
    z, c = d // 2, d % 2
    par = g % 2
    first_section = sec == 0

    def dev(sec_=None, g_=None, z_=None, c_=None):
        return (
            sec if sec_ is None else sec_,
            g if g_ is None else g_,
            (z if z_ is None else z_) * 2 + (c if c_ is None else c_),
        )

    sibling = dev(c_=1 - c)
    across = dev(g_=g + 1 - 2 * par)
    other = dev(sec_=1 - sec)

    def rcopy(src, dst, send, recv, to):
        return pltpu.make_async_remote_copy(
            src_ref=src, dst_ref=dst, send_sem=send, recv_sem=recv, device_id=to, device_id_type=MESH
        )

    def shard_row(m, owner, down=DOWN):
        row = jnp.where(m < 8, m * D + owner * rs, down + owner * (4 * rs) + (m - 8) * rs)
        return pl.multiple_of(row, 16)

    barrier = pltpu.get_barrier_semaphore()
    greeted = 0
    for to in [sibling, other]:
        pl.semaphore_signal(barrier, inc=1, device_id=to, device_id_type=MESH)
        greeted += 1
    for k in range(1, groups):
        pl.semaphore_signal(barrier, inc=1, device_id=dev(g_=(g + k) % groups), device_id_type=MESH)
        greeted += 1
    for k in range(1, depth):
        pl.semaphore_signal(barrier, inc=1, device_id=dev(z_=(z + k) % depth), device_id_type=MESH)
        greeted += 1

    own = []
    for k in range(3):
        own.append((wq_in.at[:, pl.ds(k * D, D)], k))
    own.append((wo_in, 3))
    for k in range(4):
        own.append((wu_in.at[:, pl.ds(k * D, D)], 4 + k))
    for src, k in own:
        pltpu.make_async_copy(src, big.at[pl.ds(pl.multiple_of(k * D + d * rs, 16), rs), :], local_sem.at[0]).start()
    pltpu.make_async_copy(
        wd_in, big.at[pl.ds(pl.multiple_of(DOWN + d * 4 * rs, 16), 4 * rs), :], local_sem.at[0]
    ).start()

    @pl.when(first_section)
    def _():
        pltpu.make_async_copy(emb, hbuf, local_sem.at[1]).start()

    @pl.when(~first_section)
    def _():
        pltpu.make_async_copy(token_grads, gbuf, local_sem.at[1]).start()

    small[...] = jnp.zeros_like(small)
    pl.semaphore_wait(barrier, greeted)
    pltpu.make_async_copy(
        big.at[pl.ds(0, CHUNKS * rs), :], big.at[pl.ds(0, CHUNKS * rs), :], local_sem.at[0]
    ).wait()

    def region(m, zz, half=None, cc=c):
        cols = slice(None) if half is None else span(half, HALF)
        return big.at[pl.ds(shard_row(m, 2 * zz + cc), rs), cols]

    def along(m, zz, to):
        part = region(m, zz, par)
        return rcopy(part, part, g_send.at[0], g_zr.at[m, zz], dev(z_=to))

    def over(m, zz, half):
        part = region(m, zz, half)
        return rcopy(part, part, g_send.at[1], g_xr.at[m, zz], across)

    def beside(m, zz, half):
        part = region(m, zz, half)
        return rcopy(part, part, g_send.at[2], g_sr.at[m], sibling)

    def bias_row(start, width=D):
        return bias[:, pl.ds(start, width)]

    low = lax.broadcasted_iota(jnp.int32, (1, 128), 1) < HEAD
    key = lax.broadcasted_iota(jnp.int32, (1, seq), 1)

    def pair_rows(p):
        return span(p, seq)

    def block(k):
        return big[pl.ds(k * D, D), :]

    def project(p, k):
        r = pair_rows(p)
        x = dot(hbuf[r, :], block(k))
        if k != 1:
            x = x + bias_row(0 if k == 0 else D)
        qkv[r, pl.ds(k * D, D)] = x.astype(BF)

    def attend(p):
        r = pair_rows(p)
        ok = key < lens[p]
        for j in range(HEADS // 2):
            q2 = qkv[r, pl.ds(j * 128, 128)]
            k2 = qkv[r, pl.ds((j + 6) * 128, 128)]
            v2 = qkv[r, pl.ds((j + 12) * 128, 128)]
            none = jnp.zeros_like(q2)
            both = jnp.concatenate([jnp.where(low, q2, none), jnp.where(low, none, q2)], 0)
            sc = jnp.where(ok, dot_t(both, k2) * SCALE, -1e30)
            e = jnp.exp(sc - jnp.max(sc, -1, keepdims=True))
            pr = (e * (1.0 / jnp.sum(e, -1, keepdims=True))).astype(BF)
            probs[p * HEADS + 2 * j] = pr[:seq]
            probs[p * HEADS + 2 * j + 1] = pr[seq:]
            o = dot(pr, v2)
            mixed[r, pl.ds(j * 128, 128)] = jnp.where(low, o[:seq], o[seq:]).astype(BF)

    def join(p):
        r = pair_rows(p)
        n, scale = normed(hbuf[r, :].astype(F32) + dot(mixed[r, :], block(3)) + bias_row(2 * D))
        n1[r, :] = n.astype(BF)
        r1[r, :] = scale
        y = n * gains[0:1, :] + bias_row(4 * D + FF)
        high[r, :] = y
        first_low[r, :] = y.astype(BF)

    def widen(p, k):
        r = pair_rows(p)
        for t in range(3):
            w = big[pl.ds((4 + k) * D, D), pl.ds(t * 256, 256)]
            col = k * D + t * 256
            a, dg = gelu_parts(dot(first_low[r, :], w) + bias_row(3 * D + col, 256))
            act[r, pl.ds(col, 256)] = a.astype(BF)
            gp[r, pl.ds(col, 256)] = dg.astype(BF)

    def narrow(p):
        r = pair_rows(p)
        n, scale = normed(high[r, :] + dot(act[r, :], big[pl.ds(DOWN, FF), :]) + bias_row(3 * D + FF))
        n2[r, :] = n.astype(BF)
        r2[r, :] = scale
        y = n * gains[1:2, :] + bias_row(5 * D + FF)
        outb[r, :] = y.astype(BF)

        @pl.when(~first_section)
        def _():
            small[pl.ds(HEAD_ROW, 1), :] += scores[p] * y[0:1]

    def state_copy(p):
        r = pair_rows(p)
        return rcopy(outb.at[r, :], hbuf.at[r, :], y_send.at[0], y_recv.at[p], other)

    def chunk_ready(m):
        whole = big.at[pl.ds(0, depth * rs), :]
        rcopy(whole, whole, g_send.at[2], g_sr.at[m], sibling).wait_recv()

    def own_step(n):
        @pl.when(z > 0)
        def _():
            along(n, z, z - 1).start()

        @pl.when(z < depth - 1)
        def _():
            along(n, z, z + 1).start()

        beside(n, z, None).start()

    def early(step, pieces):
        def run(n):
            @pl.when(first_section & (n == depth + 1 + step))
            def _():
                pieces()

        return run

    def both_pairs(piece):
        @pl.loop(0, pairs)
        def _(p):
            piece(p)

    def early_project(k):
        if k == 0:
            pltpu.make_async_copy(emb, hbuf, local_sem.at[1]).wait()
        chunk_ready(k)
        both_pairs(lambda p: project(p, k))

    def early_join():
        chunk_ready(3)
        both_pairs(join)

    def early_widen(k):
        chunk_ready(4 + k)
        both_pairs(lambda p: widen(p, k))

    plan = [early(k, functools.partial(early_project, k)) for k in range(3)]
    plan.append(early(3, lambda: attend(0)))
    plan.append(early(4, lambda: attend(1)))
    plan.append(early(5, early_join))
    plan += [early(5 + k, functools.partial(early_widen, k)) for k in range(4)]

    @pl.loop(0, CHUNKS + depth)
    def _(n):
        @pl.when(n < CHUNKS)
        def _():
            own_step(n)

        for t in range(1, depth):
            m = n - t
            here = (m >= 0) & (m < CHUNKS)
            for sign in (1, -1):
                zz = z + sign * t

                @pl.when(here & (zz >= 0) & (zz < depth))
                def _(m=m, zz=zz, sign=sign):
                    along(m, zz, z).wait_recv()

                    @pl.when((z - sign >= 0) & (z - sign < depth))
                    def _():
                        along(m, zz, z - sign).start()

                    over(m, zz, par).start()
                    beside(m, zz, par).start()

        for t in range(1, depth):
            m = n - t - 1
            here = (m >= 0) & (m < CHUNKS)
            for sign in (1, -1):
                zz = z + sign * t

                @pl.when(here & (zz >= 0) & (zz < depth))
                def _(m=m, zz=zz):
                    over(m, zz, 1 - par).wait_recv()
                    beside(m, zz, 1 - par).start()

        for run in plan:
            run(n)

    @pl.loop(jnp.where(first_section, 8, 0), CHUNKS)
    def _(m):
        chunk_ready(m)

    @pl.when(first_section)
    def _():
        @pl.loop(0, pairs)
        def _(p):
            narrow(p)
            state_copy(p).start()

    @pl.when(~first_section)
    def _():
        pltpu.make_async_copy(token_grads, gbuf, local_sem.at[1]).wait()

        @pl.loop(0, pairs)
        def _(p):
            state_copy(p).wait_recv()
            for k in range(3):
                project(p, k)
            attend(p)
            join(p)
            for k in range(4):
                widen(p, k)
            narrow(p)

    pltpu.make_async_copy(outb, out_sec, io_sem.at[0]).start()

    for k in range(depth):
        count = (depth - k if k > 0 else 0) + (k + 1 if k < depth - 1 else 0)

        @pl.when(z == k)
        def _(count=count):
            sent = big.at[pl.ds(0, CHUNKS * count * rs), pl.ds(0, HALF)]
            rcopy(sent, sent, g_send.at[0], g_zr.at[0, 0], across).wait_send()

    sent = big.at[pl.ds(0, CHUNKS * (depth - 1) * rs), pl.ds(0, HALF)]
    rcopy(sent, sent, g_send.at[1], g_xr.at[0, 0], across).wait_send()
    sent = big.at[pl.ds(0, CHUNKS * depth * rs), :]
    rcopy(sent, sent, g_send.at[2], g_sr.at[0], sibling).wait_send()

    def add_small(row, x):
        small[pl.ds(row, 1), :] += row_sum(x)

    def outer_norm(p):
        r = pair_rows(p)
        length = jnp.where(first_section, seq, lens[p])
        score = jnp.where(first_section, 0.0, scores[p])
        place = lax.broadcasted_iota(jnp.int32, (seq, 1), 0)
        grad = jnp.where(place < length, gbuf[r, :].astype(F32), 0.0)
        grad = grad + jnp.where(place == 0, score * head_w[...].reshape(1, D), 0.0)
        n = n2[r, :].astype(F32)
        x = norm_back(grad, n, r2[r, :], gains[1:2, :])
        xl = x.astype(BF)
        high[r, :] = x
        dd[r, :] = xl
        add_small(BD, xl.astype(F32))
        add_small(BETA2, grad)
        add_small(GAIN2, grad * n)

    def act_back(p):
        r = pair_rows(p)
        for k in range(4):
            c4 = pl.ds(k * D, D)
            x = (dot_t(dd[r, :], big[pl.ds(DOWN + k * D, D), :]) * gp[r, c4].astype(F32)).astype(BF)
            gp[r, c4] = x
            add_small(BU + k, x.astype(F32))

    def inner_norm(p):
        r = pair_rows(p)
        grad = high[r, :]
        for k in range(4):
            grad = grad + dot_t(gp[r, pl.ds(k * D, D)], block(4 + k))
        n = n1[r, :].astype(F32)
        x = norm_back(grad, n, r1[r, :], gains[0:1, :])
        xl = x.astype(BF)
        high[r, :] = x
        da[r, :] = xl
        add_small(BO, xl.astype(F32))
        add_small(BETA1, grad)
        add_small(GAIN1, grad * n)
        dm[r, :] = dot_t(xl, block(3)).astype(BF)

    def attend_back(p):
        r = pair_rows(p)
        for j in range(HEADS // 2):
            q2 = qkv[r, pl.ds(j * 128, 128)]
            k2 = qkv[r, pl.ds((j + 6) * 128, 128)]
            v2 = qkv[r, pl.ds((j + 12) * 128, 128)]
            d2 = dm[r, pl.ds(j * 128, 128)]
            none = jnp.zeros_like(d2)
            both = jnp.concatenate([jnp.where(low, d2, none), jnp.where(low, none, d2)], 0)
            pr = jnp.concatenate([probs[p * HEADS + 2 * j], probs[p * HEADS + 2 * j + 1]], 0)
            pf = pr.astype(F32)
            t = pf * dot_t(both, v2)
            ds = (t - pf * jnp.sum(t, -1, keepdims=True)).astype(BF)
            dq = dot(ds, k2)
            dq = (jnp.where(low, dq[:seq], dq[seq:]) * SCALE).astype(BF)
            qt, dt = q2.T, d2.T
            dk = jnp.concatenate([dot(qt[:HEAD], ds[:seq]), dot(qt[HEAD:], ds[seq:])], 0)
            dv = jnp.concatenate([dot(dt[:HEAD], pr[:seq]), dot(dt[HEAD:], pr[seq:])], 0)
            dk = (dk * SCALE).astype(BF).T
            dv = dv.astype(BF).T
            dqkv[r, pl.ds(j * 128, 128)] = dq
            dqkv[r, pl.ds((j + 6) * 128, 128)] = dk
            dqkv[r, pl.ds((j + 12) * 128, 128)] = dv
            small[pl.ds(BQ, 1), pl.ds(j * 128, 128)] += row_sum(dq.astype(F32))
            small[pl.ds(BV, 1), pl.ds(j * 128, 128)] += row_sum(dv.astype(F32))

    def hidden_back(p):
        r = pair_rows(p)
        grad = high[r, :]
        for k in range(3):
            grad = grad + dot_t(dqkv[r, pl.ds(k * D, D)], block(k))
        high[r, :] = grad
        outb[r, :] = grad.astype(BF)

    def grad_copy(p):
        r = pair_rows(p)
        return rcopy(outb.at[r, :], gbuf.at[r, :], y_send.at[1], y_recv.at[2 + p], other)

    def weight_grad(left, lcol, right, rcol, row):
        a = left[:, pl.ds(pl.multiple_of(lcol, 256), D)]
        b = right[:, pl.ds(pl.multiple_of(rcol, 256), D)]
        big[pl.ds(pl.multiple_of(row, 256), D), :] = dot_c(a, b).astype(BF)

    def ordered(i):
        return jnp.where(i < 4, i + 8, jnp.where(i < 8, i, jnp.where(i == 8, 3, i - 9)))

    def sib_copy(m, zz):
        return rcopy(
            big.at[pl.ds(shard_row(m, 2 * zz + 1 - c, DOWN_GRAD), rs), :],
            s1.at[m, zz], r_send.at[0], r_sib.at[m], sibling,
        )

    def sib_send(m):
        @pl.loop(0, depth)
        def _(zz):
            sib_copy(m, zz).start()

    def make_down():
        @pl.loop(0, 4)
        def _(k):
            weight_grad(act, k * D, dd, 0, DOWN_GRAD + k * D)

        @pl.loop(8, 12)
        def _(m):
            sib_send(m)

    def make_up():
        @pl.loop(0, 4)
        def _(k):
            weight_grad(first_low, 0, gp, k * D, (4 + k) * D)
            sib_send(4 + k)

    def make_attn():
        weight_grad(mixed, 0, da, 0, 3 * D)
        sib_send(3)

    def make_qkv():
        @pl.loop(0, 3)
        def _(k):
            weight_grad(hbuf, 0, dqkv, k * D, k * D)
            sib_send(k)

    def x_copy(m):
        return rcopy(
            s1.at[m, :, :, span(1 - par, HALF)], xr.at[m], r_send.at[1], r_x.at[m], across
        )

    def z_copy(m, to):
        return rcopy(xr.at[m, to], zr.at[m, z], r_send.at[2], r_z.at[m, z], dev(z_=to))

    def fin_copy(m):
        return rcopy(fin.at[m, par], fin.at[m, par], r_send.at[3], r_fin.at[m], across)

    def pair_sums(m):
        rcopy(s1.at[m], s1.at[m], r_send.at[0], r_sib.at[m], sibling).wait_recv()

        @pl.loop(0, depth)
        def _(zz):
            mine = big[pl.ds(shard_row(m, 2 * zz + c, DOWN_GRAD), rs), :]
            s1[m, zz] = (mine.astype(F32) + s1[m, zz].astype(F32)).astype(BF)

        x_copy(m).start()

    def across_sums(m):
        x_copy(m).wait_recv()

        @pl.loop(0, depth)
        def _(zz):
            mine = s1[m, zz, :, span(par, HALF)]
            xr[m, zz] = (mine.astype(F32) + xr[m, zz].astype(F32)).astype(BF)

        for k in range(1, depth):
            z_copy(m, (z + k) % depth).start()

    def line_sums(m):
        total = xr[m, z].astype(F32)
        for k in range(1, depth):
            zz = (z + k) % depth
            rcopy(xr.at[m, z], zr.at[m, zz], r_send.at[2], r_z.at[m, zz], across).wait_recv()
            total = total + zr[m, zz].astype(F32)
        if groups > 2:
            teams = groups // 2
            team = g // 2
            peers[m, team] = total.astype(BF)
            for k in range(1, teams):
                to = dev(g_=((team + k) % teams) * 2 + par)
                rcopy(peers.at[m, team], peers.at[m, team], r_send.at[4], r_peer.at[m, team], to).start()
            for k in range(1, teams):
                tt = (team + k) % teams
                rcopy(peers.at[m, tt], peers.at[m, tt], r_send.at[4], r_peer.at[m, tt], across).wait_recv()
            total = peers[m, 0].astype(F32)
            for k in range(1, teams):
                total = total + peers[m, k].astype(F32)
        fin[m, par] = total.astype(BF)
        fin_copy(m).start()

    def finish(m):
        rcopy(fin.at[m, 1 - par], fin.at[m, 1 - par], r_send.at[3], r_fin.at[m], across).wait_recv()
        for h in range(2):

            def put(to, row, col, h=h):
                rows = pl.ds(pl.multiple_of(row, 16), rs)
                cols = pl.ds(pl.multiple_of(col + h * HALF, 128), HALF)
                pltpu.make_async_copy(fin.at[m, h], to.at[rows, cols], io_sem.at[2]).start()

            @pl.when(m >= 8)
            def _(put=put):
                put(out_d, (m - 8) * rs, 0)

            @pl.when((m >= 4) & (m < 8))
            def _(put=put):
                put(out_u, 0, (m - 4) * D)

            @pl.when(m == 3)
            def _(put=put):
                put(out_o, 0, 0)

            @pl.when(m < 3)
            def _(put=put):
                put(out_q, 0, m * D)

    stages = (pair_sums, across_sums, line_sums, finish)

    def sum_step(i):
        for lag, stage in enumerate(stages):

            @pl.when((i >= lag) & (i < CHUNKS + lag))
            def _(lag=lag, stage=stage):
                stage(ordered(i - lag))

    pltpu.make_async_copy(outb, out_sec, io_sem.at[0]).wait()

    @pl.when(first_section)
    def _():
        rcopy(outb, outb, y_send.at[0], y_recv.at[0], other).wait_send()

    @pl.loop(0, pairs)
    def _(p):
        start_sums = first_section & (p == pairs - 1)

        @pl.when(first_section)
        def _():
            grad_copy(p).wait_recv()

        outer_norm(p)
        pl.when(start_sums)(make_down)
        act_back(p)

        @pl.when(start_sums)
        def _():
            sum_step(0)

        inner_norm(p)

        @pl.when(start_sums)
        def _():
            make_up()
            sum_step(1)

        attend_back(p)

        @pl.when(start_sums)
        def _():
            sum_step(2)

        hidden_back(p)

        @pl.when(~first_section)
        def _():
            grad_copy(p).start()

    pltpu.make_async_copy(high, out_gin, io_sem.at[1]).start()

    @pl.when(~first_section)
    def _():
        make_down()
        sum_step(0)
        make_up()
        sum_step(1)
        sum_step(2)

    make_attn()
    make_qkv()

    def sm_copy(src, dst, recv, to):
        return rcopy(src, dst, sm_send.at[0], recv, to)

    def small_sib():
        sm_copy(small, sm_sib, sm_recv.at[0], sibling).start()

    def small_grp():
        sm_copy(small, sm_sib, sm_recv.at[0], sibling).wait_recv()
        sm_grp[g] = small[...] + sm_sib[...]
        for k in range(1, groups):
            sm_copy(sm_grp.at[g], sm_grp.at[g], sm_recv.at[1 + g], dev(g_=(g + k) % groups)).start()

    def small_dp():
        for k in range(1, groups):
            gg = (g + k) % groups
            sm_copy(sm_grp.at[gg], sm_grp.at[gg], sm_recv.at[1 + gg], across).wait_recv()
        total = sm_grp[0]
        for k in range(1, groups):
            total = total + sm_grp[k]
        sm_dp[z] = total
        for k in range(1, depth):
            sm_copy(sm_dp.at[z], sm_dp.at[z], sm_recv.at[1 + groups + z], dev(z_=(z + k) % depth)).start()

    def head_copy():
        return rcopy(out_small, sm_sec, sm_send.at[1], sm_recv.at[1 + groups + depth], other)

    def small_sec():
        for k in range(1, depth):
            zz = (z + k) % depth
            sm_copy(sm_dp.at[zz], sm_dp.at[zz], sm_recv.at[1 + groups + zz], across).wait_recv()
        total = sm_dp[0]
        for k in range(1, depth):
            total = total + sm_dp[k]
        out_small[...] = total

        @pl.when(~first_section)
        def _():
            head_copy().start()

    def small_head():
        @pl.when(first_section)
        def _():
            head_copy().wait_recv()
            out_small[pl.ds(HEAD_ROW, 1), :] = sm_sec[pl.ds(HEAD_ROW, 1), :]

        @pl.when(~first_section)
        def _():
            head_copy().wait_send()

    @pl.loop(3, CHUNKS + len(stages) - 1)
    def _(i):
        for at, part in ((3, small_sib), (5, small_grp), (7, small_dp), (9, small_sec), (11, small_head)):
            pl.when(i == at)(part)
        sum_step(i)

    count = 1 + (groups - 1) + (depth - 1)
    sent = high.at[pl.ds(0, count * SMALL), :]
    rcopy(sent, sent, sm_send.at[0], sm_recv.at[0], other).wait_send()

    @pl.when(~first_section)
    def _():
        rcopy(outb, outb, y_send.at[1], y_recv.at[0], other).wait_send()

    pltpu.make_async_copy(high, out_gin, io_sem.at[1]).wait()
    pltpu.make_async_copy(fin, fin, io_sem.at[2]).wait()
    rcopy(s1, s1, r_send.at[0], r_sib.at[0], sibling).wait_send()
    rcopy(xr, xr, r_send.at[1], r_x.at[0], across).wait_send()
    part = zr.at[:, pl.ds(0, depth - 1)]
    rcopy(part, part, r_send.at[2], r_z.at[0, 0], across).wait_send()
    part = fin.at[:, 0]
    rcopy(part, part, r_send.at[3], r_fin.at[0], across).wait_send()
    if groups > 2:
        part = peers.at[:, pl.ds(0, groups // 2 - 1)]
        rcopy(part, part, r_send.at[4], r_peer.at[0, 0], across).wait_send()


def on_device(groups, depth, embedded, lengths, token_grads, score_grads, w_qkv, w_attn_out, w_up, w_down, biases, gains, head_weight):
    micro, _, seq, _ = embedded.shape
    tokens = micro * seq
    rs = w_qkv.shape[1]
    vmem = pl.BlockSpec(memory_space=pltpu.VMEM)
    smem = pl.BlockSpec(memory_space=pltpu.SMEM)
    hbm = pl.BlockSpec(memory_space=pl.ANY)
    teams = max(groups // 2, 1)
    out_shape = (
        jax.ShapeDtypeStruct((tokens, D), BF),
        jax.ShapeDtypeStruct((tokens, D), F32),
        jax.ShapeDtypeStruct((rs, 3 * D), BF),
        jax.ShapeDtypeStruct((rs, D), BF),
        jax.ShapeDtypeStruct((rs, FF), BF),
        jax.ShapeDtypeStruct((4 * rs, D), BF),
        jax.ShapeDtypeStruct((SMALL, D), F32),
    )
    scratch = [
        pltpu.VMEM((CHUNKS * D + FF, D), BF),
        pltpu.VMEM((CHUNKS, depth, rs, D), BF),
        pltpu.VMEM((CHUNKS, depth, rs, HALF), BF),
        pltpu.VMEM((CHUNKS, depth, rs, HALF), BF),
        pltpu.VMEM((CHUNKS, 2, rs, HALF), BF),
        pltpu.VMEM((CHUNKS, teams, rs, HALF) if groups > 2 else (1, 1, 16, 128), BF),
        pltpu.VMEM((tokens, D), BF),
        pltpu.VMEM((tokens, 3 * D), BF),
        pltpu.VMEM((micro * HEADS, seq, seq), BF),
        pltpu.VMEM((tokens, D), BF),
        pltpu.VMEM((tokens, D), BF),
        pltpu.VMEM((tokens, 1), F32),
        pltpu.VMEM((tokens, D), BF),
        pltpu.VMEM((tokens, FF), BF),
        pltpu.VMEM((tokens, FF), BF),
        pltpu.VMEM((tokens, D), BF),
        pltpu.VMEM((tokens, 1), F32),
        pltpu.VMEM((tokens, D), BF),
        pltpu.VMEM((tokens, D), BF),
        pltpu.VMEM((tokens, D), F32),
        pltpu.VMEM((tokens, D), BF),
        pltpu.VMEM((tokens, D), BF),
        pltpu.VMEM((tokens, D), BF),
        pltpu.VMEM((tokens, 3 * D), BF),
        pltpu.VMEM((SMALL, D), F32),
        pltpu.VMEM((SMALL, D), F32),
        pltpu.VMEM((groups, SMALL, D), F32),
        pltpu.VMEM((depth, SMALL, D), F32),
        pltpu.VMEM((SMALL, D), F32),
        pltpu.SemaphoreType.DMA((2,)),
        pltpu.SemaphoreType.DMA((3,)),
        pltpu.SemaphoreType.DMA((CHUNKS, depth)),
        pltpu.SemaphoreType.DMA((CHUNKS, depth)),
        pltpu.SemaphoreType.DMA((CHUNKS,)),
        pltpu.SemaphoreType.DMA((3,)),
        pltpu.SemaphoreType.DMA((2,)),
        pltpu.SemaphoreType.DMA((4,)),
        pltpu.SemaphoreType.DMA((5,)),
        pltpu.SemaphoreType.DMA((CHUNKS,)),
        pltpu.SemaphoreType.DMA((CHUNKS,)),
        pltpu.SemaphoreType.DMA((CHUNKS, depth)),
        pltpu.SemaphoreType.DMA((CHUNKS,)),
        pltpu.SemaphoreType.DMA((CHUNKS, teams)),
        pltpu.SemaphoreType.DMA((2,)),
        pltpu.SemaphoreType.DMA((2 + groups + depth,)),
    ]
    state, grad_in, *grads, small = pl.pallas_call(
        functools.partial(kernel, (groups, depth, rs, seq)),
        out_shape=out_shape,
        in_specs=[hbm] * 6 + [smem] * 2 + [vmem] * 3,
        out_specs=(hbm,) * 6 + (vmem,),
        scratch_shapes=scratch,
        compiler_params=pltpu.CompilerParams(
            collective_id=0, has_side_effects=True, vmem_limit_bytes=63 * 1024 * 1024
        ),
    )(
        embedded.reshape(tokens, D),
        token_grads.reshape(tokens, D),
        w_qkv[0],
        w_attn_out[0],
        w_up[0],
        w_down[0],
        lengths.reshape(micro),
        score_grads.reshape(micro),
        biases,
        gains[0],
        head_weight,
    )
    results = pl.pallas_call(
        hand_out,
        out_shape=[jax.ShapeDtypeStruct(x.shape, x.dtype) for x in (state, grad_in)]
        + [jax.ShapeDtypeStruct(x.shape, F32) for x in grads]
        + [jax.ShapeDtypeStruct(x, F32) for x in ((1, 10 * D), (2, D), (D,))],
        in_specs=[vmem] * 7,
        out_specs=[vmem] * 9,
    )(state, grad_in, *grads, small)
    state, grad_in, g_qkv, g_attn, g_up, g_down, g_bias, g_gain, g_head = results
    return (
        state.reshape(1, micro, 1, seq, D),
        grad_in.reshape(1, micro, 1, seq, D),
        g_qkv[None],
        g_attn[None],
        g_up[None],
        g_down[None],
        g_bias,
        g_gain[None],
        g_head,
    )


def hand_out(state, grad_in, gq, go, gu, gd, small, o_state, o_gin, o_q, o_o, o_u, o_d, o_bias, o_gain, o_head):
    for src, dst in ((state, o_state), (grad_in, o_gin), (gq, o_q), (go, o_o), (gu, o_u), (gd, o_d)):
        dst[...] = src[...].astype(dst.dtype)
    for k in range(10):
        o_bias[:, pl.ds(k * D, D)] = small[pl.ds(k, 1), :]
    o_gain[...] = small[pl.ds(GAIN1, 2), :]
    o_head[...] = small[HEAD_ROW, :]


def solution(mesh):
    return jax.shard_map(
        functools.partial(on_device, mesh.shape["grp"], mesh.shape["dp"] // 2),
        mesh=mesh,
        in_specs=(
            P(None, ("grp", "dp"), None, None),
            P(None, ("grp", "dp")),
            P(None, ("grp", "dp"), None, None),
            P(None, ("grp", "dp")),
            P("section", "dp", None),
            P("section", "dp", None),
            P("section", "dp", None),
            P("section", "dp", None),
            P("section", None),
            P("section", None, None),
            P(),
        ),
        out_specs=(
            P("section", None, ("grp", "dp"), None, None),
            P("section", None, ("grp", "dp"), None, None),
            P("section", "dp", None),
            P("section", "dp", None),
            P("section", "dp", None),
            P("section", "dp", None),
            P("section", None),
            P("section", None, None),
            P(),
        ),
        check_vma=False,
    )
```

```python
import functools
import math

import jax
import jax.numpy as jnp
from jax import lax
from jax.experimental import pallas as pl
from jax.experimental.pallas import tpu as pltpu
from jax.sharding import PartitionSpec as P

D = 768
FF = 3072
HEADS = 12
HEAD = 64
EPSILON = 1e-06
CHUNKS = 12
HALF = D // 2
DOWN = 8 * D
DOWN_GRAD = 12 * D
SCALE = 1.0 / math.sqrt(HEAD)
F32 = jnp.float32
BF = jnp.bfloat16
MESH = pl.DeviceIdType.MESH
BQ, BV, BO, BU, BD, BETA1, BETA2, GAIN1, GAIN2, HEAD_ROW = 0, 1, 2, 3, 7, 8, 9, 10, 11, 12
SMALL = 16
X_FIRST = (8, 4, 5, 6, 3, 0, 1, 2)
Z_FIRST = (9, 10, 11, 7)


def dot(a, b):
    return lax.dot_general(a, b, (((1,), (0,)), ((), ())), preferred_element_type=F32)


def dot_t(a, b):
    return lax.dot_general(a, b, (((1,), (1,)), ((), ())), preferred_element_type=F32)


def dot_c(a, b):
    return lax.dot_general(a, b, (((0,), (0,)), ((), ())), preferred_element_type=F32)


def span(i, width):
    return pl.ds(pl.multiple_of(i * width, width), width)


def flip(index, mask):
    bit = 1
    while bit <= mask:
        if mask & bit:
            index = index + bit - 2 * bit * ((index // bit) % 2)
        bit *= 2
    return index


def masks(bits):
    found = [0]
    for bit in bits:
        found = found + [mask ^ bit for mask in found]
    return found


def pick(i, values):
    found = values[-1]
    for k in range(len(values) - 2, -1, -1):
        found = jnp.where(i == k, values[k], found)
    return found


def row_sum(x):
    return jnp.sum(x, 0, keepdims=True)


def gelu_parts(x):
    t = 1.0 / (1.0 + (0.3275911 * math.sqrt(0.5)) * jnp.abs(x))
    e = jnp.exp(-0.5 * x * x)
    tail = t * (0.127414796 + t * (-0.142248368 + t * (0.7107068705 + t * (-0.7265760135 + t * 0.5307027145)))) * e
    phi = jnp.where(x >= 0, 1.0 - tail, tail)
    return x * phi, phi + x * (e * (1.0 / math.sqrt(2.0 * math.pi)))


def normed(x):
    centred = x - jnp.mean(x, -1, keepdims=True)
    scale = lax.rsqrt(jnp.mean(centred * centred, -1, keepdims=True) + EPSILON)
    return centred * scale, scale


def norm_back(grad, n, scale, gain):
    gg = gain * grad
    return (gg - jnp.mean(gg, -1, keepdims=True) - n * jnp.mean(gg * n, -1, keepdims=True)) * scale


def kernel(sizes, *refs):
    groups, depth, rs, seq = sizes
    (emb, token_grads, wq_in, wo_in, wu_in, wd_in, lens, scores, bias, gains, head_w,
     out_sec, out_gin, out_q, out_o, out_u, out_d, out_small,
     big, s1, xr, zr, zw, xw, fin, peers,
     hbuf, qkv, probs, mixed, n1, r1, first_low, act, gp, n2, r2, outb, gbuf, high, dd, da, dm, dqkv,
     small, sm_sib, sm_grp, sm_dp, sm_sec,
     local_sem, io_sem, g_zr, g_xr, g_sr, g_send, y_send, y_recv,
     r_send, r_sib, r_x, r_z, r_grp, r_fin, r_peer, sm_send, sm_recv) = refs
    stages = depth.bit_length() - 1
    pairs = 2
    sec = lax.axis_index("section")
    g = lax.axis_index("grp")
    d = lax.axis_index("dp")
    z, c = d // 2, d % 2
    par = g % 2
    first_section = sec == 0

    def dev(sec_=None, g_=None, z_=None, c_=None):
        return (
            sec if sec_ is None else sec_,
            g if g_ is None else g_,
            (z if z_ is None else z_) * 2 + (c if c_ is None else c_),
        )

    sibling = dev(c_=1 - c)
    across = dev(g_=g + 1 - 2 * par)
    other = dev(sec_=1 - sec)

    def rcopy(src, dst, send, recv, to):
        return pltpu.make_async_remote_copy(
            src_ref=src, dst_ref=dst, send_sem=send, recv_sem=recv, device_id=to, device_id_type=MESH
        )

    def shard_row(m, owner, down=DOWN):
        row = jnp.where(m < 8, m * D + owner * rs, down + owner * (4 * rs) + (m - 8) * rs)
        return pl.multiple_of(row, 16)

    barrier = pltpu.get_barrier_semaphore()
    greeted = 0
    for to in [sibling, other]:
        pl.semaphore_signal(barrier, inc=1, device_id=to, device_id_type=MESH)
        greeted += 1
    for k in range(1, groups):
        pl.semaphore_signal(barrier, inc=1, device_id=dev(g_=(g + k) % groups), device_id_type=MESH)
        greeted += 1
    for k in range(1, depth):
        pl.semaphore_signal(barrier, inc=1, device_id=dev(z_=(z + k) % depth), device_id_type=MESH)
        greeted += 1

    own = []
    for k in range(3):
        own.append((wq_in.at[:, pl.ds(k * D, D)], k))
    own.append((wo_in, 3))
    for k in range(4):
        own.append((wu_in.at[:, pl.ds(k * D, D)], 4 + k))
    for src, k in own:
        pltpu.make_async_copy(src, big.at[pl.ds(pl.multiple_of(k * D + d * rs, 16), rs), :], local_sem.at[0]).start()
    pltpu.make_async_copy(
        wd_in, big.at[pl.ds(pl.multiple_of(DOWN + d * 4 * rs, 16), 4 * rs), :], local_sem.at[0]
    ).start()

    @pl.when(first_section)
    def _():
        pltpu.make_async_copy(emb, hbuf, local_sem.at[1]).start()

    @pl.when(~first_section)
    def _():
        pltpu.make_async_copy(token_grads, gbuf, local_sem.at[1]).start()

    small[...] = jnp.zeros_like(small)
    pl.semaphore_wait(barrier, greeted)
    pltpu.make_async_copy(
        big.at[pl.ds(0, CHUNKS * rs), :], big.at[pl.ds(0, CHUNKS * rs), :], local_sem.at[0]
    ).wait()

    def region(m, zz, half=None, cc=c):
        cols = slice(None) if half is None else span(half, HALF)
        return big.at[pl.ds(shard_row(m, 2 * zz + cc), rs), cols]

    far = [depth >> (t + 1) for t in range(stages)]
    held = [masks(far[:t]) for t in range(stages + 1)]

    def along(m, zz, t):
        part = region(m, zz, par)
        return rcopy(part, part, g_send.at[0], g_zr.at[m, zz], dev(z_=flip(z, far[t])))

    def over(m, zz, half):
        part = region(m, zz, half)
        return rcopy(part, part, g_send.at[1], g_xr.at[m, zz], across)

    def beside(m, zz, half):
        part = region(m, zz, half)
        return rcopy(part, part, g_send.at[2], g_sr.at[m], sibling)

    def bias_row(start, width=D):
        return bias[:, pl.ds(start, width)]

    low = lax.broadcasted_iota(jnp.int32, (1, 128), 1) < HEAD
    key = lax.broadcasted_iota(jnp.int32, (1, seq), 1)

    def pair_rows(p):
        return span(p, seq)

    def block(k):
        return big[pl.ds(k * D, D), :]

    def project(p, k):
        r = pair_rows(p)
        x = dot(hbuf[r, :], block(k))
        if k != 1:
            x = x + bias_row(0 if k == 0 else D)
        qkv[r, pl.ds(k * D, D)] = x.astype(BF)

    def attend(p):
        r = pair_rows(p)
        ok = key < lens[p]
        for j in range(HEADS // 2):
            q2 = qkv[r, pl.ds(j * 128, 128)]
            k2 = qkv[r, pl.ds((j + 6) * 128, 128)]
            v2 = qkv[r, pl.ds((j + 12) * 128, 128)]
            none = jnp.zeros_like(q2)
            both = jnp.concatenate([jnp.where(low, q2, none), jnp.where(low, none, q2)], 0)
            sc = jnp.where(ok, dot_t(both, k2) * SCALE, -1e30)
            e = jnp.exp(sc - jnp.max(sc, -1, keepdims=True))
            pr = (e * (1.0 / jnp.sum(e, -1, keepdims=True))).astype(BF)
            probs[p * HEADS + 2 * j] = pr[:seq]
            probs[p * HEADS + 2 * j + 1] = pr[seq:]
            o = dot(pr, v2)
            mixed[r, pl.ds(j * 128, 128)] = jnp.where(low, o[:seq], o[seq:]).astype(BF)

    def join(p):
        r = pair_rows(p)
        n, scale = normed(hbuf[r, :].astype(F32) + dot(mixed[r, :], block(3)) + bias_row(2 * D))
        n1[r, :] = n.astype(BF)
        r1[r, :] = scale
        y = n * gains[0:1, :] + bias_row(4 * D + FF)
        high[r, :] = y
        first_low[r, :] = y.astype(BF)

    def widen(p, k):
        r = pair_rows(p)
        for t in range(3):
            w = big[pl.ds((4 + k) * D, D), pl.ds(t * 256, 256)]
            col = k * D + t * 256
            a, dg = gelu_parts(dot(first_low[r, :], w) + bias_row(3 * D + col, 256))
            act[r, pl.ds(col, 256)] = a.astype(BF)
            gp[r, pl.ds(col, 256)] = dg.astype(BF)

    def narrow(p):
        r = pair_rows(p)
        n, scale = normed(high[r, :] + dot(act[r, :], big[pl.ds(DOWN, FF), :]) + bias_row(3 * D + FF))
        n2[r, :] = n.astype(BF)
        r2[r, :] = scale
        y = n * gains[1:2, :] + bias_row(5 * D + FF)
        outb[r, :] = y.astype(BF)

        @pl.when(~first_section)
        def _():
            small[pl.ds(HEAD_ROW, 1), :] += scores[p] * y[0:1]

    def state_copy(p):
        r = pair_rows(p)
        return rcopy(outb.at[r, :], hbuf.at[r, :], y_send.at[0], y_recv.at[p], other)

    def chunk_ready(m):
        whole = big.at[pl.ds(0, depth * rs), :]
        rcopy(whole, whole, g_send.at[2], g_sr.at[m], sibling).wait_recv()

    def own_step(n):
        if stages:
            along(n, z, 0).start()
        beside(n, z, None).start()

    def arrived(m, t):
        for mask in held[t]:
            zz = flip(z, far[t] ^ mask)
            along(m, zz, t).wait_recv()
            over(m, zz, par).start()
            beside(m, zz, par).start()
        if t + 1 < stages:
            for mask in held[t + 1]:
                along(m, flip(z, mask), t + 1).start()

    def crossed(m, t):
        for mask in held[t]:
            zz = flip(z, far[t] ^ mask)
            over(m, zz, 1 - par).wait_recv()
            beside(m, zz, 1 - par).start()

    def early(step, pieces):
        def run(n):
            @pl.when(first_section & (n == stages + 2 + step))
            def _():
                pieces()

        return run

    def both_pairs(piece):
        @pl.loop(0, pairs)
        def _(p):
            piece(p)

    def early_project(k):
        if k == 0:
            pltpu.make_async_copy(emb, hbuf, local_sem.at[1]).wait()
        chunk_ready(k)
        both_pairs(lambda p: project(p, k))

    def early_join():
        chunk_ready(3)
        both_pairs(join)

    def early_widen(k):
        chunk_ready(4 + k)
        both_pairs(lambda p: widen(p, k))

    plan = [early(k, functools.partial(early_project, k)) for k in range(3)]
    plan.append(early(3, lambda: attend(0)))
    plan.append(early(4, lambda: attend(1)))
    plan.append(early(5, early_join))
    plan += [early(5 + k, functools.partial(early_widen, k)) for k in range(4)]

    @pl.loop(0, CHUNKS + stages + 1)
    def _(n):
        pl.when(n < CHUNKS)(functools.partial(own_step, n))
        for t in range(stages):
            m = n - t - 1
            pl.when((m >= 0) & (m < CHUNKS))(functools.partial(arrived, m, t))
        for t in range(stages):
            m = n - t - 2
            pl.when((m >= 0) & (m < CHUNKS))(functools.partial(crossed, m, t))
        for run in plan:
            run(n)

    @pl.loop(jnp.where(first_section, 8, 0), CHUNKS)
    def _(m):
        chunk_ready(m)

    @pl.when(first_section)
    def _():
        @pl.loop(0, pairs)
        def _(p):
            narrow(p)
            state_copy(p).start()

    @pl.when(~first_section)
    def _():
        pltpu.make_async_copy(token_grads, gbuf, local_sem.at[1]).wait()

        @pl.loop(0, pairs)
        def _(p):
            state_copy(p).wait_recv()
            for k in range(3):
                project(p, k)
            attend(p)
            join(p)
            for k in range(4):
                widen(p, k)
            narrow(p)

    pltpu.make_async_copy(outb, out_sec, io_sem.at[0]).start()

    sent = big.at[pl.ds(0, CHUNKS * (depth - 1) * rs), pl.ds(0, HALF)]
    rcopy(sent, sent, g_send.at[0], g_zr.at[0, 0], across).wait_send()
    sent = big.at[pl.ds(0, CHUNKS * (depth - 1) * rs), pl.ds(0, HALF)]
    rcopy(sent, sent, g_send.at[1], g_xr.at[0, 0], across).wait_send()
    sent = big.at[pl.ds(0, CHUNKS * depth * rs), :]
    rcopy(sent, sent, g_send.at[2], g_sr.at[0], sibling).wait_send()

    def add_small(row, x):
        small[pl.ds(row, 1), :] += row_sum(x)

    def outer_norm(p):
        r = pair_rows(p)
        length = jnp.where(first_section, seq, lens[p])
        score = jnp.where(first_section, 0.0, scores[p])
        place = lax.broadcasted_iota(jnp.int32, (seq, 1), 0)
        grad = jnp.where(place < length, gbuf[r, :].astype(F32), 0.0)
        grad = grad + jnp.where(place == 0, score * head_w[...].reshape(1, D), 0.0)
        n = n2[r, :].astype(F32)
        x = norm_back(grad, n, r2[r, :], gains[1:2, :])
        xl = x.astype(BF)
        high[r, :] = x
        dd[r, :] = xl
        add_small(BD, xl.astype(F32))
        add_small(BETA2, grad)
        add_small(GAIN2, grad * n)

    def act_back(p):
        r = pair_rows(p)
        for k in range(4):
            c4 = pl.ds(k * D, D)
            x = (dot_t(dd[r, :], big[pl.ds(DOWN + k * D, D), :]) * gp[r, c4].astype(F32)).astype(BF)
            gp[r, c4] = x
            add_small(BU + k, x.astype(F32))

    def inner_norm(p):
        r = pair_rows(p)
        grad = high[r, :]
        for k in range(4):
            grad = grad + dot_t(gp[r, pl.ds(k * D, D)], block(4 + k))
        n = n1[r, :].astype(F32)
        x = norm_back(grad, n, r1[r, :], gains[0:1, :])
        xl = x.astype(BF)
        high[r, :] = x
        da[r, :] = xl
        add_small(BO, xl.astype(F32))
        add_small(BETA1, grad)
        add_small(GAIN1, grad * n)
        dm[r, :] = dot_t(xl, block(3)).astype(BF)

    def attend_back(p):
        r = pair_rows(p)
        for j in range(HEADS // 2):
            q2 = qkv[r, pl.ds(j * 128, 128)]
            k2 = qkv[r, pl.ds((j + 6) * 128, 128)]
            v2 = qkv[r, pl.ds((j + 12) * 128, 128)]
            d2 = dm[r, pl.ds(j * 128, 128)]
            none = jnp.zeros_like(d2)
            both = jnp.concatenate([jnp.where(low, d2, none), jnp.where(low, none, d2)], 0)
            pr = jnp.concatenate([probs[p * HEADS + 2 * j], probs[p * HEADS + 2 * j + 1]], 0)
            pf = pr.astype(F32)
            t = pf * dot_t(both, v2)
            ds = (t - pf * jnp.sum(t, -1, keepdims=True)).astype(BF)
            dq = dot(ds, k2)
            dq = (jnp.where(low, dq[:seq], dq[seq:]) * SCALE).astype(BF)
            qt, dt = q2.T, d2.T
            dk = jnp.concatenate([dot(qt[:HEAD], ds[:seq]), dot(qt[HEAD:], ds[seq:])], 0)
            dv = jnp.concatenate([dot(dt[:HEAD], pr[:seq]), dot(dt[HEAD:], pr[seq:])], 0)
            dk = (dk * SCALE).astype(BF).T
            dv = dv.astype(BF).T
            dqkv[r, pl.ds(j * 128, 128)] = dq
            dqkv[r, pl.ds((j + 6) * 128, 128)] = dk
            dqkv[r, pl.ds((j + 12) * 128, 128)] = dv
            small[pl.ds(BQ, 1), pl.ds(j * 128, 128)] += row_sum(dq.astype(F32))
            small[pl.ds(BV, 1), pl.ds(j * 128, 128)] += row_sum(dv.astype(F32))

    def hidden_back(p):
        r = pair_rows(p)
        grad = high[r, :]
        for k in range(3):
            grad = grad + dot_t(dqkv[r, pl.ds(k * D, D)], block(k))
        high[r, :] = grad
        outb[r, :] = grad.astype(BF)

    def grad_copy(p):
        r = pair_rows(p)
        return rcopy(outb.at[r, :], gbuf.at[r, :], y_send.at[1], y_recv.at[2 + p], other)

    def weight_grad(left, lcol, right, rcol, row):
        a = left[:, pl.ds(pl.multiple_of(lcol, 256), D)]
        b = right[:, pl.ds(pl.multiple_of(rcol, 256), D)]
        big[pl.ds(pl.multiple_of(row, 256), D), :] = dot_c(a, b).astype(BF)

    def sib_copy(m, zz):
        return rcopy(
            big.at[pl.ds(shard_row(m, 2 * zz + 1 - c, DOWN_GRAD), rs), :],
            s1.at[m, zz], r_send.at[0], r_sib.at[m], sibling,
        )

    def sib_send(m):
        @pl.loop(0, depth)
        def _(zz):
            sib_copy(m, zz).start()

    def make_down():
        @pl.loop(0, 4)
        def _(k):
            weight_grad(act, k * D, dd, 0, DOWN_GRAD + k * D)

        @pl.loop(8, 12)
        def _(m):
            sib_send(m)

    def make_up():
        @pl.loop(0, 4)
        def _(k):
            weight_grad(first_low, 0, gp, k * D, (4 + k) * D)
            sib_send(4 + k)

    def make_attn():
        weight_grad(mixed, 0, da, 0, 3 * D)
        sib_send(3)

    def make_qkv():
        @pl.loop(0, 3)
        def _(k):
            weight_grad(hbuf, 0, dqkv, k * D, k * D)
            sib_send(k)

    def pair_sums(m):
        rcopy(s1.at[m], s1.at[m], r_send.at[0], r_sib.at[m], sibling).wait_recv()

        @pl.loop(0, depth)
        def _(zz):
            mine = big[pl.ds(shard_row(m, 2 * zz + c, DOWN_GRAD), rs), :]
            s1[m, zz] = (mine.astype(F32) + s1[m, zz].astype(F32)).astype(BF)

    sides = [masks([2 << k for k in range(t, stages - 1)]) for t in range(stages)]
    slots = [sum(len(side) for side in sides[:t]) for t in range(stages)]

    def line_send(part, landing, m, t, send):
        for k, mask in enumerate(sides[t]):
            rcopy(
                part.at[flip(z, (1 << t) ^ mask)], landing.at[slots[t] + k], send, r_z.at[m, t],
                dev(z_=flip(z, 1 << t)),
            ).start()

    def line_add(part, landing, m, t, send):
        here = landing.at[pl.ds(slots[t], len(sides[t]))]
        rcopy(here, here, send, r_z.at[m, t], dev(z_=flip(z, 1 << t))).wait_recv()
        for k, mask in enumerate(sides[t]):
            zz = flip(z, mask)
            part[zz] = (part[zz].astype(F32) + landing[slots[t] + k].astype(F32)).astype(BF)

    def put_out(m):
        for h in range(2):

            def put(to, row, col, h=h):
                rows = pl.ds(pl.multiple_of(row, 16), rs)
                cols = pl.ds(pl.multiple_of(col + h * HALF, 128), HALF)
                pltpu.make_async_copy(fin.at[m, h], to.at[rows, cols], io_sem.at[2]).start()

            @pl.when(m >= 8)
            def _(put=put):
                put(out_d, (m - 8) * rs, 0)

            @pl.when((m >= 4) & (m < 8))
            def _(put=put):
                put(out_u, 0, (m - 4) * D)

            @pl.when(m == 3)
            def _(put=put):
                put(out_o, 0, 0)

            @pl.when(m < 3)
            def _(put=put):
                put(out_q, 0, m * D)

    def x_copy(q, m):
        return rcopy(
            s1.at[m, :, :, span(1 - par, HALF)], xr.at[q], r_send.at[1], r_x.at[m], across
        )

    def fin_copy(m):
        return rcopy(fin.at[m, par], fin.at[m, par], r_send.at[4], r_fin.at[m], across)

    def x_start(q, m):
        pair_sums(m)
        x_copy(q, m).start()

    def x_halves(q, m):
        x_copy(q, m).wait_recv()

        @pl.loop(0, depth)
        def _(zz):
            mine = s1[m, zz, :, span(par, HALF)]
            xr[q, zz] = (mine.astype(F32) + xr[q, zz].astype(F32)).astype(BF)

        line_send(xr.at[q], zr.at[q], m, 0, r_send.at[2])

    def x_line(t, q, m):
        line_add(xr.at[q], zr.at[q], m, t, r_send.at[2])
        if t + 1 < stages:
            line_send(xr.at[q], zr.at[q], m, t + 1, r_send.at[2])
            return
        total = xr[q, z]
        if groups > 2:
            teams = groups // 2
            team = g // 2
            peers[q, team] = total
            for k in range(1, teams):
                to = dev(g_=((team + k) % teams) * 2 + par)
                rcopy(peers.at[q, team], peers.at[q, team], r_send.at[5], r_peer.at[m, team], to).start()
            for k in range(1, teams):
                tt = (team + k) % teams
                rcopy(peers.at[q, tt], peers.at[q, tt], r_send.at[5], r_peer.at[m, tt], across).wait_recv()
            total = peers[q, 0].astype(F32)
            for k in range(1, teams):
                total = total + peers[q, k].astype(F32)
            total = total.astype(BF)
        fin[m, par] = total
        fin_copy(m).start()

    def x_finish(q, m):
        rcopy(fin.at[m, 1 - par], fin.at[m, 1 - par], r_send.at[4], r_fin.at[m], across).wait_recv()
        put_out(m)

    def z_start(q, m):
        pair_sums(m)
        line_send(s1.at[m], zw.at[q], m, 0, r_send.at[3])

    def z_line(t, q, m):
        line_add(s1.at[m], zw.at[q], m, t, r_send.at[3])
        if t + 1 < stages:
            line_send(s1.at[m], zw.at[q], m, t + 1, r_send.at[3])
            return
        xw[q, g] = s1[m, z]
        for k in range(1, groups):
            rcopy(xw.at[q, g], xw.at[q, g], r_send.at[6], r_grp.at[q, g], dev(g_=(g + k) % groups)).start()

    def z_finish(q, m):
        for k in range(1, groups):
            gg = (g + k) % groups
            rcopy(xw.at[q, gg], xw.at[q, gg], r_send.at[6], r_grp.at[q, gg], across).wait_recv()
        total = xw[q, 0].astype(F32)
        for k in range(1, groups):
            total = total + xw[q, k].astype(F32)
        total = total.astype(BF)
        fin[m, 0] = total[:, :HALF]
        fin[m, 1] = total[:, HALF:]
        put_out(m)

    x_stages = [x_start, x_halves] + [functools.partial(x_line, t) for t in range(stages)] + [x_finish]
    z_stages = [z_start] + [functools.partial(z_line, t) for t in range(stages)] + [z_finish]
    steps = max(len(X_FIRST) + len(x_stages), 2 * len(Z_FIRST) - 1 + len(z_stages)) - 1

    def sum_step(i):
        for lag in range(max(len(x_stages), len(z_stages))):
            if lag < len(x_stages):

                @pl.when((i >= lag) & (i < len(X_FIRST) + lag))
                def _(lag=lag):
                    x_stages[lag](i - lag, pick(i - lag, X_FIRST))

            if lag < len(z_stages):

                @pl.when((i >= lag) & (i < 2 * len(Z_FIRST) + lag) & ((i - lag) % 2 == 0))
                def _(lag=lag):
                    q = (i - lag) // 2
                    z_stages[lag](q, pick(q, Z_FIRST))

    pltpu.make_async_copy(outb, out_sec, io_sem.at[0]).wait()

    @pl.when(first_section)
    def _():
        rcopy(outb, outb, y_send.at[0], y_recv.at[0], other).wait_send()

    @pl.loop(0, pairs)
    def _(p):
        start_sums = first_section & (p == pairs - 1)

        @pl.when(first_section)
        def _():
            grad_copy(p).wait_recv()

        outer_norm(p)
        pl.when(start_sums)(make_down)
        act_back(p)

        @pl.when(start_sums)
        def _():
            sum_step(0)

        inner_norm(p)

        @pl.when(start_sums)
        def _():
            make_up()
            sum_step(1)

        attend_back(p)

        @pl.when(start_sums)
        def _():
            sum_step(2)

        hidden_back(p)

        @pl.when(~first_section)
        def _():
            grad_copy(p).start()

    pltpu.make_async_copy(high, out_gin, io_sem.at[1]).start()

    @pl.when(~first_section)
    def _():
        make_down()
        sum_step(0)
        make_up()
        sum_step(1)
        sum_step(2)

    make_attn()
    make_qkv()

    def sm_copy(src, dst, recv, to):
        return rcopy(src, dst, sm_send.at[0], recv, to)

    def small_sib():
        sm_copy(small, sm_sib, sm_recv.at[0], sibling).start()

    def small_grp():
        sm_copy(small, sm_sib, sm_recv.at[0], sibling).wait_recv()
        sm_grp[g] = small[...] + sm_sib[...]
        for k in range(1, groups):
            sm_copy(sm_grp.at[g], sm_grp.at[g], sm_recv.at[1 + g], dev(g_=(g + k) % groups)).start()

    def small_dp():
        for k in range(1, groups):
            gg = (g + k) % groups
            sm_copy(sm_grp.at[gg], sm_grp.at[gg], sm_recv.at[1 + gg], across).wait_recv()
        total = sm_grp[0]
        for k in range(1, groups):
            total = total + sm_grp[k]
        sm_dp[z] = total
        for k in range(1, depth):
            sm_copy(sm_dp.at[z], sm_dp.at[z], sm_recv.at[1 + groups + z], dev(z_=(z + k) % depth)).start()

    def head_copy():
        return rcopy(out_small, sm_sec, sm_send.at[1], sm_recv.at[1 + groups + depth], other)

    def small_sec():
        for k in range(1, depth):
            zz = (z + k) % depth
            sm_copy(sm_dp.at[zz], sm_dp.at[zz], sm_recv.at[1 + groups + zz], across).wait_recv()
        total = sm_dp[0]
        for k in range(1, depth):
            total = total + sm_dp[k]
        out_small[...] = total

        @pl.when(~first_section)
        def _():
            head_copy().start()

    def small_head():
        @pl.when(first_section)
        def _():
            head_copy().wait_recv()
            out_small[pl.ds(HEAD_ROW, 1), :] = sm_sec[pl.ds(HEAD_ROW, 1), :]

        @pl.when(~first_section)
        def _():
            head_copy().wait_send()

    @pl.loop(3, steps)
    def _(i):
        for at, part in ((3, small_sib), (4, small_grp), (5, small_dp), (6, small_sec), (8, small_head)):
            pl.when(i == at)(part)
        sum_step(i)

    count = 1 + (groups - 1) + (depth - 1)
    sent = high.at[pl.ds(0, count * SMALL), :]
    rcopy(sent, sent, sm_send.at[0], sm_recv.at[0], other).wait_send()

    @pl.when(~first_section)
    def _():
        rcopy(outb, outb, y_send.at[1], y_recv.at[0], other).wait_send()

    pltpu.make_async_copy(high, out_gin, io_sem.at[1]).wait()
    pltpu.make_async_copy(fin, fin, io_sem.at[2]).wait()
    rcopy(s1, s1, r_send.at[0], r_sib.at[0], sibling).wait_send()
    rcopy(xr, xr, r_send.at[1], r_x.at[0], across).wait_send()
    if stages:
        rcopy(zr, zr, r_send.at[2], r_z.at[0, 0], across).wait_send()
        rcopy(zw, zw, r_send.at[3], r_z.at[0, 0], across).wait_send()
    part = fin.at[pl.ds(0, len(X_FIRST)), 0]
    rcopy(part, part, r_send.at[4], r_fin.at[0], across).wait_send()
    if groups > 2:
        part = peers.at[:, pl.ds(0, groups // 2 - 1)]
        rcopy(part, part, r_send.at[5], r_peer.at[0, 0], across).wait_send()
    part = xw.at[:, pl.ds(0, groups - 1)]
    rcopy(part, part, r_send.at[6], r_grp.at[0, 0], across).wait_send()


def on_device(groups, depth, embedded, lengths, token_grads, score_grads, w_qkv, w_attn_out, w_up, w_down, biases, gains, head_weight):
    micro, _, seq, _ = embedded.shape
    tokens = micro * seq
    rs = w_qkv.shape[1]
    vmem = pl.BlockSpec(memory_space=pltpu.VMEM)
    smem = pl.BlockSpec(memory_space=pltpu.SMEM)
    hbm = pl.BlockSpec(memory_space=pl.ANY)
    teams = max(groups // 2, 1)
    stages = depth.bit_length() - 1
    out_shape = (
        jax.ShapeDtypeStruct((tokens, D), BF),
        jax.ShapeDtypeStruct((tokens, D), F32),
        jax.ShapeDtypeStruct((rs, 3 * D), BF),
        jax.ShapeDtypeStruct((rs, D), BF),
        jax.ShapeDtypeStruct((rs, FF), BF),
        jax.ShapeDtypeStruct((4 * rs, D), BF),
        jax.ShapeDtypeStruct((SMALL, D), F32),
    )
    nx, nz = len(X_FIRST), len(Z_FIRST)
    scratch = [
        pltpu.VMEM((CHUNKS * D + FF, D), BF),
        pltpu.VMEM((CHUNKS, depth, rs, D), BF),
        pltpu.VMEM((nx, depth, rs, HALF), BF),
        pltpu.VMEM((nx, max(depth - 1, 1), rs, HALF), BF),
        pltpu.VMEM((nz, max(depth - 1, 1), rs, D), BF),
        pltpu.VMEM((nz, groups, rs, D), BF),
        pltpu.VMEM((CHUNKS, 2, rs, HALF), BF),
        pltpu.VMEM((nx, teams, rs, HALF) if groups > 2 else (1, 1, 16, 128), BF),
        pltpu.VMEM((tokens, D), BF),
        pltpu.VMEM((tokens, 3 * D), BF),
        pltpu.VMEM((micro * HEADS, seq, seq), BF),
        pltpu.VMEM((tokens, D), BF),
        pltpu.VMEM((tokens, D), BF),
        pltpu.VMEM((tokens, 1), F32),
        pltpu.VMEM((tokens, D), BF),
        pltpu.VMEM((tokens, FF), BF),
        pltpu.VMEM((tokens, FF), BF),
        pltpu.VMEM((tokens, D), BF),
        pltpu.VMEM((tokens, 1), F32),
        pltpu.VMEM((tokens, D), BF),
        pltpu.VMEM((tokens, D), BF),
        pltpu.VMEM((tokens, D), F32),
        pltpu.VMEM((tokens, D), BF),
        pltpu.VMEM((tokens, D), BF),
        pltpu.VMEM((tokens, D), BF),
        pltpu.VMEM((tokens, 3 * D), BF),
        pltpu.VMEM((SMALL, D), F32),
        pltpu.VMEM((SMALL, D), F32),
        pltpu.VMEM((groups, SMALL, D), F32),
        pltpu.VMEM((depth, SMALL, D), F32),
        pltpu.VMEM((SMALL, D), F32),
        pltpu.SemaphoreType.DMA((2,)),
        pltpu.SemaphoreType.DMA((3,)),
        pltpu.SemaphoreType.DMA((CHUNKS, depth)),
        pltpu.SemaphoreType.DMA((CHUNKS, depth)),
        pltpu.SemaphoreType.DMA((CHUNKS,)),
        pltpu.SemaphoreType.DMA((3,)),
        pltpu.SemaphoreType.DMA((2,)),
        pltpu.SemaphoreType.DMA((4,)),
        pltpu.SemaphoreType.DMA((7,)),
        pltpu.SemaphoreType.DMA((CHUNKS,)),
        pltpu.SemaphoreType.DMA((CHUNKS,)),
        pltpu.SemaphoreType.DMA((CHUNKS, max(stages, 1))),
        pltpu.SemaphoreType.DMA((nz, groups)),
        pltpu.SemaphoreType.DMA((CHUNKS,)),
        pltpu.SemaphoreType.DMA((CHUNKS, teams)),
        pltpu.SemaphoreType.DMA((2,)),
        pltpu.SemaphoreType.DMA((2 + groups + depth,)),
    ]
    state, grad_in, *grads, small = pl.pallas_call(
        functools.partial(kernel, (groups, depth, rs, seq)),
        out_shape=out_shape,
        in_specs=[hbm] * 6 + [smem] * 2 + [vmem] * 3,
        out_specs=(hbm,) * 6 + (vmem,),
        scratch_shapes=scratch,
        compiler_params=pltpu.CompilerParams(
            collective_id=0, has_side_effects=True, vmem_limit_bytes=63 * 1024 * 1024
        ),
    )(
        embedded.reshape(tokens, D),
        token_grads.reshape(tokens, D),
        w_qkv[0],
        w_attn_out[0],
        w_up[0],
        w_down[0],
        lengths.reshape(micro),
        score_grads.reshape(micro),
        biases,
        gains[0],
        head_weight,
    )
    results = pl.pallas_call(
        hand_out,
        out_shape=[jax.ShapeDtypeStruct(x.shape, x.dtype) for x in (state, grad_in)]
        + [jax.ShapeDtypeStruct(x.shape, F32) for x in grads]
        + [jax.ShapeDtypeStruct(x, F32) for x in ((1, 10 * D), (2, D), (D,))],
        in_specs=[vmem] * 7,
        out_specs=[vmem] * 9,
    )(state, grad_in, *grads, small)
    state, grad_in, g_qkv, g_attn, g_up, g_down, g_bias, g_gain, g_head = results
    return (
        state.reshape(1, micro, 1, seq, D),
        grad_in.reshape(1, micro, 1, seq, D),
        g_qkv[None],
        g_attn[None],
        g_up[None],
        g_down[None],
        g_bias,
        g_gain[None],
        g_head,
    )


def hand_out(state, grad_in, gq, go, gu, gd, small, o_state, o_gin, o_q, o_o, o_u, o_d, o_bias, o_gain, o_head):
    for src, dst in ((state, o_state), (grad_in, o_gin), (gq, o_q), (go, o_o), (gu, o_u), (gd, o_d)):
        dst[...] = src[...].astype(dst.dtype)
    for k in range(10):
        o_bias[:, pl.ds(k * D, D)] = small[pl.ds(k, 1), :]
    o_gain[...] = small[pl.ds(GAIN1, 2), :]
    o_head[...] = small[HEAD_ROW, :]


def solution(mesh):
    return jax.shard_map(
        functools.partial(on_device, mesh.shape["grp"], mesh.shape["dp"] // 2),
        mesh=mesh,
        in_specs=(
            P(None, ("grp", "dp"), None, None),
            P(None, ("grp", "dp")),
            P(None, ("grp", "dp"), None, None),
            P(None, ("grp", "dp")),
            P("section", "dp", None),
            P("section", "dp", None),
            P("section", "dp", None),
            P("section", "dp", None),
            P("section", None),
            P("section", None, None),
            P(),
        ),
        out_specs=(
            P("section", None, ("grp", "dp"), None, None),
            P("section", None, ("grp", "dp"), None, None),
            P("section", "dp", None),
            P("section", "dp", None),
            P("section", "dp", None),
            P("section", "dp", None),
            P("section", None),
            P("section", None, None),
            P(),
        ),
        check_vma=False,
    )
```

```python
import functools
import math

import jax
import jax.numpy as jnp
from jax import lax
from jax.experimental import pallas as pl
from jax.experimental.pallas import tpu as pltpu
from jax.sharding import PartitionSpec as P

D = 768
FF = 3072
HEADS = 12
HEAD = 64
EPSILON = 1e-06
CHUNKS = 12
HALF = D // 2
DOWN = 8 * D
DOWN_GRAD = 12 * D
SCALE = 1.0 / math.sqrt(HEAD)
F32 = jnp.float32
BF = jnp.bfloat16
MESH = pl.DeviceIdType.MESH
BQ, BV, BO, BU, BD, BETA1, BETA2, GAIN1, GAIN2, HEAD_ROW = 0, 1, 2, 3, 7, 8, 9, 10, 11, 12
SMALL = 16
RELAY = 1
TAKE = (8,)
X_FIRST = (8, 4, 5, 6, 3, 0, 1, 2)
Z_FIRST = (9, 10, 11, 7)
SLOTS = (
    ("x0", (0, 1, 2, 3, 4, 5, 6, 7)),
    ("z0", (0, 2, 4, 6)),
    ("x1", (1, 2, 3, 4, 5, 6, 7, 8)),
    ("z1", (1, 3, 5, 7)),
    ("x2", (2, 3, 4, 5, 6, 7, 8, 9)),
    ("z2", (2, 4, 6, 8)),
    ("x3", (3, 4, 5, 6, 7, 8, 9, 10)),
    ("z3", (3, 5, 7, 9)),
    ("x4", (4, 5, 6, 7, 8, 9, 10, 11)),
)
BESIDE = {"down": 0, "act": 0, "inner": 1, "up": 1, "attend": 2, "hidden": 3, "qkv": 3}
SMALL_STEPS = (4, 5, 6, 8, 10)
STEPS = 1 + max(max(steps) for _, steps in SLOTS)


def dot(a, b):
    return lax.dot_general(a, b, (((1,), (0,)), ((), ())), preferred_element_type=F32)


def dot_t(a, b):
    return lax.dot_general(a, b, (((1,), (1,)), ((), ())), preferred_element_type=F32)


def dot_c(a, b):
    return lax.dot_general(a, b, (((0,), (0,)), ((), ())), preferred_element_type=F32)


def span(i, width):
    return pl.ds(pl.multiple_of(i * width, width), width)


def flip(index, mask):
    bit = 1
    while bit <= mask:
        if mask & bit:
            index = index + bit - 2 * bit * ((index // bit) % 2)
        bit *= 2
    return index


def masks(bits):
    found = [0]
    for bit in bits:
        found = found + [mask ^ bit for mask in found]
    return found


def pick(i, values):
    found = values[-1]
    for k in range(len(values) - 2, -1, -1):
        found = jnp.where(i == k, values[k], found)
    return found


def row_sum(x):
    return jnp.sum(x, 0, keepdims=True)


def gelu_parts(x):
    t = 1.0 / (1.0 + (0.3275911 * math.sqrt(0.5)) * jnp.abs(x))
    e = jnp.exp(-0.5 * x * x)
    tail = t * (0.127414796 + t * (-0.142248368 + t * (0.7107068705 + t * (-0.7265760135 + t * 0.5307027145)))) * e
    phi = jnp.where(x >= 0, 1.0 - tail, tail)
    return x * phi, phi + x * (e * (1.0 / math.sqrt(2.0 * math.pi)))


def normed(x):
    centred = x - jnp.mean(x, -1, keepdims=True)
    scale = lax.rsqrt(jnp.mean(centred * centred, -1, keepdims=True) + EPSILON)
    return centred * scale, scale


def norm_back(grad, n, scale, gain):
    gg = gain * grad
    return (gg - jnp.mean(gg, -1, keepdims=True) - n * jnp.mean(gg * n, -1, keepdims=True)) * scale


def kernel(sizes, *refs):
    groups, depth, rs, seq = sizes
    (emb, token_grads, wq_in, wo_in, wu_in, wd_in, lens, scores, bias, gains, head_w,
     out_sec, out_gin, out_q, out_o, out_u, out_d, out_small,
     big, rb, s1, xr, zr, zw, xw, fin, peers,
     hbuf, qkv, probs, mixed, n1, r1, first_low, act, gp, n2, r2, outb, gbuf, high, dd, da, dm, dqkv,
     small, sm_sib, sm_grp, sm_dp, sm_sec,
     local_sem, io_sem, g_zr, g_xr, g_sr, g_send, b_own, b_zr, b_xr, b_back, b_send, y_send, y_recv,
     r_send, r_sib, r_x, r_z, r_grp, r_fin, r_peer, sm_send, sm_recv) = refs
    stages = depth.bit_length() - 1
    pairs = 2
    sec = lax.axis_index("section")
    g = lax.axis_index("grp")
    d = lax.axis_index("dp")
    z, c = d // 2, d % 2
    par = g % 2
    first_section = sec == 0

    def dev(sec_=None, g_=None, z_=None, c_=None):
        return (
            sec if sec_ is None else sec_,
            g if g_ is None else g_,
            (z if z_ is None else z_) * 2 + (c if c_ is None else c_),
        )

    sibling = dev(c_=1 - c)
    across = dev(g_=g + 1 - 2 * par)
    other = dev(sec_=1 - sec)

    def rcopy(src, dst, send, recv, to):
        return pltpu.make_async_remote_copy(
            src_ref=src, dst_ref=dst, send_sem=send, recv_sem=recv, device_id=to, device_id_type=MESH
        )

    def shard_row(m, owner, down=DOWN):
        row = jnp.where(m < 8, m * D + owner * rs, down + owner * (4 * rs) + (m - 8) * rs)
        return pl.multiple_of(row, 16)

    barrier = pltpu.get_barrier_semaphore()
    greeted = 0
    for to in [sibling, other]:
        pl.semaphore_signal(barrier, inc=1, device_id=to, device_id_type=MESH)
        greeted += 1
    for k in range(1, groups):
        pl.semaphore_signal(barrier, inc=1, device_id=dev(g_=(g + k) % groups), device_id_type=MESH)
        greeted += 1
    for k in range(1, depth):
        pl.semaphore_signal(barrier, inc=1, device_id=dev(z_=(z + k) % depth), device_id_type=MESH)
        greeted += 1

    own = []
    for k in range(3):
        own.append((wq_in.at[:, pl.ds(k * D, D)], k))
    own.append((wo_in, 3))
    for k in range(4):
        own.append((wu_in.at[:, pl.ds(k * D, D)], 4 + k))
    for src, k in own:
        pltpu.make_async_copy(src, big.at[pl.ds(pl.multiple_of(k * D + d * rs, 16), rs), :], local_sem.at[0]).start()
    pltpu.make_async_copy(
        wd_in, big.at[pl.ds(pl.multiple_of(DOWN + d * 4 * rs, 16), 4 * rs), :], local_sem.at[0]
    ).start()

    @pl.when(first_section)
    def _():
        pltpu.make_async_copy(emb, hbuf, local_sem.at[1]).start()

    @pl.when(~first_section)
    def _():
        pltpu.make_async_copy(token_grads, gbuf, local_sem.at[1]).start()

    small[...] = jnp.zeros_like(small)
    pl.semaphore_wait(barrier, greeted)
    pltpu.make_async_copy(
        big.at[pl.ds(0, CHUNKS * rs), :], big.at[pl.ds(0, CHUNKS * rs), :], local_sem.at[0]
    ).wait()

    def region(m, zz, half=None, cc=c):
        cols = slice(None) if half is None else span(half, HALF)
        return big.at[pl.ds(shard_row(m, 2 * zz + cc), rs), cols]

    far = [depth >> (t + 1) for t in range(stages)]
    held = [masks(far[:t]) for t in range(stages + 1)]

    def along(m, zz, t):
        part = region(m, zz, par)
        return rcopy(part, part, g_send.at[0], g_zr.at[m, zz], dev(z_=flip(z, far[t])))

    def over(m, zz, half):
        part = region(m, zz, half)
        return rcopy(part, part, g_send.at[1], g_xr.at[m, zz], across)

    def beside(m, zz, half):
        part = region(m, zz, half)
        return rcopy(part, part, g_send.at[2], g_sr.at[m], sibling)

    def relayed(b, zz, half):
        return rb.at[b, zz, :, span(half, HALF)]

    def lend(b):
        return rcopy(
            region(CHUNKS - RELAY + b, z, par), relayed(b, z, par), b_send.at[0], b_own.at[b], other
        )

    def relay_along(b, zz, t):
        part = relayed(b, zz, par)
        return rcopy(part, part, b_send.at[1], b_zr.at[b, zz], dev(z_=flip(z, far[t])))

    def relay_over(b, zz, half):
        part = relayed(b, zz, half)
        return rcopy(part, part, b_send.at[2], b_xr.at[b, zz], across)

    def give_back(b, zz, half):
        return rcopy(
            relayed(b, zz, half), region(CHUNKS - RELAY + b, zz, half), b_send.at[3], b_back.at[b], other
        )

    def relay_own(b):
        lend(b).wait_recv()
        relay_along(b, z, 0).start()

    def relay_arrived(t, b):
        for mask in held[t]:
            zz = flip(z, far[t] ^ mask)
            relay_along(b, zz, t).wait_recv()
            relay_over(b, zz, par).start()
            give_back(b, zz, par).start()
        if t + 1 < stages:
            for mask in held[t + 1]:
                relay_along(b, flip(z, mask), t + 1).start()

    def relay_crossed(t, b):
        for mask in held[t]:
            zz = flip(z, far[t] ^ mask)
            relay_over(b, zz, 1 - par).wait_recv()
            give_back(b, zz, 1 - par).start()

    def take(b):
        got = big.at[pl.ds(0, (depth - 1) * rs), :]
        rcopy(got, got, b_send.at[3], b_back.at[b], other).wait_recv()
        for k in range(1, depth):
            beside(CHUNKS - RELAY + b, (z + k) % depth, None).start()

    def bias_row(start, width=D):
        return bias[:, pl.ds(start, width)]

    low = lax.broadcasted_iota(jnp.int32, (1, 128), 1) < HEAD
    key = lax.broadcasted_iota(jnp.int32, (1, seq), 1)

    def pair_rows(p):
        return span(p, seq)

    def block(k):
        return big[pl.ds(k * D, D), :]

    def project(p, k):
        r = pair_rows(p)
        x = dot(hbuf[r, :], block(k))
        if k != 1:
            x = x + bias_row(0 if k == 0 else D)
        qkv[r, pl.ds(k * D, D)] = x.astype(BF)

    def attend(p):
        r = pair_rows(p)
        ok = key < lens[p]
        for j in range(HEADS // 2):
            q2 = qkv[r, pl.ds(j * 128, 128)]
            k2 = qkv[r, pl.ds((j + 6) * 128, 128)]
            v2 = qkv[r, pl.ds((j + 12) * 128, 128)]
            none = jnp.zeros_like(q2)
            both = jnp.concatenate([jnp.where(low, q2, none), jnp.where(low, none, q2)], 0)
            sc = jnp.where(ok, dot_t(both, k2) * SCALE, -1e30)
            e = jnp.exp(sc - jnp.max(sc, -1, keepdims=True))
            pr = (e * (1.0 / jnp.sum(e, -1, keepdims=True))).astype(BF)
            probs[p * HEADS + 2 * j] = pr[:seq]
            probs[p * HEADS + 2 * j + 1] = pr[seq:]
            o = dot(pr, v2)
            mixed[r, pl.ds(j * 128, 128)] = jnp.where(low, o[:seq], o[seq:]).astype(BF)

    def join(p):
        r = pair_rows(p)
        n, scale = normed(hbuf[r, :].astype(F32) + dot(mixed[r, :], block(3)) + bias_row(2 * D))
        n1[r, :] = n.astype(BF)
        r1[r, :] = scale
        y = n * gains[0:1, :] + bias_row(4 * D + FF)
        high[r, :] = y
        first_low[r, :] = y.astype(BF)

    def widen(p, k):
        r = pair_rows(p)
        for t in range(3):
            w = big[pl.ds((4 + k) * D, D), pl.ds(t * 256, 256)]
            col = k * D + t * 256
            a, dg = gelu_parts(dot(first_low[r, :], w) + bias_row(3 * D + col, 256))
            act[r, pl.ds(col, 256)] = a.astype(BF)
            gp[r, pl.ds(col, 256)] = dg.astype(BF)

    def narrow(p):
        r = pair_rows(p)
        n, scale = normed(high[r, :] + dot(act[r, :], big[pl.ds(DOWN, FF), :]) + bias_row(3 * D + FF))
        n2[r, :] = n.astype(BF)
        r2[r, :] = scale
        y = n * gains[1:2, :] + bias_row(5 * D + FF)
        outb[r, :] = y.astype(BF)

        @pl.when(~first_section)
        def _():
            small[pl.ds(HEAD_ROW, 1), :] += scores[p] * y[0:1]

    def state_copy(p):
        r = pair_rows(p)
        return rcopy(outb.at[r, :], hbuf.at[r, :], y_send.at[0], y_recv.at[p], other)

    def chunk_ready(m):
        whole = big.at[pl.ds(0, depth * rs), :]
        rcopy(whole, whole, g_send.at[2], g_sr.at[m], sibling).wait_recv()

    def own_step(n):
        if stages:
            along(n, z, 0).start()
        beside(n, z, None).start()

    def arrived(m, t):
        for mask in held[t]:
            zz = flip(z, far[t] ^ mask)
            along(m, zz, t).wait_recv()
            over(m, zz, par).start()
            beside(m, zz, par).start()
        if t + 1 < stages:
            for mask in held[t + 1]:
                along(m, flip(z, mask), t + 1).start()

    def crossed(m, t):
        for mask in held[t]:
            zz = flip(z, far[t] ^ mask)
            over(m, zz, 1 - par).wait_recv()
            beside(m, zz, 1 - par).start()

    def early(step, pieces):
        def run(n):
            @pl.when(first_section & (n == stages + 2 + step))
            def _():
                pieces()

        return run

    def both_pairs(piece):
        @pl.loop(0, pairs)
        def _(p):
            piece(p)

    def early_project(k):
        if k == 0:
            pltpu.make_async_copy(emb, hbuf, local_sem.at[1]).wait()
        chunk_ready(k)
        both_pairs(lambda p: project(p, k))

    def early_join():
        chunk_ready(3)
        both_pairs(join)

    def early_widen(k):
        chunk_ready(4 + k)
        both_pairs(lambda p: widen(p, k))

    plan = [early(k, functools.partial(early_project, k)) for k in range(3)]
    plan.append(early(2, lambda: attend(0)))
    plan.append(early(3, lambda: attend(1)))
    plan.append(early(4, early_join))
    plan += [early(4 + k, functools.partial(early_widen, k)) for k in range(4)]

    mine = jnp.where(first_section, CHUNKS - RELAY, CHUNKS)

    @pl.loop(0, mine + stages + 1)
    def _(n):
        pl.when(n < mine)(functools.partial(own_step, n))

        @pl.when(first_section & (n < RELAY))
        def _():
            lend(n).start()
            beside(CHUNKS - RELAY + n, z, None).start()

        relay_stages = [relay_own]
        for t in range(stages):
            relay_stages.append(functools.partial(relay_arrived, t))
        for lag, stage in enumerate(relay_stages):
            b = n - 1 - lag
            pl.when(~first_section & (b >= 0) & (b < RELAY))(functools.partial(stage, b))
        for t in range(stages):
            b = n - 3 - t
            pl.when(~first_section & (b >= 0) & (b < RELAY))(functools.partial(relay_crossed, t, b))
        for t in range(stages):
            m = n - t - 1
            pl.when((m >= 0) & (m < mine))(functools.partial(arrived, m, t))
        for t in range(stages):
            m = n - t - 2
            pl.when((m >= 0) & (m < mine))(functools.partial(crossed, m, t))
        for b in range(RELAY):
            pl.when(first_section & (n == TAKE[b]))(functools.partial(take, b))
        for run in plan:
            run(n)

    @pl.loop(jnp.where(first_section, 8, 0), CHUNKS)
    def _(m):
        chunk_ready(m)

    @pl.when(first_section)
    def _():
        @pl.loop(0, pairs)
        def _(p):
            narrow(p)
            state_copy(p).start()

    @pl.when(~first_section)
    def _():
        pltpu.make_async_copy(token_grads, gbuf, local_sem.at[1]).wait()

        @pl.loop(0, pairs)
        def _(p):
            state_copy(p).wait_recv()
            for k in range(3):
                project(p, k)
            attend(p)
            join(p)
            for k in range(4):
                widen(p, k)
            narrow(p)

    pltpu.make_async_copy(outb, out_sec, io_sem.at[0]).start()

    for is_first, count in ((first_section, CHUNKS - RELAY), (~first_section, CHUNKS)):

        @pl.when(is_first)
        def _(count=count):
            sent = big.at[pl.ds(0, count * (depth - 1) * rs), pl.ds(0, HALF)]
            rcopy(sent, sent, g_send.at[0], g_zr.at[0, 0], across).wait_send()
            rcopy(sent, sent, g_send.at[1], g_xr.at[0, 0], across).wait_send()

    def relay_sent(k, rows, cols):
        sent = big.at[pl.ds(0, rows), pl.ds(0, cols)]
        rcopy(sent, sent, b_send.at[k], b_own.at[0], other).wait_send()

    @pl.when(first_section)
    def _():
        relay_sent(0, RELAY * rs, HALF)

    @pl.when(~first_section)
    def _():
        relay_sent(1, RELAY * (depth - 1) * rs, HALF)
        relay_sent(2, RELAY * (depth - 1) * rs, HALF)
        relay_sent(3, RELAY * (depth - 1) * rs, D)

    sent = big.at[pl.ds(0, CHUNKS * depth * rs), :]
    rcopy(sent, sent, g_send.at[2], g_sr.at[0], sibling).wait_send()

    def add_small(row, x):
        small[pl.ds(row, 1), :] += row_sum(x)

    def outer_norm(p):
        r = pair_rows(p)
        length = jnp.where(first_section, seq, lens[p])
        score = jnp.where(first_section, 0.0, scores[p])
        place = lax.broadcasted_iota(jnp.int32, (seq, 1), 0)
        grad = jnp.where(place < length, gbuf[r, :].astype(F32), 0.0)
        grad = grad + jnp.where(place == 0, score * head_w[...].reshape(1, D), 0.0)
        n = n2[r, :].astype(F32)
        x = norm_back(grad, n, r2[r, :], gains[1:2, :])
        xl = x.astype(BF)
        high[r, :] = x
        dd[r, :] = xl
        add_small(BD, xl.astype(F32))
        add_small(BETA2, grad)
        add_small(GAIN2, grad * n)

    def act_back(p):
        r = pair_rows(p)
        for k in range(4):
            c4 = pl.ds(k * D, D)
            x = (dot_t(dd[r, :], big[pl.ds(DOWN + k * D, D), :]) * gp[r, c4].astype(F32)).astype(BF)
            gp[r, c4] = x
            add_small(BU + k, x.astype(F32))

    def inner_norm(p):
        r = pair_rows(p)
        grad = high[r, :]
        for k in range(4):
            grad = grad + dot_t(gp[r, pl.ds(k * D, D)], block(4 + k))
        n = n1[r, :].astype(F32)
        x = norm_back(grad, n, r1[r, :], gains[0:1, :])
        xl = x.astype(BF)
        high[r, :] = x
        da[r, :] = xl
        add_small(BO, xl.astype(F32))
        add_small(BETA1, grad)
        add_small(GAIN1, grad * n)
        dm[r, :] = dot_t(xl, block(3)).astype(BF)

    def attend_back(p):
        r = pair_rows(p)
        for j in range(HEADS // 2):
            q2 = qkv[r, pl.ds(j * 128, 128)]
            k2 = qkv[r, pl.ds((j + 6) * 128, 128)]
            v2 = qkv[r, pl.ds((j + 12) * 128, 128)]
            d2 = dm[r, pl.ds(j * 128, 128)]
            none = jnp.zeros_like(d2)
            both = jnp.concatenate([jnp.where(low, d2, none), jnp.where(low, none, d2)], 0)
            pr = jnp.concatenate([probs[p * HEADS + 2 * j], probs[p * HEADS + 2 * j + 1]], 0)
            pf = pr.astype(F32)
            t = pf * dot_t(both, v2)
            ds = (t - pf * jnp.sum(t, -1, keepdims=True)).astype(BF)
            dq = dot(ds, k2)
            dq = (jnp.where(low, dq[:seq], dq[seq:]) * SCALE).astype(BF)
            qt, dt = q2.T, d2.T
            dk = jnp.concatenate([dot(qt[:HEAD], ds[:seq]), dot(qt[HEAD:], ds[seq:])], 0)
            dv = jnp.concatenate([dot(dt[:HEAD], pr[:seq]), dot(dt[HEAD:], pr[seq:])], 0)
            dk = (dk * SCALE).astype(BF).T
            dv = dv.astype(BF).T
            dqkv[r, pl.ds(j * 128, 128)] = dq
            dqkv[r, pl.ds((j + 6) * 128, 128)] = dk
            dqkv[r, pl.ds((j + 12) * 128, 128)] = dv
            small[pl.ds(BQ, 1), pl.ds(j * 128, 128)] += row_sum(dq.astype(F32))
            small[pl.ds(BV, 1), pl.ds(j * 128, 128)] += row_sum(dv.astype(F32))

    def hidden_back(p):
        r = pair_rows(p)
        grad = high[r, :]
        for k in range(3):
            grad = grad + dot_t(dqkv[r, pl.ds(k * D, D)], block(k))
        high[r, :] = grad
        outb[r, :] = grad.astype(BF)

    def grad_copy(p):
        r = pair_rows(p)
        return rcopy(outb.at[r, :], gbuf.at[r, :], y_send.at[1], y_recv.at[2 + p], other)

    def weight_grad(left, lcol, right, rcol, row):
        a = left[:, pl.ds(pl.multiple_of(lcol, 256), D)]
        b = right[:, pl.ds(pl.multiple_of(rcol, 256), D)]
        big[pl.ds(pl.multiple_of(row, 256), D), :] = dot_c(a, b).astype(BF)

    def sib_copy(m, zz):
        return rcopy(
            big.at[pl.ds(shard_row(m, 2 * zz + 1 - c, DOWN_GRAD), rs), :],
            s1.at[m, zz], r_send.at[0], r_sib.at[m], sibling,
        )

    def sib_send(m):
        @pl.loop(0, depth)
        def _(zz):
            sib_copy(m, zz).start()

    def make_down():
        @pl.loop(0, 4)
        def _(k):
            weight_grad(act, k * D, dd, 0, DOWN_GRAD + k * D)

        @pl.loop(8, 12)
        def _(m):
            sib_send(m)

    def make_up(k):
        weight_grad(first_low, 0, gp, k * D, (4 + k) * D)
        sib_send(4 + k)

    def make_attn():
        weight_grad(mixed, 0, da, 0, 3 * D)
        sib_send(3)

    def make_qkv(k):
        weight_grad(hbuf, 0, dqkv, k * D, k * D)
        sib_send(k)

    def pair_sums(m):
        rcopy(s1.at[m], s1.at[m], r_send.at[0], r_sib.at[m], sibling).wait_recv()

        @pl.loop(0, depth)
        def _(zz):
            mine = big[pl.ds(shard_row(m, 2 * zz + c, DOWN_GRAD), rs), :]
            s1[m, zz] = (mine.astype(F32) + s1[m, zz].astype(F32)).astype(BF)

    sides = [masks([2 << k for k in range(t, stages - 1)]) for t in range(stages)]
    slots = [sum(len(side) for side in sides[:t]) for t in range(stages)]

    def line_send(part, landing, m, t, send):
        for k, mask in enumerate(sides[t]):
            rcopy(
                part.at[flip(z, (1 << t) ^ mask)], landing.at[slots[t] + k], send, r_z.at[m, t],
                dev(z_=flip(z, 1 << t)),
            ).start()

    def line_add(part, landing, m, t, send):
        here = landing.at[pl.ds(slots[t], len(sides[t]))]
        rcopy(here, here, send, r_z.at[m, t], dev(z_=flip(z, 1 << t))).wait_recv()
        for k, mask in enumerate(sides[t]):
            zz = flip(z, mask)
            part[zz] = (part[zz].astype(F32) + landing[slots[t] + k].astype(F32)).astype(BF)

    def put_out(m):
        def put(to, row, col):
            for h in range(2):
                rows = pl.ds(pl.multiple_of(row, 16), rs)
                cols = pl.ds(pl.multiple_of(col + h * HALF, 128), HALF)
                pltpu.make_async_copy(fin.at[m, h], to.at[rows, cols], io_sem.at[2]).start()

        pl.when(m >= 8)(lambda: put(out_d, (m - 8) * rs, 0))
        pl.when((m >= 4) & (m < 8))(lambda: put(out_u, 0, (m - 4) * D))
        pl.when(m == 3)(lambda: put(out_o, 0, 0))
        pl.when(m < 3)(lambda: put(out_q, 0, m * D))

    def x_copy(q, m):
        return rcopy(
            s1.at[m, :, :, span(1 - par, HALF)], xr.at[q], r_send.at[1], r_x.at[m], across
        )

    def fin_copy(m):
        return rcopy(fin.at[m, par], fin.at[m, par], r_send.at[4], r_fin.at[m], across)

    def x_start(q, m):
        pair_sums(m)
        x_copy(q, m).start()

    def x_halves(q, m):
        x_copy(q, m).wait_recv()

        @pl.loop(0, depth)
        def _(zz):
            mine = s1[m, zz, :, span(par, HALF)]
            xr[q, zz] = (mine.astype(F32) + xr[q, zz].astype(F32)).astype(BF)

        line_send(xr.at[q], zr.at[q], m, 0, r_send.at[2])

    def lines(part, landing, m, ts, send):
        for t in ts:
            line_add(part, landing, m, t, send)
            if t + 1 < stages:
                line_send(part, landing, m, t + 1, send)

    def x_line(ts, q, m):
        lines(xr.at[q], zr.at[q], m, ts, r_send.at[2])
        if stages - 1 not in ts:
            return
        total = xr[q, z]
        if groups > 2:
            teams = groups // 2
            team = g // 2
            peers[q, team] = total
            for k in range(1, teams):
                to = dev(g_=((team + k) % teams) * 2 + par)
                rcopy(peers.at[q, team], peers.at[q, team], r_send.at[5], r_peer.at[m, team], to).start()
            for k in range(1, teams):
                tt = (team + k) % teams
                rcopy(peers.at[q, tt], peers.at[q, tt], r_send.at[5], r_peer.at[m, tt], across).wait_recv()
            total = peers[q, 0].astype(F32)
            for k in range(1, teams):
                total = total + peers[q, k].astype(F32)
            total = total.astype(BF)
        fin[m, par] = total
        fin_copy(m).start()

    def x_finish(q, m):
        rcopy(fin.at[m, 1 - par], fin.at[m, 1 - par], r_send.at[4], r_fin.at[m], across).wait_recv()
        put_out(m)

    def z_start(q, m):
        pair_sums(m)
        line_send(s1.at[m], zw.at[q], m, 0, r_send.at[3])

    def z_line(ts, q, m):
        lines(s1.at[m], zw.at[q], m, ts, r_send.at[3])
        if stages - 1 not in ts:
            return
        xw[q, g] = s1[m, z]
        for k in range(1, groups):
            rcopy(xw.at[q, g], xw.at[q, g], r_send.at[6], r_grp.at[q, g], dev(g_=(g + k) % groups)).start()

    def z_finish(q, m):
        for k in range(1, groups):
            gg = (g + k) % groups
            rcopy(xw.at[q, gg], xw.at[q, gg], r_send.at[6], r_grp.at[q, gg], across).wait_recv()
        total = xw[q, 0].astype(F32)
        for k in range(1, groups):
            total = total + xw[q, k].astype(F32)
        total = total.astype(BF)
        fin[m, 0] = total[:, :HALF]
        fin[m, 1] = total[:, HALF:]
        put_out(m)

    first_line, last_lines = range(0, 1), range(1, stages)
    if stages == 1:
        first_line, last_lines = range(0, 0), range(0, 1)
    x_stages = [
        x_start, x_halves, functools.partial(x_line, first_line), functools.partial(x_line, last_lines), x_finish
    ]
    z_stages = [z_start, functools.partial(z_line, first_line), functools.partial(z_line, last_lines), z_finish]

    pltpu.make_async_copy(outb, out_sec, io_sem.at[0]).wait()

    @pl.when(first_section)
    def _():
        rcopy(outb, outb, y_send.at[0], y_recv.at[0], other).wait_send()

    last = pairs - 1

    @pl.loop(0, jnp.where(first_section, last, pairs))
    def _(p):
        @pl.when(first_section)
        def _():
            grad_copy(p).wait_recv()

        outer_norm(p)
        act_back(p)
        inner_norm(p)
        attend_back(p)
        hidden_back(p)

        @pl.when(~first_section)
        def _():
            grad_copy(p).start()

    def sm_copy(src, dst, recv, to):
        return rcopy(src, dst, sm_send.at[0], recv, to)

    def small_sib():
        sm_copy(small, sm_sib, sm_recv.at[0], sibling).start()

    def small_grp():
        sm_copy(small, sm_sib, sm_recv.at[0], sibling).wait_recv()
        sm_grp[g] = small[...] + sm_sib[...]
        for k in range(1, groups):
            sm_copy(sm_grp.at[g], sm_grp.at[g], sm_recv.at[1 + g], dev(g_=(g + k) % groups)).start()

    def small_dp():
        for k in range(1, groups):
            gg = (g + k) % groups
            sm_copy(sm_grp.at[gg], sm_grp.at[gg], sm_recv.at[1 + gg], across).wait_recv()
        total = sm_grp[0]
        for k in range(1, groups):
            total = total + sm_grp[k]
        sm_dp[z] = total
        for k in range(1, depth):
            sm_copy(sm_dp.at[z], sm_dp.at[z], sm_recv.at[1 + groups + z], dev(z_=(z + k) % depth)).start()

    def head_copy():
        return rcopy(out_small, sm_sec, sm_send.at[1], sm_recv.at[1 + groups + depth], other)

    def small_sec():
        for k in range(1, depth):
            zz = (z + k) % depth
            sm_copy(sm_dp.at[zz], sm_dp.at[zz], sm_recv.at[1 + groups + zz], across).wait_recv()
        total = sm_dp[0]
        for k in range(1, depth):
            total = total + sm_dp[k]
        out_small[...] = total

        @pl.when(~first_section)
        def _():
            head_copy().start()

    def small_head():
        @pl.when(first_section)
        def _():
            head_copy().wait_recv()
            out_small[pl.ds(HEAD_ROW, 1), :] = sm_sec[pl.ds(HEAD_ROW, 1), :]

        @pl.when(~first_section)
        def _():
            head_copy().wait_send()

    def make_inner():
        @pl.loop(0, 4)
        def _(k):
            make_up(k)

    def make_outer():
        make_attn()

        @pl.loop(0, 3)
        def _(k):
            make_qkv(k)

        pltpu.make_async_copy(high, out_gin, io_sem.at[1]).start()

    beside = (
        ("down", make_down, False),
        ("act", act_back, True),
        ("inner", inner_norm, True),
        ("up", make_inner, False),
        ("attend", attend_back, True),
        ("hidden", hidden_back, True),
        ("qkv", make_outer, False),
    )
    smalls = (small_sib, small_grp, small_dp, small_sec, small_head)

    @pl.when(first_section)
    def _():
        grad_copy(last).wait_recv()
        outer_norm(last)

    @pl.loop(0, STEPS)
    def _(i):
        for name, part, inside in beside:
            if inside:
                pl.when(first_section & (i == BESIDE[name]))(functools.partial(part, last))
            else:
                pl.when(i == BESIDE[name])(part)
        for step, part in zip(SMALL_STEPS, smalls):
            pl.when(i == step)(part)
        for name, at in SLOTS:
            chunks, parts = (X_FIRST, x_stages) if name[0] == "x" else (Z_FIRST, z_stages)
            q = jnp.int32(-1)
            for k, step in enumerate(at):
                q = jnp.where(i == step, k, q)

            @pl.when(q >= 0)
            def _(q=q, chunks=chunks, part=parts[int(name[1])]):
                part(q, pick(q, chunks))

    count = 1 + (groups - 1) + (depth - 1)
    sent = high.at[pl.ds(0, count * SMALL), :]
    rcopy(sent, sent, sm_send.at[0], sm_recv.at[0], other).wait_send()

    @pl.when(~first_section)
    def _():
        rcopy(outb, outb, y_send.at[1], y_recv.at[0], other).wait_send()

    pltpu.make_async_copy(high, out_gin, io_sem.at[1]).wait()
    pltpu.make_async_copy(fin, fin, io_sem.at[2]).wait()
    rcopy(s1, s1, r_send.at[0], r_sib.at[0], sibling).wait_send()
    rcopy(xr, xr, r_send.at[1], r_x.at[0], across).wait_send()
    if stages:
        rcopy(zr, zr, r_send.at[2], r_z.at[0, 0], across).wait_send()
        rcopy(zw, zw, r_send.at[3], r_z.at[0, 0], across).wait_send()
    part = fin.at[pl.ds(0, len(X_FIRST)), 0]
    rcopy(part, part, r_send.at[4], r_fin.at[0], across).wait_send()
    if groups > 2:
        part = peers.at[:, pl.ds(0, groups // 2 - 1)]
        rcopy(part, part, r_send.at[5], r_peer.at[0, 0], across).wait_send()
    part = xw.at[:, pl.ds(0, groups - 1)]
    rcopy(part, part, r_send.at[6], r_grp.at[0, 0], across).wait_send()


def on_device(groups, depth, embedded, lengths, token_grads, score_grads, w_qkv, w_attn_out, w_up, w_down, biases, gains, head_weight):
    micro, _, seq, _ = embedded.shape
    tokens = micro * seq
    rs = w_qkv.shape[1]
    vmem = pl.BlockSpec(memory_space=pltpu.VMEM)
    smem = pl.BlockSpec(memory_space=pltpu.SMEM)
    hbm = pl.BlockSpec(memory_space=pl.ANY)
    teams = max(groups // 2, 1)
    stages = depth.bit_length() - 1
    out_shape = (
        jax.ShapeDtypeStruct((tokens, D), BF),
        jax.ShapeDtypeStruct((tokens, D), F32),
        jax.ShapeDtypeStruct((rs, 3 * D), BF),
        jax.ShapeDtypeStruct((rs, D), BF),
        jax.ShapeDtypeStruct((rs, FF), BF),
        jax.ShapeDtypeStruct((4 * rs, D), BF),
        jax.ShapeDtypeStruct((SMALL, D), F32),
    )
    nx, nz = len(X_FIRST), len(Z_FIRST)
    scratch = [
        pltpu.VMEM((CHUNKS * D + FF, D), BF),
        pltpu.VMEM((RELAY, depth, rs, D), BF),
        pltpu.VMEM((CHUNKS, depth, rs, D), BF),
        pltpu.VMEM((nx, depth, rs, HALF), BF),
        pltpu.VMEM((nx, max(depth - 1, 1), rs, HALF), BF),
        pltpu.VMEM((nz, max(depth - 1, 1), rs, D), BF),
        pltpu.VMEM((nz, groups, rs, D), BF),
        pltpu.VMEM((CHUNKS, 2, rs, HALF), BF),
        pltpu.VMEM((nx, teams, rs, HALF) if groups > 2 else (1, 1, 16, 128), BF),
        pltpu.VMEM((tokens, D), BF),
        pltpu.VMEM((tokens, 3 * D), BF),
        pltpu.VMEM((micro * HEADS, seq, seq), BF),
        pltpu.VMEM((tokens, D), BF),
        pltpu.VMEM((tokens, D), BF),
        pltpu.VMEM((tokens, 1), F32),
        pltpu.VMEM((tokens, D), BF),
        pltpu.VMEM((tokens, FF), BF),
        pltpu.VMEM((tokens, FF), BF),
        pltpu.VMEM((tokens, D), BF),
        pltpu.VMEM((tokens, 1), F32),
        pltpu.VMEM((tokens, D), BF),
        pltpu.VMEM((tokens, D), BF),
        pltpu.VMEM((tokens, D), F32),
        pltpu.VMEM((tokens, D), BF),
        pltpu.VMEM((tokens, D), BF),
        pltpu.VMEM((tokens, D), BF),
        pltpu.VMEM((tokens, 3 * D), BF),
        pltpu.VMEM((SMALL, D), F32),
        pltpu.VMEM((SMALL, D), F32),
        pltpu.VMEM((groups, SMALL, D), F32),
        pltpu.VMEM((depth, SMALL, D), F32),
        pltpu.VMEM((SMALL, D), F32),
        pltpu.SemaphoreType.DMA((2,)),
        pltpu.SemaphoreType.DMA((3,)),
        pltpu.SemaphoreType.DMA((CHUNKS, depth)),
        pltpu.SemaphoreType.DMA((CHUNKS, depth)),
        pltpu.SemaphoreType.DMA((CHUNKS,)),
        pltpu.SemaphoreType.DMA((3,)),
        pltpu.SemaphoreType.DMA((RELAY,)),
        pltpu.SemaphoreType.DMA((RELAY, depth)),
        pltpu.SemaphoreType.DMA((RELAY, depth)),
        pltpu.SemaphoreType.DMA((RELAY,)),
        pltpu.SemaphoreType.DMA((4,)),
        pltpu.SemaphoreType.DMA((2,)),
        pltpu.SemaphoreType.DMA((4,)),
        pltpu.SemaphoreType.DMA((7,)),
        pltpu.SemaphoreType.DMA((CHUNKS,)),
        pltpu.SemaphoreType.DMA((CHUNKS,)),
        pltpu.SemaphoreType.DMA((CHUNKS, max(stages, 1))),
        pltpu.SemaphoreType.DMA((nz, groups)),
        pltpu.SemaphoreType.DMA((CHUNKS,)),
        pltpu.SemaphoreType.DMA((CHUNKS, teams)),
        pltpu.SemaphoreType.DMA((2,)),
        pltpu.SemaphoreType.DMA((2 + groups + depth,)),
    ]
    state, grad_in, *grads, small = pl.pallas_call(
        functools.partial(kernel, (groups, depth, rs, seq)),
        out_shape=out_shape,
        in_specs=[hbm] * 6 + [smem] * 2 + [vmem] * 3,
        out_specs=(hbm,) * 6 + (vmem,),
        scratch_shapes=scratch,
        compiler_params=pltpu.CompilerParams(
            collective_id=0, has_side_effects=True, vmem_limit_bytes=63 * 1024 * 1024
        ),
    )(
        embedded.reshape(tokens, D),
        token_grads.reshape(tokens, D),
        w_qkv[0],
        w_attn_out[0],
        w_up[0],
        w_down[0],
        lengths.reshape(micro),
        score_grads.reshape(micro),
        biases,
        gains[0],
        head_weight,
    )
    results = pl.pallas_call(
        hand_out,
        out_shape=[jax.ShapeDtypeStruct(x.shape, x.dtype) for x in (state, grad_in)]
        + [jax.ShapeDtypeStruct(x.shape, F32) for x in grads]
        + [jax.ShapeDtypeStruct(x, F32) for x in ((1, 10 * D), (2, D), (D,))],
        in_specs=[vmem] * 7,
        out_specs=[vmem] * 9,
    )(state, grad_in, *grads, small)
    state, grad_in, g_qkv, g_attn, g_up, g_down, g_bias, g_gain, g_head = results
    return (
        state.reshape(1, micro, 1, seq, D),
        grad_in.reshape(1, micro, 1, seq, D),
        g_qkv[None],
        g_attn[None],
        g_up[None],
        g_down[None],
        g_bias,
        g_gain[None],
        g_head,
    )


def hand_out(state, grad_in, gq, go, gu, gd, small, o_state, o_gin, o_q, o_o, o_u, o_d, o_bias, o_gain, o_head):
    for src, dst in ((state, o_state), (grad_in, o_gin), (gq, o_q), (go, o_o), (gu, o_u), (gd, o_d)):
        dst[...] = src[...].astype(dst.dtype)
    for k in range(10):
        o_bias[:, pl.ds(k * D, D)] = small[pl.ds(k, 1), :]
    o_gain[...] = small[pl.ds(GAIN1, 2), :]
    o_head[...] = small[HEAD_ROW, :]


def solution(mesh):
    return jax.shard_map(
        functools.partial(on_device, mesh.shape["grp"], mesh.shape["dp"] // 2),
        mesh=mesh,
        in_specs=(
            P(None, ("grp", "dp"), None, None),
            P(None, ("grp", "dp")),
            P(None, ("grp", "dp"), None, None),
            P(None, ("grp", "dp")),
            P("section", "dp", None),
            P("section", "dp", None),
            P("section", "dp", None),
            P("section", "dp", None),
            P("section", None),
            P("section", None, None),
            P(),
        ),
        out_specs=(
            P("section", None, ("grp", "dp"), None, None),
            P("section", None, ("grp", "dp"), None, None),
            P("section", "dp", None),
            P("section", "dp", None),
            P("section", "dp", None),
            P("section", "dp", None),
            P("section", None),
            P("section", None, None),
            P(),
        ),
        check_vma=False,
    )
```

```python
import functools
import math

import jax
import jax.numpy as jnp
from jax import lax
from jax.experimental import pallas as pl
from jax.experimental.pallas import tpu as pltpu
from jax.sharding import PartitionSpec as P

D = 768
FF = 3072
HEADS = 12
HEAD = 64
EPSILON = 1e-06
CHUNKS = 12
HALF = D // 2
DOWN = 8 * D
DOWN_GRAD = 12 * D
SCALE = 1.0 / math.sqrt(HEAD)
F32 = jnp.float32
BF = jnp.bfloat16
MESH = pl.DeviceIdType.MESH
BQ, BV, BO, BU, BD, BETA1, BETA2, GAIN1, GAIN2, HEAD_ROW = 0, 1, 2, 3, 7, 8, 9, 10, 11, 12
SMALL = 16
RELAY = 1
TAKE = (8,)
X_FIRST = (8, 4, 5, 6, 7, 3, 0, 1, 2)
Z_FIRST = (9, 10, 11)
SLOTS = (
    ("x0", (0, 2, 1, 4, 3, 6, 5, 7, 9)),
    ("z0", (0, 3, 2)),
    ("z3", (14, 15, 17)),
    ("x4", (8, 12, 9, 13, 11, 14, 15, 16, 17)),
    ("x3", (6, 9, 7, 11, 8, 12, 13, 14, 15)),
    ("z2", (4, 11, 13)),
    ("x2", (3, 6, 4, 8, 7, 9, 11, 12, 13)),
    ("z1", (2, 5, 7)),
    ("x1", (1, 3, 2, 5, 4, 7, 8, 10, 11)),
)
BESIDE = {"down": 0, "act": 1, "inner": 1, "up": 1, "attend": 3, "hidden": 4, "qkv": 5}
SMALL_STEPS = (4, 5, 6, 8, 10)
STEPS = 1 + max(max(steps) for _, steps in SLOTS)


def dot(a, b):
    return lax.dot_general(a, b, (((1,), (0,)), ((), ())), preferred_element_type=F32)


def dot_t(a, b):
    return lax.dot_general(a, b, (((1,), (1,)), ((), ())), preferred_element_type=F32)


def dot_c(a, b):
    return lax.dot_general(a, b, (((0,), (0,)), ((), ())), preferred_element_type=F32)


def span(i, width):
    return pl.ds(pl.multiple_of(i * width, width), width)


def flip(index, mask):
    bit = 1
    while bit <= mask:
        if mask & bit:
            index = index + bit - 2 * bit * ((index // bit) % 2)
        bit *= 2
    return index


def masks(bits):
    found = [0]
    for bit in bits:
        found = found + [mask ^ bit for mask in found]
    return found


def pick(i, values):
    found = values[-1]
    for k in range(len(values) - 2, -1, -1):
        found = jnp.where(i == k, values[k], found)
    return found


def row_sum(x):
    return jnp.sum(x, 0, keepdims=True)


def gelu_parts(x):
    t = 1.0 / (1.0 + (0.3275911 * math.sqrt(0.5)) * jnp.abs(x))
    e = jnp.exp2((-0.5 * math.log2(math.e)) * (x * x))
    tail = t * (0.127414796 + t * (-0.142248368 + t * (0.7107068705 + t * (-0.7265760135 + t * 0.5307027145)))) * e
    phi = jnp.where(x >= 0, 1.0 - tail, tail)
    return x * phi, phi + x * (e * (1.0 / math.sqrt(2.0 * math.pi)))


def normed(x):
    centred = x - jnp.mean(x, -1, keepdims=True)
    scale = lax.rsqrt(jnp.mean(centred * centred, -1, keepdims=True) + EPSILON)
    return centred * scale, scale


def norm_back(grad, n, scale, gain):
    gg = gain * grad
    return (gg - jnp.mean(gg, -1, keepdims=True) - n * jnp.mean(gg * n, -1, keepdims=True)) * scale


def kernel(sizes, *refs):
    groups, depth, rs, seq = sizes
    (emb, token_grads, wq_in, wo_in, wu_in, wd_in, lens, scores, bias, gains, head_w,
     out_sec, out_gin, out_q, out_o, out_u, out_d, out_small,
     big, s1, xr, zr, zw, xw, fin, peers,
     hbuf, qkv, probs, mixed, n1, r1, first_low, act, gp, n2, r2, outb, gbuf, high, dd, da, dm, dqkv,
     small, sm_sib, sm_grp, sm_dp, sm_sec,
     local_sem, io_sem, g_zr, g_xr, g_sr, g_send, b_own, b_zr, b_xr, b_back, b_send, y_send, y_recv,
     r_send, r_sib, r_x, r_z, r_grp, r_fin, r_peer, sm_send, sm_recv) = refs
    stages = depth.bit_length() - 1
    pairs = 2
    sec = lax.axis_index("section")
    g = lax.axis_index("grp")
    d = lax.axis_index("dp")
    z, c = d // 2, d % 2
    par = g % 2
    first_section = sec == 0

    def dev(sec_=None, g_=None, z_=None, c_=None):
        return (
            sec if sec_ is None else sec_,
            g if g_ is None else g_,
            (z if z_ is None else z_) * 2 + (c if c_ is None else c_),
        )

    sibling = dev(c_=1 - c)
    across = dev(g_=g + 1 - 2 * par)
    other = dev(sec_=1 - sec)

    def rcopy(src, dst, send, recv, to):
        return pltpu.make_async_remote_copy(
            src_ref=src, dst_ref=dst, send_sem=send, recv_sem=recv, device_id=to, device_id_type=MESH
        )

    def shard_row(m, owner, down=DOWN):
        row = jnp.where(m < 8, m * D + owner * rs, down + owner * (4 * rs) + (m - 8) * rs)
        return pl.multiple_of(row, 16)

    barrier = pltpu.get_barrier_semaphore()
    greeted = 0
    for to in [sibling, other]:
        pl.semaphore_signal(barrier, inc=1, device_id=to, device_id_type=MESH)
        greeted += 1
    for k in range(1, groups):
        pl.semaphore_signal(barrier, inc=1, device_id=dev(g_=(g + k) % groups), device_id_type=MESH)
        greeted += 1
    for k in range(1, depth):
        pl.semaphore_signal(barrier, inc=1, device_id=dev(z_=(z + k) % depth), device_id_type=MESH)
        greeted += 1

    own = []
    for k in range(3):
        own.append((wq_in.at[:, pl.ds(k * D, D)], k))
    own.append((wo_in, 3))
    for k in range(4):
        own.append((wu_in.at[:, pl.ds(k * D, D)], 4 + k))
    for src, k in own:
        pltpu.make_async_copy(src, big.at[pl.ds(pl.multiple_of(k * D + d * rs, 16), rs), :], local_sem.at[0]).start()
    pltpu.make_async_copy(
        wd_in, big.at[pl.ds(pl.multiple_of(DOWN + d * 4 * rs, 16), 4 * rs), :], local_sem.at[0]
    ).start()

    @pl.when(first_section)
    def _():
        pltpu.make_async_copy(emb, hbuf, local_sem.at[1]).start()

    @pl.when(~first_section)
    def _():
        pltpu.make_async_copy(token_grads, gbuf, local_sem.at[1]).start()

    small[...] = jnp.zeros_like(small)
    pl.semaphore_wait(barrier, greeted)
    pltpu.make_async_copy(
        big.at[pl.ds(0, CHUNKS * rs), :], big.at[pl.ds(0, CHUNKS * rs), :], local_sem.at[0]
    ).wait()

    def region(m, zz, half=None, cc=c):
        cols = slice(None) if half is None else span(half, HALF)
        return big.at[pl.ds(shard_row(m, 2 * zz + cc), rs), cols]

    far = [depth >> (t + 1) for t in range(stages)]
    held = [masks(far[:t]) for t in range(stages + 1)]

    def along(m, zz, t):
        part = region(m, zz, par)
        return rcopy(part, part, g_send.at[0], g_zr.at[m, zz], dev(z_=flip(z, far[t])))

    def over(m, zz, half):
        part = region(m, zz, half)
        return rcopy(part, part, g_send.at[1], g_xr.at[m, zz], across)

    def beside(m, zz, half):
        part = region(m, zz, half)
        return rcopy(part, part, g_send.at[2], g_sr.at[m], sibling)

    def relayed(b, zz, half):
        return dd.at[pl.ds(pl.multiple_of((b * depth + zz) * rs, 16), rs), span(half, HALF)]

    def lend(b):
        return rcopy(
            region(CHUNKS - RELAY + b, z, par), relayed(b, z, par), b_send.at[0], b_own.at[b], other
        )

    def relay_along(b, zz, t):
        part = relayed(b, zz, par)
        return rcopy(part, part, b_send.at[1], b_zr.at[b, zz], dev(z_=flip(z, far[t])))

    def relay_over(b, zz, half):
        part = relayed(b, zz, half)
        return rcopy(part, part, b_send.at[2], b_xr.at[b, zz], across)

    def give_back(b, zz, half):
        return rcopy(
            relayed(b, zz, half), region(CHUNKS - RELAY + b, zz, half), b_send.at[3], b_back.at[b], other
        )

    def relay_own(b):
        lend(b).wait_recv()
        relay_along(b, z, 0).start()

    def relay_arrived(t, b):
        for mask in held[t]:
            zz = flip(z, far[t] ^ mask)
            relay_along(b, zz, t).wait_recv()
            relay_over(b, zz, par).start()
            give_back(b, zz, par).start()
        if t + 1 < stages:
            for mask in held[t + 1]:
                relay_along(b, flip(z, mask), t + 1).start()

    def relay_crossed(t, b):
        for mask in held[t]:
            zz = flip(z, far[t] ^ mask)
            relay_over(b, zz, 1 - par).wait_recv()
            give_back(b, zz, 1 - par).start()

    def take(b):
        got = big.at[pl.ds(0, (depth - 1) * rs), :]
        rcopy(got, got, b_send.at[3], b_back.at[b], other).wait_recv()
        for k in range(1, depth):
            beside(CHUNKS - RELAY + b, (z + k) % depth, None).start()

    def bias_row(start, width=D):
        return bias[:, pl.ds(start, width)]

    low = lax.broadcasted_iota(jnp.int32, (1, 128), 1) < HEAD
    key = lax.broadcasted_iota(jnp.int32, (1, seq), 1)

    def pair_rows(p):
        return span(p, seq)

    def block(k):
        return big[pl.ds(k * D, D), :]

    def project(p, k):
        r = pair_rows(p)
        x = dot(hbuf[r, :], block(k))
        if k != 1:
            x = x + bias_row(0 if k == 0 else D)
        qkv[r, pl.ds(k * D, D)] = x.astype(BF)

    def both_heads(x):
        none = jnp.zeros_like(x)
        return jnp.concatenate([jnp.where(low, x, none), jnp.where(low, none, x)], 0)

    def ahead(make):
        coming = make(0)
        for j in range(HEADS // 2):
            now, coming = coming, make(j + 1) if j + 1 < HEADS // 2 else None
            yield j, now

    def attend(p):
        r = pair_rows(p)
        ok = key < lens[p]

        def scores_of(j):
            q2 = qkv[r, pl.ds(j * 128, 128)] * jnp.asarray(SCALE, BF)
            return dot_t(both_heads(q2), qkv[r, pl.ds((j + 6) * 128, 128)])

        for j, sc in ahead(scores_of):
            sc = jnp.where(ok, sc, -1e30)
            e = jnp.exp(sc - jnp.max(sc, -1, keepdims=True))
            pr = (e * (1.0 / jnp.sum(e, -1, keepdims=True))).astype(BF)
            probs[p * HEADS + 2 * j] = pr[:seq]
            probs[p * HEADS + 2 * j + 1] = pr[seq:]
            o = dot(pr, qkv[r, pl.ds((j + 12) * 128, 128)])
            mixed[r, pl.ds(j * 128, 128)] = jnp.where(low, o[:seq], o[seq:]).astype(BF)

    def join(p):
        r = pair_rows(p)
        n, scale = normed(hbuf[r, :].astype(F32) + dot(mixed[r, :], block(3)) + bias_row(2 * D))
        n1[r, :] = n.astype(BF)
        r1[r, :] = scale
        y = n * gains[0:1, :] + bias_row(4 * D + FF)
        high[r, :] = y
        first_low[r, :] = y.astype(BF)

    def widen(p, k):
        r = pair_rows(p)
        for t in range(3):
            w = big[pl.ds((4 + k) * D, D), pl.ds(t * 256, 256)]
            col = k * D + t * 256
            a, dg = gelu_parts(dot(first_low[r, :], w) + bias_row(3 * D + col, 256))
            act[r, pl.ds(col, 256)] = a.astype(BF)
            gp[r, pl.ds(col, 256)] = dg.astype(BF)

    def narrow(p):
        r = pair_rows(p)
        n, scale = normed(high[r, :] + dot(act[r, :], big[pl.ds(DOWN, FF), :]) + bias_row(3 * D + FF))
        n2[r, :] = n.astype(BF)
        r2[r, :] = scale
        y = n * gains[1:2, :] + bias_row(5 * D + FF)
        outb[r, :] = y.astype(BF)

        @pl.when(~first_section)
        def _():
            small[pl.ds(HEAD_ROW, 1), :] += scores[p] * y[0:1]

    def state_copy(p):
        r = pair_rows(p)
        return rcopy(outb.at[r, :], hbuf.at[r, :], y_send.at[p], y_recv.at[p], other)

    def out_copy(p):
        r = pair_rows(p)
        return pltpu.make_async_copy(outb.at[r, :], out_sec.at[r, :], io_sem.at[p])

    def chunk_ready(m):
        whole = big.at[pl.ds(0, depth * rs), :]
        rcopy(whole, whole, g_send.at[2], g_sr.at[m], sibling).wait_recv()

    def own_step(n):
        if stages:
            along(n, z, 0).start()
        beside(n, z, None).start()

    def arrived(m, t):
        for mask in held[t]:
            zz = flip(z, far[t] ^ mask)
            along(m, zz, t).wait_recv()
            over(m, zz, par).start()
            beside(m, zz, par).start()
        if t + 1 < stages:
            for mask in held[t + 1]:
                along(m, flip(z, mask), t + 1).start()

    def crossed(m, t):
        for mask in held[t]:
            zz = flip(z, far[t] ^ mask)
            over(m, zz, 1 - par).wait_recv()
            beside(m, zz, 1 - par).start()

    def early(step, pieces):
        def run(n):
            @pl.when(first_section & (n == stages + 2 + step))
            def _():
                pieces()

        return run

    def both_pairs(piece):
        @pl.loop(0, pairs)
        def _(p):
            piece(p)

    def early_project(k):
        if k == 0:
            pltpu.make_async_copy(emb, hbuf, local_sem.at[1]).wait()
        chunk_ready(k)
        both_pairs(lambda p: project(p, k))

    def early_join():
        chunk_ready(3)
        both_pairs(join)

    def early_widen(k):
        chunk_ready(4 + k)
        both_pairs(lambda p: widen(p, k))

    plan = [early(k, functools.partial(early_project, k)) for k in range(3)]
    plan.append(early(2, lambda: attend(0)))
    plan.append(early(3, lambda: attend(1)))
    plan.append(early(4, early_join))
    plan += [early(4 + k, functools.partial(early_widen, k)) for k in range(4)]

    mine = jnp.where(first_section, CHUNKS - RELAY, CHUNKS)

    @pl.loop(0, mine + stages + 1)
    def _(n):
        pl.when(n < mine)(functools.partial(own_step, n))

        @pl.when(first_section & (n < RELAY))
        def _():
            lend(n).start()
            beside(CHUNKS - RELAY + n, z, None).start()

        relay_stages = [relay_own]
        for t in range(stages):
            relay_stages.append(functools.partial(relay_arrived, t))
        for lag, stage in enumerate(relay_stages):
            b = n - 1 - lag
            pl.when(~first_section & (b >= 0) & (b < RELAY))(functools.partial(stage, b))
        for t in range(stages):
            b = n - 3 - t
            pl.when(~first_section & (b >= 0) & (b < RELAY))(functools.partial(relay_crossed, t, b))
        for t in range(stages):
            m = n - t - 1
            pl.when((m >= 0) & (m < mine))(functools.partial(arrived, m, t))
        for t in range(stages):
            m = n - t - 2
            pl.when((m >= 0) & (m < mine))(functools.partial(crossed, m, t))
        for b in range(RELAY):
            pl.when(first_section & (n == TAKE[b]))(functools.partial(take, b))
        for run in plan:
            run(n)

    @pl.loop(jnp.where(first_section, 8, 0), CHUNKS)
    def _(m):
        chunk_ready(m)

    @pl.when(first_section)
    def _():
        @pl.loop(0, pairs)
        def _(p):
            narrow(p)
            state_copy(p).start()
            out_copy(p).start()

    @pl.when(~first_section)
    def _():
        pltpu.make_async_copy(token_grads, gbuf, local_sem.at[1]).wait()

    for is_first, count in ((first_section, CHUNKS - RELAY), (~first_section, CHUNKS)):

        @pl.when(is_first)
        def _(count=count):
            sent = big.at[pl.ds(0, count * (depth - 1) * rs), pl.ds(0, HALF)]
            rcopy(sent, sent, g_send.at[0], g_zr.at[0, 0], across).wait_send()
            rcopy(sent, sent, g_send.at[1], g_xr.at[0, 0], across).wait_send()

    def relay_sent(k, rows, cols):
        sent = big.at[pl.ds(0, rows), pl.ds(0, cols)]
        rcopy(sent, sent, b_send.at[k], b_own.at[0], other).wait_send()

    @pl.when(first_section)
    def _():
        relay_sent(0, RELAY * rs, HALF)

    @pl.when(~first_section)
    def _():
        relay_sent(1, RELAY * (depth - 1) * rs, HALF)
        relay_sent(2, RELAY * (depth - 1) * rs, HALF)
        relay_sent(3, RELAY * (depth - 1) * rs, D)

    sent = big.at[pl.ds(0, CHUNKS * depth * rs), :]
    rcopy(sent, sent, g_send.at[2], g_sr.at[0], sibling).wait_send()

    def add_small(row, x):
        small[pl.ds(row, 1), :] += row_sum(x)

    def outer_norm(p):
        r = pair_rows(p)
        length = jnp.where(first_section, seq, lens[p])
        score = jnp.where(first_section, 0.0, scores[p])
        place = lax.broadcasted_iota(jnp.int32, (seq, 1), 0)
        grad = jnp.where(place < length, gbuf[r, :].astype(F32), 0.0)
        grad = grad + jnp.where(place == 0, score * head_w[...].reshape(1, D), 0.0)
        n = n2[r, :].astype(F32)
        x = norm_back(grad, n, r2[r, :], gains[1:2, :])
        xl = x.astype(BF)
        high[r, :] = x
        dd[r, :] = xl
        add_small(BD, xl.astype(F32))
        add_small(BETA2, grad)
        add_small(GAIN2, grad * n)

    def act_back(p):
        r = pair_rows(p)
        for k in range(4):
            c4 = pl.ds(k * D, D)
            x = (dot_t(dd[r, :], big[pl.ds(DOWN + k * D, D), :]) * gp[r, c4].astype(F32)).astype(BF)
            gp[r, c4] = x
            add_small(BU + k, x.astype(F32))

    def inner_norm(p):
        r = pair_rows(p)
        grad = high[r, :]
        for k in range(4):
            grad = grad + dot_t(gp[r, pl.ds(k * D, D)], block(4 + k))
        n = n1[r, :].astype(F32)
        x = norm_back(grad, n, r1[r, :], gains[0:1, :])
        xl = x.astype(BF)
        high[r, :] = x
        da[r, :] = xl
        add_small(BO, xl.astype(F32))
        add_small(BETA1, grad)
        add_small(GAIN1, grad * n)
        dm[r, :] = dot_t(xl, block(3)).astype(BF)

    def attend_back(p):
        r = pair_rows(p)

        def dprobs_of(j):
            return dot_t(both_heads(dm[r, pl.ds(j * 128, 128)]), qkv[r, pl.ds((j + 12) * 128, 128)])

        for j, dp in ahead(dprobs_of):
            q2 = qkv[r, pl.ds(j * 128, 128)]
            k2 = qkv[r, pl.ds((j + 6) * 128, 128)]
            pr = jnp.concatenate([probs[p * HEADS + 2 * j], probs[p * HEADS + 2 * j + 1]], 0)
            pf = pr.astype(F32)
            t = pf * dp
            ds = (t - pf * jnp.sum(t, -1, keepdims=True)).astype(BF)
            dq = dot(ds, k2)
            dq = (jnp.where(low, dq[:seq], dq[seq:]) * SCALE).astype(BF)
            qt, dt = q2.T, dm[r, pl.ds(j * 128, 128)].T
            dk = jnp.concatenate([dot(qt[:HEAD], ds[:seq]), dot(qt[HEAD:], ds[seq:])], 0)
            dv = jnp.concatenate([dot(dt[:HEAD], pr[:seq]), dot(dt[HEAD:], pr[seq:])], 0)
            dk = (dk * SCALE).astype(BF).T
            dv = dv.astype(BF).T
            dqkv[r, pl.ds(j * 128, 128)] = dq
            dqkv[r, pl.ds((j + 6) * 128, 128)] = dk
            dqkv[r, pl.ds((j + 12) * 128, 128)] = dv
            small[pl.ds(BQ, 1), pl.ds(j * 128, 128)] += row_sum(dq.astype(F32))
            small[pl.ds(BV, 1), pl.ds(j * 128, 128)] += row_sum(dv.astype(F32))

    def hidden_back(p):
        r = pair_rows(p)
        grad = high[r, :]
        for k in range(3):
            grad = grad + dot_t(dqkv[r, pl.ds(k * D, D)], block(k))
        high[r, :] = grad
        outb[r, :] = grad.astype(BF)

    def grad_copy(p):
        r = pair_rows(p)
        return rcopy(outb.at[r, :], gbuf.at[r, :], y_send.at[2 + p], y_recv.at[2 + p], other)

    def weight_grad(left, lcol, right, rcol, row):
        a = left[:, pl.ds(pl.multiple_of(lcol, 256), D)]
        b = right[:, pl.ds(pl.multiple_of(rcol, 256), D)]
        big[pl.ds(pl.multiple_of(row, 256), D), :] = dot_c(a, b).astype(BF)

    def sib_copy(m, zz):
        return rcopy(
            big.at[pl.ds(shard_row(m, 2 * zz + 1 - c, DOWN_GRAD), rs), :],
            s1.at[m, zz], r_send.at[0], r_sib.at[m], sibling,
        )

    def sib_send(m):
        @pl.loop(0, depth)
        def _(zz):
            sib_copy(m, zz).start()

    def half_down(p):
        r = pair_rows(p)

        @pl.loop(0, 4)
        def _(k):
            x = dot_c(act[r, span(k, D)], dd[r, :])
            place = pl.ds(pl.multiple_of(DOWN_GRAD + k * D, 256), D)
            if p > 0:
                x = x + big[place, :].astype(F32)
            big[place, :] = x.astype(BF)

    def make_down():
        half_down(last)

        @pl.loop(8, 12)
        def _(m):
            sib_send(m)

    def make_up(k):
        weight_grad(first_low, 0, gp, k * D, (4 + k) * D)
        sib_send(4 + k)

    def make_attn():
        weight_grad(mixed, 0, da, 0, 3 * D)
        sib_send(3)

    def make_qkv(k):
        weight_grad(hbuf, 0, dqkv, k * D, k * D)
        sib_send(k)

    def pair_sums(m):
        rcopy(s1.at[m], s1.at[m], r_send.at[0], r_sib.at[m], sibling).wait_recv()

        @pl.loop(0, depth)
        def _(zz):
            mine = big[pl.ds(shard_row(m, 2 * zz + c, DOWN_GRAD), rs), :]
            s1[m, zz] = (mine.astype(F32) + s1[m, zz].astype(F32)).astype(BF)

    sides = [masks([2 << k for k in range(t, stages - 1)]) for t in range(stages)]
    slots = [sum(len(side) for side in sides[:t]) for t in range(stages)]

    def line_send(part, landing, m, t, send):
        for k, mask in enumerate(sides[t]):
            rcopy(
                part.at[flip(z, (1 << t) ^ mask)], landing.at[slots[t] + k], send, r_z.at[m, t],
                dev(z_=flip(z, 1 << t)),
            ).start()

    def line_add(part, landing, m, t, send):
        here = landing.at[pl.ds(slots[t], len(sides[t]))]
        rcopy(here, here, send, r_z.at[m, t], dev(z_=flip(z, 1 << t))).wait_recv()
        for k, mask in enumerate(sides[t]):
            zz = flip(z, mask)
            part[zz] = (part[zz].astype(F32) + landing[slots[t] + k].astype(F32)).astype(BF)

    def put_out(m):
        def put(to, row, col):
            for h in range(2):
                rows = pl.ds(pl.multiple_of(row, 16), rs)
                cols = pl.ds(pl.multiple_of(col + h * HALF, 128), HALF)
                pltpu.make_async_copy(fin.at[m, h], to.at[rows, cols], io_sem.at[3]).start()

        pl.when(m >= 8)(lambda: put(out_d, (m - 8) * rs, 0))
        pl.when((m >= 4) & (m < 8))(lambda: put(out_u, 0, (m - 4) * D))
        pl.when(m == 3)(lambda: put(out_o, 0, 0))
        pl.when(m < 3)(lambda: put(out_q, 0, m * D))

    def x_copy(q, m):
        return rcopy(
            s1.at[m, :, :, span(1 - par, HALF)], xr.at[q], r_send.at[1], r_x.at[m], across
        )

    def fin_copy(m):
        return rcopy(fin.at[m, par], fin.at[m, par], r_send.at[4], r_fin.at[m], across)

    def x_start(q, m):
        pair_sums(m)
        x_copy(q, m).start()

    def x_halves(q, m):
        x_copy(q, m).wait_recv()

        @pl.loop(0, depth)
        def _(zz):
            mine = s1[m, zz, :, span(par, HALF)]
            xr[q, zz] = (mine.astype(F32) + xr[q, zz].astype(F32)).astype(BF)

        line_send(xr.at[q], zr.at[q], m, 0, r_send.at[2])

    def lines(part, landing, m, ts, send):
        for t in ts:
            line_add(part, landing, m, t, send)
            if t + 1 < stages:
                line_send(part, landing, m, t + 1, send)

    def x_line(ts, q, m):
        lines(xr.at[q], zr.at[q], m, ts, r_send.at[2])
        if stages - 1 not in ts:
            return
        total = xr[q, z]
        if groups > 2:
            teams = groups // 2
            team = g // 2
            peers[q, team] = total
            for k in range(1, teams):
                to = dev(g_=((team + k) % teams) * 2 + par)
                rcopy(peers.at[q, team], peers.at[q, team], r_send.at[5], r_peer.at[m, team], to).start()
            for k in range(1, teams):
                tt = (team + k) % teams
                rcopy(peers.at[q, tt], peers.at[q, tt], r_send.at[5], r_peer.at[m, tt], across).wait_recv()
            total = peers[q, 0].astype(F32)
            for k in range(1, teams):
                total = total + peers[q, k].astype(F32)
            total = total.astype(BF)
        fin[m, par] = total
        fin_copy(m).start()

    def x_finish(q, m):
        rcopy(fin.at[m, 1 - par], fin.at[m, 1 - par], r_send.at[4], r_fin.at[m], across).wait_recv()
        put_out(m)

    def z_start(q, m):
        pair_sums(m)
        line_send(s1.at[m], zw.at[q], m, 0, r_send.at[3])

    def z_line(ts, q, m):
        lines(s1.at[m], zw.at[q], m, ts, r_send.at[3])
        if stages - 1 not in ts:
            return
        xw[q, g] = s1[m, z]
        for k in range(1, groups):
            rcopy(xw.at[q, g], xw.at[q, g], r_send.at[6], r_grp.at[q, g], dev(g_=(g + k) % groups)).start()

    def z_finish(q, m):
        for k in range(1, groups):
            gg = (g + k) % groups
            rcopy(xw.at[q, gg], xw.at[q, gg], r_send.at[6], r_grp.at[q, gg], across).wait_recv()
        total = xw[q, 0].astype(F32)
        for k in range(1, groups):
            total = total + xw[q, k].astype(F32)
        total = total.astype(BF)
        fin[m, 0] = total[:, :HALF]
        fin[m, 1] = total[:, HALF:]
        put_out(m)

    first_line, last_lines = range(0, 1), range(1, stages)
    if stages == 1:
        first_line, last_lines = range(0, 0), range(0, 1)
    x_stages = [
        x_start, x_halves, functools.partial(x_line, first_line), functools.partial(x_line, last_lines), x_finish
    ]
    z_stages = [z_start, functools.partial(z_line, first_line), functools.partial(z_line, last_lines), z_finish]

    last = pairs - 1

    def hidden_step(p):
        out_copy(p).wait()

        @pl.when(first_section)
        def _():
            state_copy(p).wait_send()

        hidden_back(p)

    @pl.loop(0, jnp.where(first_section, last, pairs))
    def _(p):
        @pl.when(~first_section)
        def _():
            state_copy(p).wait_recv()
            for k in range(3):
                project(p, k)
            attend(p)
            join(p)
            for k in range(4):
                widen(p, k)
            narrow(p)
            out_copy(p).start()

        @pl.when(first_section)
        def _():
            grad_copy(p).wait_recv()

        outer_norm(p)
        act_back(p)
        inner_norm(p)
        attend_back(p)
        hidden_step(p)

        @pl.when(~first_section)
        def _():
            grad_copy(p).start()

    def sm_copy(src, dst, recv, to):
        return rcopy(src, dst, sm_send.at[0], recv, to)

    def small_sib():
        sm_copy(small, sm_sib, sm_recv.at[0], sibling).start()

    def small_grp():
        sm_copy(small, sm_sib, sm_recv.at[0], sibling).wait_recv()
        sm_grp[g] = small[...] + sm_sib[...]
        for k in range(1, groups):
            sm_copy(sm_grp.at[g], sm_grp.at[g], sm_recv.at[1 + g], dev(g_=(g + k) % groups)).start()

    def small_dp():
        for k in range(1, groups):
            gg = (g + k) % groups
            sm_copy(sm_grp.at[gg], sm_grp.at[gg], sm_recv.at[1 + gg], across).wait_recv()
        total = sm_grp[0]
        for k in range(1, groups):
            total = total + sm_grp[k]
        sm_dp[z] = total
        for k in range(1, depth):
            sm_copy(sm_dp.at[z], sm_dp.at[z], sm_recv.at[1 + groups + z], dev(z_=(z + k) % depth)).start()

    def head_copy():
        return rcopy(out_small, sm_sec, sm_send.at[1], sm_recv.at[1 + groups + depth], other)

    def small_sec():
        for k in range(1, depth):
            zz = (z + k) % depth
            sm_copy(sm_dp.at[zz], sm_dp.at[zz], sm_recv.at[1 + groups + zz], across).wait_recv()
        total = sm_dp[0]
        for k in range(1, depth):
            total = total + sm_dp[k]
        out_small[...] = total

        @pl.when(~first_section)
        def _():
            head_copy().start()

    def small_head():
        @pl.when(first_section)
        def _():
            head_copy().wait_recv()
            out_small[pl.ds(HEAD_ROW, 1), :] = sm_sec[pl.ds(HEAD_ROW, 1), :]

        @pl.when(~first_section)
        def _():
            head_copy().wait_send()

    def make_inner():
        @pl.loop(0, 4)
        def _(k):
            make_up(k)

    def make_outer():
        make_attn()

        @pl.loop(0, 3)
        def _(k):
            make_qkv(k)

        pltpu.make_async_copy(high, out_gin, io_sem.at[2]).start()

    beside = (
        ("down", make_down, False),
        ("act", act_back, True),
        ("inner", inner_norm, True),
        ("up", make_inner, False),
        ("attend", attend_back, True),
        ("hidden", hidden_step, True),
        ("qkv", make_outer, False),
    )
    smalls = (small_sib, small_grp, small_dp, small_sec, small_head)

    for p in range(last):
        half_down(p)

    @pl.when(first_section)
    def _():
        grad_copy(last).wait_recv()
        outer_norm(last)

    @pl.loop(0, STEPS)
    def _(i):
        for name, part, inside in beside:
            if inside:
                pl.when(first_section & (i == BESIDE[name]))(functools.partial(part, last))
            else:
                pl.when(i == BESIDE[name])(part)
        for step, part in zip(SMALL_STEPS, smalls):
            pl.when(i == step)(part)
        for name, at in SLOTS:
            chunks, parts = (X_FIRST, x_stages) if name[0] == "x" else (Z_FIRST, z_stages)
            q = jnp.int32(-1)
            for k, step in enumerate(at):
                q = jnp.where(i == step, k, q)

            @pl.when(q >= 0)
            def _(q=q, chunks=chunks, part=parts[int(name[1])]):
                part(q, pick(q, chunks))

    count = 1 + (groups - 1) + (depth - 1)
    sent = high.at[pl.ds(0, count * SMALL), :]
    rcopy(sent, sent, sm_send.at[0], sm_recv.at[0], other).wait_send()

    @pl.when(~first_section)
    def _():
        for p in range(pairs):
            grad_copy(p).wait_send()

    pltpu.make_async_copy(high, out_gin, io_sem.at[2]).wait()
    pltpu.make_async_copy(fin, fin, io_sem.at[3]).wait()
    rcopy(s1, s1, r_send.at[0], r_sib.at[0], sibling).wait_send()
    rcopy(xr, xr, r_send.at[1], r_x.at[0], across).wait_send()
    if stages:
        rcopy(zr, zr, r_send.at[2], r_z.at[0, 0], across).wait_send()
        rcopy(zw, zw, r_send.at[3], r_z.at[0, 0], across).wait_send()
    part = fin.at[pl.ds(0, len(X_FIRST)), 0]
    rcopy(part, part, r_send.at[4], r_fin.at[0], across).wait_send()
    if groups > 2:
        part = peers.at[:, pl.ds(0, groups // 2 - 1)]
        rcopy(part, part, r_send.at[5], r_peer.at[0, 0], across).wait_send()
    part = xw.at[:, pl.ds(0, groups - 1)]
    rcopy(part, part, r_send.at[6], r_grp.at[0, 0], across).wait_send()


def on_device(groups, depth, embedded, lengths, token_grads, score_grads, w_qkv, w_attn_out, w_up, w_down, biases, gains, head_weight):
    micro, _, seq, _ = embedded.shape
    tokens = micro * seq
    rs = w_qkv.shape[1]
    vmem = pl.BlockSpec(memory_space=pltpu.VMEM)
    smem = pl.BlockSpec(memory_space=pltpu.SMEM)
    hbm = pl.BlockSpec(memory_space=pl.ANY)
    teams = max(groups // 2, 1)
    stages = depth.bit_length() - 1
    out_shape = (
        jax.ShapeDtypeStruct((tokens, D), BF),
        jax.ShapeDtypeStruct((tokens, D), F32),
        jax.ShapeDtypeStruct((rs, 3 * D), BF),
        jax.ShapeDtypeStruct((rs, D), BF),
        jax.ShapeDtypeStruct((rs, FF), BF),
        jax.ShapeDtypeStruct((4 * rs, D), BF),
        jax.ShapeDtypeStruct((SMALL, D), F32),
    )
    nx, nz = len(X_FIRST), len(Z_FIRST)
    scratch = [
        pltpu.VMEM((CHUNKS * D + FF, D), BF),
        pltpu.VMEM((CHUNKS, depth, rs, D), BF),
        pltpu.VMEM((nx, depth, rs, HALF), BF),
        pltpu.VMEM((nx, max(depth - 1, 1), rs, HALF), BF),
        pltpu.VMEM((nz, max(depth - 1, 1), rs, D), BF),
        pltpu.VMEM((nz, groups, rs, D), BF),
        pltpu.VMEM((CHUNKS, 2, rs, HALF), BF),
        pltpu.VMEM((nx, teams, rs, HALF) if groups > 2 else (1, 1, 16, 128), BF),
        pltpu.VMEM((tokens, D), BF),
        pltpu.VMEM((tokens, 3 * D), BF),
        pltpu.VMEM((micro * HEADS, seq, seq), BF),
        pltpu.VMEM((tokens, D), BF),
        pltpu.VMEM((tokens, D), BF),
        pltpu.VMEM((tokens, 1), F32),
        pltpu.VMEM((tokens, D), BF),
        pltpu.VMEM((tokens, FF), BF),
        pltpu.VMEM((tokens, FF), BF),
        pltpu.VMEM((tokens, D), BF),
        pltpu.VMEM((tokens, 1), F32),
        pltpu.VMEM((tokens, D), BF),
        pltpu.VMEM((tokens, D), BF),
        pltpu.VMEM((tokens, D), F32),
        pltpu.VMEM((tokens, D), BF),
        pltpu.VMEM((tokens, D), BF),
        pltpu.VMEM((tokens, D), BF),
        pltpu.VMEM((tokens, 3 * D), BF),
        pltpu.VMEM((SMALL, D), F32),
        pltpu.VMEM((SMALL, D), F32),
        pltpu.VMEM((groups, SMALL, D), F32),
        pltpu.VMEM((depth, SMALL, D), F32),
        pltpu.VMEM((SMALL, D), F32),
        pltpu.SemaphoreType.DMA((2,)),
        pltpu.SemaphoreType.DMA((4,)),
        pltpu.SemaphoreType.DMA((CHUNKS, depth)),
        pltpu.SemaphoreType.DMA((CHUNKS, depth)),
        pltpu.SemaphoreType.DMA((CHUNKS,)),
        pltpu.SemaphoreType.DMA((3,)),
        pltpu.SemaphoreType.DMA((RELAY,)),
        pltpu.SemaphoreType.DMA((RELAY, depth)),
        pltpu.SemaphoreType.DMA((RELAY, depth)),
        pltpu.SemaphoreType.DMA((RELAY,)),
        pltpu.SemaphoreType.DMA((4,)),
        pltpu.SemaphoreType.DMA((4,)),
        pltpu.SemaphoreType.DMA((4,)),
        pltpu.SemaphoreType.DMA((7,)),
        pltpu.SemaphoreType.DMA((CHUNKS,)),
        pltpu.SemaphoreType.DMA((CHUNKS,)),
        pltpu.SemaphoreType.DMA((CHUNKS, max(stages, 1))),
        pltpu.SemaphoreType.DMA((nz, groups)),
        pltpu.SemaphoreType.DMA((CHUNKS,)),
        pltpu.SemaphoreType.DMA((CHUNKS, teams)),
        pltpu.SemaphoreType.DMA((2,)),
        pltpu.SemaphoreType.DMA((2 + groups + depth,)),
    ]
    state, grad_in, *grads, small = pl.pallas_call(
        functools.partial(kernel, (groups, depth, rs, seq)),
        out_shape=out_shape,
        in_specs=[hbm] * 6 + [smem] * 2 + [vmem] * 3,
        out_specs=(hbm,) * 6 + (vmem,),
        scratch_shapes=scratch,
        compiler_params=pltpu.CompilerParams(
            collective_id=0, has_side_effects=True, vmem_limit_bytes=65300 * 1024
        ),
    )(
        embedded.reshape(tokens, D),
        token_grads.reshape(tokens, D),
        w_qkv[0],
        w_attn_out[0],
        w_up[0],
        w_down[0],
        lengths.reshape(micro),
        score_grads.reshape(micro),
        biases,
        gains[0],
        head_weight,
    )
    results = pl.pallas_call(
        hand_out,
        out_shape=[jax.ShapeDtypeStruct(x.shape, x.dtype) for x in (state, grad_in)]
        + [jax.ShapeDtypeStruct(x.shape, F32) for x in grads]
        + [jax.ShapeDtypeStruct(x, F32) for x in ((1, 10 * D), (2, D), (D,))],
        in_specs=[vmem] * 7,
        out_specs=[vmem] * 9,
    )(state, grad_in, *grads, small)
    state, grad_in, g_qkv, g_attn, g_up, g_down, g_bias, g_gain, g_head = results
    return (
        state.reshape(1, micro, 1, seq, D),
        grad_in.reshape(1, micro, 1, seq, D),
        g_qkv[None],
        g_attn[None],
        g_up[None],
        g_down[None],
        g_bias,
        g_gain[None],
        g_head,
    )


def hand_out(state, grad_in, gq, go, gu, gd, small, o_state, o_gin, o_q, o_o, o_u, o_d, o_bias, o_gain, o_head):
    for src, dst in ((state, o_state), (grad_in, o_gin), (gq, o_q), (go, o_o), (gu, o_u), (gd, o_d)):
        dst[...] = src[...].astype(dst.dtype)
    for k in range(10):
        o_bias[:, pl.ds(k * D, D)] = small[pl.ds(k, 1), :]
    o_gain[...] = small[pl.ds(GAIN1, 2), :]
    o_head[...] = small[HEAD_ROW, :]


def solution(mesh):
    return jax.shard_map(
        functools.partial(on_device, mesh.shape["grp"], mesh.shape["dp"] // 2),
        mesh=mesh,
        in_specs=(
            P(None, ("grp", "dp"), None, None),
            P(None, ("grp", "dp")),
            P(None, ("grp", "dp"), None, None),
            P(None, ("grp", "dp")),
            P("section", "dp", None),
            P("section", "dp", None),
            P("section", "dp", None),
            P("section", "dp", None),
            P("section", None),
            P("section", None, None),
            P(),
        ),
        out_specs=(
            P("section", None, ("grp", "dp"), None, None),
            P("section", None, ("grp", "dp"), None, None),
            P("section", "dp", None),
            P("section", "dp", None),
            P("section", "dp", None),
            P("section", "dp", None),
            P("section", None),
            P("section", None, None),
            P(),
        ),
        check_vma=False,
    )
```

```python
import functools
import math

import jax
import jax.numpy as jnp
from jax import lax
from jax.experimental import pallas as pl
from jax.experimental.pallas import tpu as pltpu
from jax.sharding import PartitionSpec as P

D = 768
FF = 3072
HEADS = 12
HEAD = 64
EPSILON = 1e-06
CHUNKS = 12
HALF = D // 2
DOWN = 8 * D
DOWN_GRAD = 12 * D
SCALE = 1.0 / math.sqrt(HEAD)
F32 = jnp.float32
BF = jnp.bfloat16
MESH = pl.DeviceIdType.MESH
BQ, BV, BO, BU, BD, BETA1, BETA2, GAIN1, GAIN2, HEAD_ROW = 0, 1, 2, 3, 7, 8, 9, 10, 11, 12
SMALL = 16
RELAY = 1
TAKE = (8,)
X_FIRST = (8, 4, 5, 6, 7, 3, 0, 1, 2)
Z_FIRST = (9, 10, 11)
SLOTS = (
    ("x0", (0, 2, 1, 4, 3, 6, 5, 7, 9)),
    ("z0", (0, 3, 2)),
    ("z3", (14, 15, 17)),
    ("x4", (8, 12, 9, 13, 11, 14, 15, 16, 17)),
    ("x3", (6, 9, 7, 11, 8, 12, 13, 14, 15)),
    ("z2", (4, 11, 13)),
    ("x2", (3, 6, 4, 8, 7, 9, 11, 12, 13)),
    ("z1", (2, 5, 7)),
    ("x1", (1, 3, 2, 5, 4, 7, 8, 10, 11)),
)
BESIDE = {"down": 0, "act": 1, "inner": 1, "up": 1, "attend": 3, "hidden": 4, "qkv": 5}
SMALL_STEPS = (4, 5, 6, 8, 10)
LENT = 4
LENT_STEPS = (7, 9, 11, 13)
LENT_BACK = 17
STEPS = 1 + max(LENT_BACK, max(max(steps) for _, steps in SLOTS))


def dot(a, b):
    return lax.dot_general(a, b, (((1,), (0,)), ((), ())), preferred_element_type=F32)


def dot_t(a, b):
    return lax.dot_general(a, b, (((1,), (1,)), ((), ())), preferred_element_type=F32)


def dot_c(a, b):
    return lax.dot_general(a, b, (((0,), (0,)), ((), ())), preferred_element_type=F32)


def span(i, width):
    return pl.ds(pl.multiple_of(i * width, width), width)


def flip(index, mask):
    bit = 1
    while bit <= mask:
        if mask & bit:
            index = index + bit - 2 * bit * ((index // bit) % 2)
        bit *= 2
    return index


def masks(bits):
    found = [0]
    for bit in bits:
        found = found + [mask ^ bit for mask in found]
    return found


def pick(i, values):
    found = values[-1]
    for k in range(len(values) - 2, -1, -1):
        found = jnp.where(i == k, values[k], found)
    return found


def row_sum(x):
    return jnp.sum(x, 0, keepdims=True)


def gelu_parts(x):
    t = 1.0 / (1.0 + (0.3275911 * math.sqrt(0.5)) * jnp.abs(x))
    e = jnp.exp2((-0.5 * math.log2(math.e)) * (x * x))
    tail = t * (0.127414796 + t * (-0.142248368 + t * (0.7107068705 + t * (-0.7265760135 + t * 0.5307027145)))) * e
    phi = jnp.where(x >= 0, 1.0 - tail, tail)
    return x * phi, phi + x * (e * (1.0 / math.sqrt(2.0 * math.pi)))


def normed(x):
    centred = x - jnp.mean(x, -1, keepdims=True)
    scale = lax.rsqrt(jnp.mean(centred * centred, -1, keepdims=True) + EPSILON)
    return centred * scale, scale


def norm_back(grad, n, scale, gain):
    gg = gain * grad
    return (gg - jnp.mean(gg, -1, keepdims=True) - n * jnp.mean(gg * n, -1, keepdims=True)) * scale


def kernel(sizes, *refs):
    groups, depth, rs, seq = sizes
    (emb, token_grads, wq_in, wo_in, wu_in, wd_in, lens, scores, bias, gains, head_w,
     out_sec, out_gin, out_q, out_o, out_u, out_d, out_small,
     big, s1, xr, zr, zw, xw, fin, peers, rz, rg,
     hbuf, qkv, probs, mixed, n1, r1, first_low, act, gp, n2, r2, outb, gbuf, high, dd, dqkv,
     small, sm_sib, sm_grp, sm_dp, sm_sec,
     local_sem, io_sem, g_zr, g_xr, g_sr, g_send, b_own, b_zr, b_xr, b_back, b_send, k_in, k_z, k_g, k_out, k_send, y_send, y_recv,
     r_send, r_sib, r_x, r_z, r_grp, r_fin, r_peer, sm_send, sm_recv) = refs
    stages = depth.bit_length() - 1
    da, dm = n1, n2
    pairs = 2
    sec = lax.axis_index("section")
    g = lax.axis_index("grp")
    d = lax.axis_index("dp")
    z, c = d // 2, d % 2
    par = g % 2
    first_section = sec == 0

    def dev(sec_=None, g_=None, z_=None, c_=None):
        return (
            sec if sec_ is None else sec_,
            g if g_ is None else g_,
            (z if z_ is None else z_) * 2 + (c if c_ is None else c_),
        )

    sibling = dev(c_=1 - c)
    across = dev(g_=g + 1 - 2 * par)
    other = dev(sec_=1 - sec)

    def rcopy(src, dst, send, recv, to):
        return pltpu.make_async_remote_copy(
            src_ref=src, dst_ref=dst, send_sem=send, recv_sem=recv, device_id=to, device_id_type=MESH
        )

    def shard_row(m, owner, down=DOWN):
        row = jnp.where(m < 8, m * D + owner * rs, down + owner * (4 * rs) + (m - 8) * rs)
        return pl.multiple_of(row, 16)

    barrier = pltpu.get_barrier_semaphore()
    greeted = 0
    for to in [sibling, other]:
        pl.semaphore_signal(barrier, inc=1, device_id=to, device_id_type=MESH)
        greeted += 1
    for k in range(1, groups):
        pl.semaphore_signal(barrier, inc=1, device_id=dev(g_=(g + k) % groups), device_id_type=MESH)
        greeted += 1
    for k in range(1, depth):
        pl.semaphore_signal(barrier, inc=1, device_id=dev(z_=(z + k) % depth), device_id_type=MESH)
        greeted += 1

    own = []
    for k in range(3):
        own.append((wq_in.at[:, pl.ds(k * D, D)], k))
    own.append((wo_in, 3))
    for k in range(4):
        own.append((wu_in.at[:, pl.ds(k * D, D)], 4 + k))
    for src, k in own:
        pltpu.make_async_copy(src, big.at[pl.ds(pl.multiple_of(k * D + d * rs, 16), rs), :], local_sem.at[0]).start()
    pltpu.make_async_copy(
        wd_in, big.at[pl.ds(pl.multiple_of(DOWN + d * 4 * rs, 16), 4 * rs), :], local_sem.at[0]
    ).start()

    @pl.when(first_section)
    def _():
        pltpu.make_async_copy(emb, hbuf, local_sem.at[1]).start()

    @pl.when(~first_section)
    def _():
        pltpu.make_async_copy(token_grads, gbuf, local_sem.at[1]).start()

    small[...] = jnp.zeros_like(small)
    pl.semaphore_wait(barrier, greeted)
    pltpu.make_async_copy(
        big.at[pl.ds(0, CHUNKS * rs), :], big.at[pl.ds(0, CHUNKS * rs), :], local_sem.at[0]
    ).wait()

    def region(m, zz, half=None, cc=c):
        cols = slice(None) if half is None else span(half, HALF)
        return big.at[pl.ds(shard_row(m, 2 * zz + cc), rs), cols]

    far = [depth >> (t + 1) for t in range(stages)]
    held = [masks(far[:t]) for t in range(stages + 1)]

    def along(m, zz, t):
        part = region(m, zz, par)
        return rcopy(part, part, g_send.at[0], g_zr.at[m, zz], dev(z_=flip(z, far[t])))

    def over(m, zz, half):
        part = region(m, zz, half)
        return rcopy(part, part, g_send.at[1], g_xr.at[m, zz], across)

    def beside(m, zz, half):
        part = region(m, zz, half)
        return rcopy(part, part, g_send.at[2], g_sr.at[m], sibling)

    def relayed(b, zz, half):
        return dd.at[pl.ds(pl.multiple_of((b * depth + zz) * rs, 16), rs), span(half, HALF)]

    def lend(b):
        return rcopy(
            region(CHUNKS - RELAY + b, z, par), relayed(b, z, par), b_send.at[0], b_own.at[b], other
        )

    def relay_along(b, zz, t):
        part = relayed(b, zz, par)
        return rcopy(part, part, b_send.at[1], b_zr.at[b, zz], dev(z_=flip(z, far[t])))

    def relay_over(b, zz, half):
        part = relayed(b, zz, half)
        return rcopy(part, part, b_send.at[2], b_xr.at[b, zz], across)

    def give_back(b, zz, half):
        return rcopy(
            relayed(b, zz, half), region(CHUNKS - RELAY + b, zz, half), b_send.at[3], b_back.at[b], other
        )

    def relay_own(b):
        lend(b).wait_recv()
        relay_along(b, z, 0).start()

    def relay_arrived(t, b):
        for mask in held[t]:
            zz = flip(z, far[t] ^ mask)
            relay_along(b, zz, t).wait_recv()
            relay_over(b, zz, par).start()
            give_back(b, zz, par).start()
        if t + 1 < stages:
            for mask in held[t + 1]:
                relay_along(b, flip(z, mask), t + 1).start()

    def relay_crossed(t, b):
        for mask in held[t]:
            zz = flip(z, far[t] ^ mask)
            relay_over(b, zz, 1 - par).wait_recv()
            give_back(b, zz, 1 - par).start()

    def take(b):
        got = big.at[pl.ds(0, (depth - 1) * rs), :]
        rcopy(got, got, b_send.at[3], b_back.at[b], other).wait_recv()
        for k in range(1, depth):
            beside(CHUNKS - RELAY + b, (z + k) % depth, None).start()

    def bias_row(start, width=D):
        return bias[:, pl.ds(start, width)]

    low = lax.broadcasted_iota(jnp.int32, (1, 128), 1) < HEAD
    key = lax.broadcasted_iota(jnp.int32, (1, seq), 1)

    def pair_rows(p):
        return span(p, seq)

    def block(k):
        return big[pl.ds(k * D, D), :]

    def project(p, k):
        r = pair_rows(p)
        x = dot(hbuf[r, :], block(k))
        if k != 1:
            x = x + bias_row(0 if k == 0 else D)
        qkv[r, pl.ds(k * D, D)] = x.astype(BF)

    def both_heads(x):
        none = jnp.zeros_like(x)
        return jnp.concatenate([jnp.where(low, x, none), jnp.where(low, none, x)], 0)

    def ahead(make):
        coming = make(0)
        for j in range(HEADS // 2):
            now, coming = coming, make(j + 1) if j + 1 < HEADS // 2 else None
            yield j, now

    def attend(p):
        r = pair_rows(p)
        ok = key < lens[p]

        def scores_of(j):
            q2 = qkv[r, pl.ds(j * 128, 128)] * jnp.asarray(SCALE, BF)
            return dot_t(both_heads(q2), qkv[r, pl.ds((j + 6) * 128, 128)])

        for j, sc in ahead(scores_of):
            sc = jnp.where(ok, sc, -1e30)
            e = jnp.exp(sc - jnp.max(sc, -1, keepdims=True))
            pr = (e * (1.0 / jnp.sum(e, -1, keepdims=True))).astype(BF)
            probs[p * HEADS + 2 * j] = pr[:seq]
            probs[p * HEADS + 2 * j + 1] = pr[seq:]
            o = dot(pr, qkv[r, pl.ds((j + 12) * 128, 128)])
            mixed[r, pl.ds(j * 128, 128)] = jnp.where(low, o[:seq], o[seq:]).astype(BF)

    def join(p):
        r = pair_rows(p)
        n, scale = normed(hbuf[r, :].astype(F32) + dot(mixed[r, :], block(3)) + bias_row(2 * D))
        n1[r, :] = n.astype(BF)
        r1[r, :] = scale
        y = n * gains[0:1, :] + bias_row(4 * D + FF)
        high[r, :] = y
        first_low[r, :] = y.astype(BF)

    def widen(p, k):
        r = pair_rows(p)
        for t in range(3):
            w = big[pl.ds((4 + k) * D, D), pl.ds(t * 256, 256)]
            col = k * D + t * 256
            a, dg = gelu_parts(dot(first_low[r, :], w) + bias_row(3 * D + col, 256))
            act[r, pl.ds(col, 256)] = a.astype(BF)
            gp[r, pl.ds(col, 256)] = dg.astype(BF)

    def narrow(p):
        r = pair_rows(p)
        n, scale = normed(high[r, :] + dot(act[r, :], big[pl.ds(DOWN, FF), :]) + bias_row(3 * D + FF))
        n2[r, :] = n.astype(BF)
        r2[r, :] = scale
        y = n * gains[1:2, :] + bias_row(5 * D + FF)
        outb[r, :] = y.astype(BF)

        @pl.when(~first_section)
        def _():
            small[pl.ds(HEAD_ROW, 1), :] += scores[p] * y[0:1]

    def state_copy(p):
        r = pair_rows(p)
        return rcopy(outb.at[r, :], hbuf.at[r, :], y_send.at[p], y_recv.at[p], other)

    def out_copy(p):
        r = pair_rows(p)
        return pltpu.make_async_copy(outb.at[r, :], out_sec.at[r, :], io_sem.at[p])

    def chunk_ready(m):
        whole = big.at[pl.ds(0, depth * rs), :]
        rcopy(whole, whole, g_send.at[2], g_sr.at[m], sibling).wait_recv()

    def own_step(n):
        if stages:
            along(n, z, 0).start()
        beside(n, z, None).start()

    def arrived(m, t):
        for mask in held[t]:
            zz = flip(z, far[t] ^ mask)
            along(m, zz, t).wait_recv()
            over(m, zz, par).start()
            beside(m, zz, par).start()
        if t + 1 < stages:
            for mask in held[t + 1]:
                along(m, flip(z, mask), t + 1).start()

    def crossed(m, t):
        for mask in held[t]:
            zz = flip(z, far[t] ^ mask)
            over(m, zz, 1 - par).wait_recv()
            beside(m, zz, 1 - par).start()

    def early(step, pieces):
        def run(n):
            @pl.when(first_section & (n == stages + 2 + step))
            def _():
                pieces()

        return run

    def both_pairs(piece):
        @pl.loop(0, pairs)
        def _(p):
            piece(p)

    def early_project(k):
        if k == 0:
            pltpu.make_async_copy(emb, hbuf, local_sem.at[1]).wait()
        chunk_ready(k)
        both_pairs(lambda p: project(p, k))

    def early_join():
        chunk_ready(3)
        both_pairs(join)

    def early_widen(k):
        chunk_ready(4 + k)
        both_pairs(lambda p: widen(p, k))

    plan = [early(k, functools.partial(early_project, k)) for k in range(3)]
    plan.append(early(2, lambda: attend(0)))
    plan.append(early(3, lambda: attend(1)))
    plan.append(early(4, early_join))
    plan += [early(4 + k, functools.partial(early_widen, k)) for k in range(4)]

    mine = jnp.where(first_section, CHUNKS - RELAY, CHUNKS)

    @pl.loop(0, mine + stages + 1)
    def _(n):
        pl.when(n < mine)(functools.partial(own_step, n))

        @pl.when(first_section & (n < RELAY))
        def _():
            lend(n).start()
            beside(CHUNKS - RELAY + n, z, None).start()

        relay_stages = [relay_own]
        for t in range(stages):
            relay_stages.append(functools.partial(relay_arrived, t))
        for lag, stage in enumerate(relay_stages):
            b = n - 1 - lag
            pl.when(~first_section & (b >= 0) & (b < RELAY))(functools.partial(stage, b))
        for t in range(stages):
            b = n - 3 - t
            pl.when(~first_section & (b >= 0) & (b < RELAY))(functools.partial(relay_crossed, t, b))
        for t in range(stages):
            m = n - t - 1
            pl.when((m >= 0) & (m < mine))(functools.partial(arrived, m, t))
        for t in range(stages):
            m = n - t - 2
            pl.when((m >= 0) & (m < mine))(functools.partial(crossed, m, t))
        for b in range(RELAY):
            pl.when(first_section & (n == TAKE[b]))(functools.partial(take, b))
        for run in plan:
            run(n)

    @pl.loop(jnp.where(first_section, 8, 0), CHUNKS)
    def _(m):
        chunk_ready(m)

    @pl.when(first_section)
    def _():
        @pl.loop(0, pairs)
        def _(p):
            narrow(p)
            state_copy(p).start()
            out_copy(p).start()

    @pl.when(~first_section)
    def _():
        pltpu.make_async_copy(token_grads, gbuf, local_sem.at[1]).wait()

    for is_first, count in ((first_section, CHUNKS - RELAY), (~first_section, CHUNKS)):

        @pl.when(is_first)
        def _(count=count):
            sent = big.at[pl.ds(0, count * (depth - 1) * rs), pl.ds(0, HALF)]
            rcopy(sent, sent, g_send.at[0], g_zr.at[0, 0], across).wait_send()
            rcopy(sent, sent, g_send.at[1], g_xr.at[0, 0], across).wait_send()

    def relay_sent(k, rows, cols):
        sent = big.at[pl.ds(0, rows), pl.ds(0, cols)]
        rcopy(sent, sent, b_send.at[k], b_own.at[0], other).wait_send()

    @pl.when(first_section)
    def _():
        relay_sent(0, RELAY * rs, HALF)

    @pl.when(~first_section)
    def _():
        relay_sent(1, RELAY * (depth - 1) * rs, HALF)
        relay_sent(2, RELAY * (depth - 1) * rs, HALF)
        relay_sent(3, RELAY * (depth - 1) * rs, D)

    sent = big.at[pl.ds(0, CHUNKS * depth * rs), :]
    rcopy(sent, sent, g_send.at[2], g_sr.at[0], sibling).wait_send()

    def add_small(row, x):
        small[pl.ds(row, 1), :] += row_sum(x)

    def outer_norm(p):
        r = pair_rows(p)
        length = jnp.where(first_section, seq, lens[p])
        score = jnp.where(first_section, 0.0, scores[p])
        place = lax.broadcasted_iota(jnp.int32, (seq, 1), 0)
        grad = jnp.where(place < length, gbuf[r, :].astype(F32), 0.0)
        grad = grad + jnp.where(place == 0, score * head_w[...].reshape(1, D), 0.0)
        n = n2[r, :].astype(F32)
        x = norm_back(grad, n, r2[r, :], gains[1:2, :])
        xl = x.astype(BF)
        high[r, :] = x
        dd[r, :] = xl
        add_small(BD, xl.astype(F32))
        add_small(BETA2, grad)
        add_small(GAIN2, grad * n)

    def act_back(p):
        r = pair_rows(p)
        for k in range(4):
            c4 = pl.ds(k * D, D)
            x = (dot_t(dd[r, :], big[pl.ds(DOWN + k * D, D), :]) * gp[r, c4].astype(F32)).astype(BF)
            gp[r, c4] = x
            add_small(BU + k, x.astype(F32))

    def inner_norm(p):
        r = pair_rows(p)
        grad = high[r, :]
        for k in range(4):
            grad = grad + dot_t(gp[r, pl.ds(k * D, D)], block(4 + k))
        n = n1[r, :].astype(F32)
        x = norm_back(grad, n, r1[r, :], gains[0:1, :])
        xl = x.astype(BF)
        high[r, :] = x
        da[r, :] = xl
        add_small(BO, xl.astype(F32))
        add_small(BETA1, grad)
        add_small(GAIN1, grad * n)
        dm[r, :] = dot_t(xl, block(3)).astype(BF)

    def attend_back(p):
        r = pair_rows(p)

        def dprobs_of(j):
            return dot_t(both_heads(dm[r, pl.ds(j * 128, 128)]), qkv[r, pl.ds((j + 12) * 128, 128)])

        for j, dp in ahead(dprobs_of):
            q2 = qkv[r, pl.ds(j * 128, 128)]
            k2 = qkv[r, pl.ds((j + 6) * 128, 128)]
            pr = jnp.concatenate([probs[p * HEADS + 2 * j], probs[p * HEADS + 2 * j + 1]], 0)
            pf = pr.astype(F32)
            t = pf * dp
            ds = (t - pf * jnp.sum(t, -1, keepdims=True)).astype(BF)
            dq = dot(ds, k2)
            dq = (jnp.where(low, dq[:seq], dq[seq:]) * SCALE).astype(BF)
            qt, dt = q2.T, dm[r, pl.ds(j * 128, 128)].T
            dk = jnp.concatenate([dot(qt[:HEAD], ds[:seq]), dot(qt[HEAD:], ds[seq:])], 0)
            dv = jnp.concatenate([dot(dt[:HEAD], pr[:seq]), dot(dt[HEAD:], pr[seq:])], 0)
            dk = (dk * SCALE).astype(BF).T
            dv = dv.astype(BF).T
            dqkv[r, pl.ds(j * 128, 128)] = dq
            dqkv[r, pl.ds((j + 6) * 128, 128)] = dk
            dqkv[r, pl.ds((j + 12) * 128, 128)] = dv
            small[pl.ds(BQ, 1), pl.ds(j * 128, 128)] += row_sum(dq.astype(F32))
            small[pl.ds(BV, 1), pl.ds(j * 128, 128)] += row_sum(dv.astype(F32))

    def hidden_back(p):
        r = pair_rows(p)
        grad = high[r, :]
        for k in range(3):
            grad = grad + dot_t(dqkv[r, pl.ds(k * D, D)], block(k))
        high[r, :] = grad
        outb[r, :] = grad.astype(BF)

    def grad_copy(p):
        r = pair_rows(p)
        return rcopy(outb.at[r, :], gbuf.at[r, :], y_send.at[2 + p], y_recv.at[2 + p], other)

    def weight_grad(left, lcol, right, rcol, row):
        a = left[:, pl.ds(pl.multiple_of(lcol, 256), D)]
        b = right[:, pl.ds(pl.multiple_of(rcol, 256), D)]
        big[pl.ds(pl.multiple_of(row, 256), D), :] = dot_c(a, b).astype(BF)

    def sib_copy(m, zz):
        return rcopy(
            big.at[pl.ds(shard_row(m, 2 * zz + 1 - c, DOWN_GRAD), rs), :],
            s1.at[m, zz], r_send.at[0], r_sib.at[m], sibling,
        )

    def sib_send(m):
        @pl.loop(0, depth)
        def _(zz):
            sib_copy(m, zz).start()

    def half_down(p):
        r = pair_rows(p)

        @pl.loop(0, 4)
        def _(k):
            x = dot_c(act[r, span(k, D)], dd[r, :])
            place = pl.ds(pl.multiple_of(DOWN_GRAD + k * D, 256), D)
            if p > 0:
                x = x + big[place, :].astype(F32)
            big[place, :] = x.astype(BF)

    def make_down():
        half_down(last)

        @pl.loop(8, 12)
        def _(m):
            sib_send(m)

    def make_up(k):
        weight_grad(first_low, 0, gp, k * D, (4 + k) * D)
        sib_send(4 + k)

    def make_attn():
        weight_grad(mixed, 0, da, 0, 3 * D)
        sib_send(3)

    def make_qkv(k):
        weight_grad(hbuf, 0, dqkv, k * D, k * D)
        sib_send(k)

    def pair_sums(m):
        rcopy(s1.at[m], s1.at[m], r_send.at[0], r_sib.at[m], sibling).wait_recv()

        @pl.loop(0, depth)
        def _(zz):
            mine = big[pl.ds(shard_row(m, 2 * zz + c, DOWN_GRAD), rs), :]
            s1[m, zz] = (mine.astype(F32) + s1[m, zz].astype(F32)).astype(BF)

    sides = [masks([2 << k for k in range(t, stages - 1)]) for t in range(stages)]
    slots = [sum(len(side) for side in sides[:t]) for t in range(stages)]

    def line_send(part, landing, m, t, send):
        for k, mask in enumerate(sides[t]):
            rcopy(
                part.at[flip(z, (1 << t) ^ mask)], landing.at[slots[t] + k], send, r_z.at[m, t],
                dev(z_=flip(z, 1 << t)),
            ).start()

    def line_add(part, landing, m, t, send):
        here = landing.at[pl.ds(slots[t], len(sides[t]))]
        rcopy(here, here, send, r_z.at[m, t], dev(z_=flip(z, 1 << t))).wait_recv()
        for k, mask in enumerate(sides[t]):
            zz = flip(z, mask)
            part[zz] = (part[zz].astype(F32) + landing[slots[t] + k].astype(F32)).astype(BF)

    def put_out(m):
        def put(to, row, col):
            for h in range(2):
                rows = pl.ds(pl.multiple_of(row, 16), rs)
                cols = pl.ds(pl.multiple_of(col + h * HALF, 128), HALF)
                pltpu.make_async_copy(fin.at[m, h], to.at[rows, cols], io_sem.at[3]).start()

        pl.when(m >= 8)(lambda: put(out_d, (m - 8) * rs, 0))
        pl.when((m >= 4) & (m < 8))(lambda: put(out_u, 0, (m - 4) * D))
        pl.when(m == 3)(lambda: put(out_o, 0, 0))
        pl.when(m < 3)(lambda: put(out_q, 0, m * D))

    def x_copy(q, m):
        return rcopy(
            s1.at[m, :, :, span(1 - par, HALF)], xr.at[q], r_send.at[1], r_x.at[m], across
        )

    def fin_copy(m):
        return rcopy(fin.at[m, par], fin.at[m, par], r_send.at[4], r_fin.at[m], across)

    lent = X_FIRST[LENT]

    def lent_shard(zz):
        return qkv.at[pl.ds(pl.multiple_of(zz * rs, 16), rs), pl.ds(0, D)]

    def lend_sums():
        for zz in range(depth):
            rcopy(s1.at[lent, zz], lent_shard(zz), k_send.at[0], k_in.at[0], other).start()

    def lent_send(t):
        for k, mask in enumerate(sides[t]):
            rcopy(
                lent_shard(flip(z, (1 << t) ^ mask)), rz.at[slots[t] + k], k_send.at[1], k_z.at[t],
                dev(z_=flip(z, 1 << t)),
            ).start()

    def lent_add(t):
        here = rz.at[pl.ds(slots[t], len(sides[t]))]
        rcopy(here, here, k_send.at[1], k_z.at[t], dev(z_=flip(z, 1 << t))).wait_recv()
        for k, mask in enumerate(sides[t]):
            part = lent_shard(flip(z, mask))
            part[...] = (part[...].astype(F32) + rz[slots[t] + k].astype(F32)).astype(BF)

    def lent_start():
        whole = qkv.at[pl.ds(0, depth * rs), pl.ds(0, D)]
        rcopy(whole, whole, k_send.at[0], k_in.at[0], other).wait_recv()
        lent_send(0)

    def lent_line(ts):
        for t in ts:
            lent_add(t)
            if t + 1 < stages:
                lent_send(t + 1)
        if stages - 1 in ts:
            rg[g] = lent_shard(z)[...]
            for k in range(1, groups):
                rcopy(rg.at[g], rg.at[g], k_send.at[2], k_g.at[g], dev(g_=(g + k) % groups)).start()

    def lent_done():
        for k in range(1, groups):
            gg = (g + k) % groups
            rcopy(rg.at[gg], rg.at[gg], k_send.at[2], k_g.at[gg], across).wait_recv()
        total = rg[0].astype(F32)
        for k in range(1, groups):
            total = total + rg[k].astype(F32)
        qkv[pl.ds(0, rs), pl.ds(D, D)] = total.astype(BF)
        for h in range(2):
            rcopy(
                qkv.at[pl.ds(0, rs), pl.ds(D + h * HALF, HALF)], fin.at[lent, h], k_send.at[3], k_out.at[0], other
            ).start()

    def lent_back():
        rcopy(fin.at[lent], fin.at[lent], k_send.at[3], k_out.at[0], other).wait_recv()
        put_out(jnp.int32(lent))

    def x_start(q, m):
        pair_sums(m)
        lends = first_section & (q == LENT)
        pl.when(lends)(lend_sums)
        pl.when(~lends)(lambda: x_copy(q, m).start())

    def x_halves(q, m):
        x_copy(q, m).wait_recv()

        @pl.loop(0, depth)
        def _(zz):
            mine = s1[m, zz, :, span(par, HALF)]
            xr[q, zz] = (mine.astype(F32) + xr[q, zz].astype(F32)).astype(BF)

        line_send(xr.at[q], zr.at[q], m, 0, r_send.at[2])

    def lines(part, landing, m, ts, send):
        for t in ts:
            line_add(part, landing, m, t, send)
            if t + 1 < stages:
                line_send(part, landing, m, t + 1, send)

    def x_line(ts, q, m):
        lines(xr.at[q], zr.at[q], m, ts, r_send.at[2])
        if stages - 1 not in ts:
            return
        total = xr[q, z]
        if groups > 2:
            teams = groups // 2
            team = g // 2
            peers[q, team] = total
            for k in range(1, teams):
                to = dev(g_=((team + k) % teams) * 2 + par)
                rcopy(peers.at[q, team], peers.at[q, team], r_send.at[5], r_peer.at[m, team], to).start()
            for k in range(1, teams):
                tt = (team + k) % teams
                rcopy(peers.at[q, tt], peers.at[q, tt], r_send.at[5], r_peer.at[m, tt], across).wait_recv()
            total = peers[q, 0].astype(F32)
            for k in range(1, teams):
                total = total + peers[q, k].astype(F32)
            total = total.astype(BF)
        fin[m, par] = total
        fin_copy(m).start()

    def x_finish(q, m):
        rcopy(fin.at[m, 1 - par], fin.at[m, 1 - par], r_send.at[4], r_fin.at[m], across).wait_recv()
        put_out(m)

    def z_start(q, m):
        pair_sums(m)
        line_send(s1.at[m], zw.at[q], m, 0, r_send.at[3])

    def z_line(ts, q, m):
        lines(s1.at[m], zw.at[q], m, ts, r_send.at[3])
        if stages - 1 not in ts:
            return
        xw[q, g] = s1[m, z]
        for k in range(1, groups):
            rcopy(xw.at[q, g], xw.at[q, g], r_send.at[6], r_grp.at[q, g], dev(g_=(g + k) % groups)).start()

    def z_finish(q, m):
        for k in range(1, groups):
            gg = (g + k) % groups
            rcopy(xw.at[q, gg], xw.at[q, gg], r_send.at[6], r_grp.at[q, gg], across).wait_recv()
        total = xw[q, 0].astype(F32)
        for k in range(1, groups):
            total = total + xw[q, k].astype(F32)
        total = total.astype(BF)
        fin[m, 0] = total[:, :HALF]
        fin[m, 1] = total[:, HALF:]
        put_out(m)

    first_line, last_lines = range(0, 1), range(1, stages)
    if stages == 1:
        first_line, last_lines = range(0, 0), range(0, 1)
    x_stages = [
        x_start, x_halves, functools.partial(x_line, first_line), functools.partial(x_line, last_lines), x_finish
    ]
    z_stages = [z_start, functools.partial(z_line, first_line), functools.partial(z_line, last_lines), z_finish]

    last = pairs - 1

    def hidden_step(p):
        out_copy(p).wait()

        @pl.when(first_section)
        def _():
            state_copy(p).wait_send()

        hidden_back(p)

    @pl.loop(0, jnp.where(first_section, last, pairs))
    def _(p):
        @pl.when(~first_section)
        def _():
            state_copy(p).wait_recv()
            for k in range(3):
                project(p, k)
            attend(p)
            join(p)
            for k in range(4):
                widen(p, k)
            narrow(p)
            out_copy(p).start()

        @pl.when(first_section)
        def _():
            grad_copy(p).wait_recv()

        outer_norm(p)
        act_back(p)
        inner_norm(p)
        attend_back(p)
        hidden_step(p)

        @pl.when(~first_section)
        def _():
            grad_copy(p).start()

    def sm_copy(src, dst, recv, to):
        return rcopy(src, dst, sm_send.at[0], recv, to)

    def small_sib():
        sm_copy(small, sm_sib, sm_recv.at[0], sibling).start()

    def small_grp():
        sm_copy(small, sm_sib, sm_recv.at[0], sibling).wait_recv()
        sm_grp[g] = small[...] + sm_sib[...]
        for k in range(1, groups):
            sm_copy(sm_grp.at[g], sm_grp.at[g], sm_recv.at[1 + g], dev(g_=(g + k) % groups)).start()

    def small_dp():
        for k in range(1, groups):
            gg = (g + k) % groups
            sm_copy(sm_grp.at[gg], sm_grp.at[gg], sm_recv.at[1 + gg], across).wait_recv()
        total = sm_grp[0]
        for k in range(1, groups):
            total = total + sm_grp[k]
        sm_dp[z] = total
        for k in range(1, depth):
            sm_copy(sm_dp.at[z], sm_dp.at[z], sm_recv.at[1 + groups + z], dev(z_=(z + k) % depth)).start()

    def head_copy():
        return rcopy(out_small, sm_sec, sm_send.at[1], sm_recv.at[1 + groups + depth], other)

    def small_sec():
        for k in range(1, depth):
            zz = (z + k) % depth
            sm_copy(sm_dp.at[zz], sm_dp.at[zz], sm_recv.at[1 + groups + zz], across).wait_recv()
        total = sm_dp[0]
        for k in range(1, depth):
            total = total + sm_dp[k]
        out_small[...] = total

        @pl.when(~first_section)
        def _():
            head_copy().start()

    def small_head():
        @pl.when(first_section)
        def _():
            head_copy().wait_recv()
            out_small[pl.ds(HEAD_ROW, 1), :] = sm_sec[pl.ds(HEAD_ROW, 1), :]

        @pl.when(~first_section)
        def _():
            head_copy().wait_send()

    def make_inner():
        @pl.loop(0, 4)
        def _(k):
            make_up(k)

    def make_outer():
        make_attn()

        @pl.loop(0, 3)
        def _(k):
            make_qkv(k)

        pltpu.make_async_copy(high, out_gin, io_sem.at[2]).start()

    beside = (
        ("down", make_down, False),
        ("act", act_back, True),
        ("inner", inner_norm, True),
        ("up", make_inner, False),
        ("attend", attend_back, True),
        ("hidden", hidden_step, True),
        ("qkv", make_outer, False),
    )
    lent_parts = (
        lent_start, functools.partial(lent_line, first_line), functools.partial(lent_line, last_lines), lent_done
    )
    smalls = (small_sib, small_grp, small_dp, small_sec, small_head)

    for p in range(last):
        half_down(p)

    @pl.when(first_section)
    def _():
        grad_copy(last).wait_recv()
        outer_norm(last)

    @pl.loop(0, STEPS)
    def _(i):
        for name, part, inside in beside:
            if inside:
                pl.when(first_section & (i == BESIDE[name]))(functools.partial(part, last))
            else:
                pl.when(i == BESIDE[name])(part)
        for step, part in zip(SMALL_STEPS, smalls):
            pl.when(i == step)(part)
        for step, part in zip(LENT_STEPS, lent_parts):
            pl.when(~first_section & (i == step))(part)
        pl.when(first_section & (i == LENT_BACK))(lent_back)
        for name, at in SLOTS:
            chunks, parts = (X_FIRST, x_stages) if name[0] == "x" else (Z_FIRST, z_stages)
            q = jnp.int32(-1)
            for k, step in enumerate(at):
                q = jnp.where(i == step, k, q)

            runs = q >= 0
            if name[0] == "x" and name[1] != "0":
                runs = runs & ~(first_section & (q == LENT))

            @pl.when(runs)
            def _(q=q, chunks=chunks, part=parts[int(name[1])]):
                part(q, pick(q, chunks))

    count = 1 + (groups - 1) + (depth - 1)
    sent = high.at[pl.ds(0, count * SMALL), :]
    rcopy(sent, sent, sm_send.at[0], sm_recv.at[0], other).wait_send()

    @pl.when(~first_section)
    def _():
        for p in range(pairs):
            grad_copy(p).wait_send()

    pltpu.make_async_copy(high, out_gin, io_sem.at[2]).wait()
    pltpu.make_async_copy(fin, fin, io_sem.at[3]).wait()
    rcopy(s1, s1, r_send.at[0], r_sib.at[0], sibling).wait_send()
    for is_here, chunks in ((first_section, len(X_FIRST) - 1), (~first_section, len(X_FIRST))):

        @pl.when(is_here)
        def _(chunks=chunks):
            part = xr.at[pl.ds(0, chunks)]
            rcopy(part, part, r_send.at[1], r_x.at[0], across).wait_send()
            part = zr.at[pl.ds(0, chunks)]
            rcopy(part, part, r_send.at[2], r_z.at[0, 0], across).wait_send()
            part = fin.at[pl.ds(0, chunks), 0]
            rcopy(part, part, r_send.at[4], r_fin.at[0], across).wait_send()
            if groups > 2:
                part = peers.at[pl.ds(0, chunks), pl.ds(0, groups // 2 - 1)]
                rcopy(part, part, r_send.at[5], r_peer.at[0, 0], across).wait_send()

    rcopy(zw, zw, r_send.at[3], r_z.at[0, 0], across).wait_send()

    @pl.when(first_section)
    def _():
        rcopy(s1.at[0], s1.at[0], k_send.at[0], k_in.at[0], other).wait_send()

    @pl.when(~first_section)
    def _():
        rcopy(rz, rz, k_send.at[1], k_z.at[0], across).wait_send()
        part = rg.at[pl.ds(0, groups - 1)]
        rcopy(part, part, k_send.at[2], k_g.at[0], across).wait_send()
        rcopy(fin.at[0], fin.at[0], k_send.at[3], k_out.at[0], other).wait_send()

    part = xw.at[:, pl.ds(0, groups - 1)]
    rcopy(part, part, r_send.at[6], r_grp.at[0, 0], across).wait_send()


def on_device(groups, depth, embedded, lengths, token_grads, score_grads, w_qkv, w_attn_out, w_up, w_down, biases, gains, head_weight):
    micro, _, seq, _ = embedded.shape
    tokens = micro * seq
    rs = w_qkv.shape[1]
    vmem = pl.BlockSpec(memory_space=pltpu.VMEM)
    smem = pl.BlockSpec(memory_space=pltpu.SMEM)
    hbm = pl.BlockSpec(memory_space=pl.ANY)
    teams = max(groups // 2, 1)
    stages = depth.bit_length() - 1
    out_shape = (
        jax.ShapeDtypeStruct((tokens, D), BF),
        jax.ShapeDtypeStruct((tokens, D), F32),
        jax.ShapeDtypeStruct((rs, 3 * D), BF),
        jax.ShapeDtypeStruct((rs, D), BF),
        jax.ShapeDtypeStruct((rs, FF), BF),
        jax.ShapeDtypeStruct((4 * rs, D), BF),
        jax.ShapeDtypeStruct((SMALL, D), F32),
    )
    nx, nz = len(X_FIRST), len(Z_FIRST)
    scratch = [
        pltpu.VMEM((CHUNKS * D + FF, D), BF),
        pltpu.VMEM((CHUNKS, depth, rs, D), BF),
        pltpu.VMEM((nx, depth, rs, HALF), BF),
        pltpu.VMEM((nx, max(depth - 1, 1), rs, HALF), BF),
        pltpu.VMEM((nz, max(depth - 1, 1), rs, D), BF),
        pltpu.VMEM((nz, groups, rs, D), BF),
        pltpu.VMEM((CHUNKS, 2, rs, HALF), BF),
        pltpu.VMEM((nx, teams, rs, HALF) if groups > 2 else (1, 1, 16, 128), BF),
        pltpu.VMEM((max(depth - 1, 1), rs, D), BF),
        pltpu.VMEM((groups, rs, D), BF),
        pltpu.VMEM((tokens, D), BF),
        pltpu.VMEM((tokens, 3 * D), BF),
        pltpu.VMEM((micro * HEADS, seq, seq), BF),
        pltpu.VMEM((tokens, D), BF),
        pltpu.VMEM((tokens, D), BF),
        pltpu.VMEM((tokens, 1), F32),
        pltpu.VMEM((tokens, D), BF),
        pltpu.VMEM((tokens, FF), BF),
        pltpu.VMEM((tokens, FF), BF),
        pltpu.VMEM((tokens, D), BF),
        pltpu.VMEM((tokens, 1), F32),
        pltpu.VMEM((tokens, D), BF),
        pltpu.VMEM((tokens, D), BF),
        pltpu.VMEM((tokens, D), F32),
        pltpu.VMEM((tokens, D), BF),
        pltpu.VMEM((tokens, 3 * D), BF),
        pltpu.VMEM((SMALL, D), F32),
        pltpu.VMEM((SMALL, D), F32),
        pltpu.VMEM((groups, SMALL, D), F32),
        pltpu.VMEM((depth, SMALL, D), F32),
        pltpu.VMEM((SMALL, D), F32),
        pltpu.SemaphoreType.DMA((2,)),
        pltpu.SemaphoreType.DMA((4,)),
        pltpu.SemaphoreType.DMA((CHUNKS, depth)),
        pltpu.SemaphoreType.DMA((CHUNKS, depth)),
        pltpu.SemaphoreType.DMA((CHUNKS,)),
        pltpu.SemaphoreType.DMA((3,)),
        pltpu.SemaphoreType.DMA((RELAY,)),
        pltpu.SemaphoreType.DMA((RELAY, depth)),
        pltpu.SemaphoreType.DMA((RELAY, depth)),
        pltpu.SemaphoreType.DMA((RELAY,)),
        pltpu.SemaphoreType.DMA((4,)),
        pltpu.SemaphoreType.DMA((1,)),
        pltpu.SemaphoreType.DMA((max(stages, 1),)),
        pltpu.SemaphoreType.DMA((groups,)),
        pltpu.SemaphoreType.DMA((1,)),
        pltpu.SemaphoreType.DMA((4,)),
        pltpu.SemaphoreType.DMA((4,)),
        pltpu.SemaphoreType.DMA((4,)),
        pltpu.SemaphoreType.DMA((7,)),
        pltpu.SemaphoreType.DMA((CHUNKS,)),
        pltpu.SemaphoreType.DMA((CHUNKS,)),
        pltpu.SemaphoreType.DMA((CHUNKS, max(stages, 1))),
        pltpu.SemaphoreType.DMA((nz, groups)),
        pltpu.SemaphoreType.DMA((CHUNKS,)),
        pltpu.SemaphoreType.DMA((CHUNKS, teams)),
        pltpu.SemaphoreType.DMA((2,)),
        pltpu.SemaphoreType.DMA((2 + groups + depth,)),
    ]
    state, grad_in, *grads, small = pl.pallas_call(
        functools.partial(kernel, (groups, depth, rs, seq)),
        out_shape=out_shape,
        in_specs=[hbm] * 6 + [smem] * 2 + [vmem] * 3,
        out_specs=(hbm,) * 6 + (vmem,),
        scratch_shapes=scratch,
        compiler_params=pltpu.CompilerParams(
            collective_id=0, has_side_effects=True, vmem_limit_bytes=65300 * 1024
        ),
    )(
        embedded.reshape(tokens, D),
        token_grads.reshape(tokens, D),
        w_qkv[0],
        w_attn_out[0],
        w_up[0],
        w_down[0],
        lengths.reshape(micro),
        score_grads.reshape(micro),
        biases,
        gains[0],
        head_weight,
    )
    results = pl.pallas_call(
        hand_out,
        out_shape=[jax.ShapeDtypeStruct(x.shape, x.dtype) for x in (state, grad_in)]
        + [jax.ShapeDtypeStruct(x.shape, F32) for x in grads]
        + [jax.ShapeDtypeStruct(x, F32) for x in ((1, 10 * D), (2, D), (D,))],
        in_specs=[vmem] * 7,
        out_specs=[vmem] * 9,
    )(state, grad_in, *grads, small)
    state, grad_in, g_qkv, g_attn, g_up, g_down, g_bias, g_gain, g_head = results
    return (
        state.reshape(1, micro, 1, seq, D),
        grad_in.reshape(1, micro, 1, seq, D),
        g_qkv[None],
        g_attn[None],
        g_up[None],
        g_down[None],
        g_bias,
        g_gain[None],
        g_head,
    )


def hand_out(state, grad_in, gq, go, gu, gd, small, o_state, o_gin, o_q, o_o, o_u, o_d, o_bias, o_gain, o_head):
    for src, dst in ((state, o_state), (grad_in, o_gin), (gq, o_q), (go, o_o), (gu, o_u), (gd, o_d)):
        dst[...] = src[...].astype(dst.dtype)
    for k in range(10):
        o_bias[:, pl.ds(k * D, D)] = small[pl.ds(k, 1), :]
    o_gain[...] = small[pl.ds(GAIN1, 2), :]
    o_head[...] = small[HEAD_ROW, :]


def solution(mesh):
    return jax.shard_map(
        functools.partial(on_device, mesh.shape["grp"], mesh.shape["dp"] // 2),
        mesh=mesh,
        in_specs=(
            P(None, ("grp", "dp"), None, None),
            P(None, ("grp", "dp")),
            P(None, ("grp", "dp"), None, None),
            P(None, ("grp", "dp")),
            P("section", "dp", None),
            P("section", "dp", None),
            P("section", "dp", None),
            P("section", "dp", None),
            P("section", None),
            P("section", None, None),
            P(),
        ),
        out_specs=(
            P("section", None, ("grp", "dp"), None, None),
            P("section", None, ("grp", "dp"), None, None),
            P("section", "dp", None),
            P("section", "dp", None),
            P("section", "dp", None),
            P("section", "dp", None),
            P("section", None),
            P("section", None, None),
            P(),
        ),
        check_vma=False,
    )
```

```python
import functools
import math

import jax
import jax.numpy as jnp
from jax import lax
from jax.experimental import pallas as pl
from jax.experimental.pallas import tpu as pltpu
from jax.sharding import PartitionSpec as P

D = 768
FF = 3072
HEADS = 12
HEAD = 64
EPSILON = 1e-06
CHUNKS = 12
HALF = D // 2
DOWN = 8 * D
DOWN_GRAD = 12 * D
SCALE = 1.0 / math.sqrt(HEAD)
F32 = jnp.float32
BF = jnp.bfloat16
MESH = pl.DeviceIdType.MESH
BQ, BV, BO, BU, BD, BETA1, BETA2, GAIN1, GAIN2, HEAD_ROW = 0, 1, 2, 3, 7, 8, 9, 10, 11, 12
SMALL = 16
RELAY = 1
TAKE = (8,)
X_FIRST = (8, 4, 5, 6, 7, 3, 0, 1, 2)
Z_FIRST = (9, 10, 11)
SLOTS = (
    ("x0", (0, 2, 1, 4, 3, 6, 5, 7, 9)),
    ("z0", (0, 3, 2)),
    ("z3", (14, 15, 17)),
    ("x4", (8, 12, 9, 13, 11, 14, 15, 16, 17)),
    ("x3", (6, 9, 7, 11, 8, 12, 13, 14, 15)),
    ("z2", (4, 11, 13)),
    ("x2", (3, 6, 4, 8, 7, 9, 11, 12, 13)),
    ("z1", (2, 5, 7)),
    ("x1", (1, 3, 2, 5, 4, 7, 8, 10, 11)),
)
BESIDE = {"down": 0, "act": 1, "inner": 1, "up": 1, "attend": 3, "hidden": 4, "qkv": 5}
SMALL_STEPS = (4, 5, 6, 8, 10)
LENT = 4
LENT_STEPS = (7, 9, 11, 13)
LENT_BACK = 17
STEPS = 1 + max(LENT_BACK, max(max(steps) for _, steps in SLOTS))


def dot(a, b):
    return lax.dot_general(a, b, (((1,), (0,)), ((), ())), preferred_element_type=F32)


def dot_t(a, b):
    return lax.dot_general(a, b, (((1,), (1,)), ((), ())), preferred_element_type=F32)


def dot_c(a, b):
    return lax.dot_general(a, b, (((0,), (0,)), ((), ())), preferred_element_type=F32)


def span(i, width):
    return pl.ds(pl.multiple_of(i * width, width), width)


def flip(index, mask):
    bit = 1
    while bit <= mask:
        if mask & bit:
            index = index + bit - 2 * bit * ((index // bit) % 2)
        bit *= 2
    return index


def masks(bits):
    found = [0]
    for bit in bits:
        found = found + [mask ^ bit for mask in found]
    return found


def pick(i, values):
    found = values[-1]
    for k in range(len(values) - 2, -1, -1):
        found = jnp.where(i == k, values[k], found)
    return found


def row_sum(x):
    return jnp.sum(x, 0, keepdims=True)


def gelu_parts(x):
    t = 1.0 / (1.0 + (0.3275911 * math.sqrt(0.5)) * jnp.abs(x))
    e = jnp.exp2((-0.5 * math.log2(math.e)) * (x * x))
    tail = t * (0.127414796 + t * (-0.142248368 + t * (0.7107068705 + t * (-0.7265760135 + t * 0.5307027145)))) * e
    phi = jnp.where(x >= 0, 1.0 - tail, tail)
    return x * phi, phi + x * (e * (1.0 / math.sqrt(2.0 * math.pi)))


def normed(x):
    centred = x - jnp.mean(x, -1, keepdims=True)
    scale = lax.rsqrt(jnp.mean(centred * centred, -1, keepdims=True) + EPSILON)
    return centred * scale, scale


def norm_back(grad, n, scale, gain):
    gg = gain * grad
    return (gg - jnp.mean(gg, -1, keepdims=True) - n * jnp.mean(gg * n, -1, keepdims=True)) * scale


def kernel(sizes, *refs):
    groups, depth, rs, seq = sizes
    (emb, token_grads, wq_in, wo_in, wu_in, wd_in, bias_in, gains_in, head_in, lens, scores,
     out_sec, out_gin, out_q, out_o, out_u, out_d, out_small,
     big, s1, xr, zr, zw, xw, fin, peers, rz, rg,
     hbuf, qkv, probs, mixed, n1, r1, first_low, act, gp, n2, r2, outb, gbuf, high, dd, dqkv,
     small, sm_sib, sm_grp, sm_dp, sm_sec,
     bias, gains, head_w, local_sem, io_sem, g_zr, g_xr, g_sr, g_send, b_own, b_zr, b_xr, b_back, b_send, k_in, k_z, k_g, k_out, k_send, y_send, y_recv,
     r_send, r_sib, r_x, r_z, r_grp, r_fin, r_peer, sm_send, sm_recv) = refs
    stages = depth.bit_length() - 1
    da, dm = n1, n2
    pairs = 2
    sec = lax.axis_index("section")
    g = lax.axis_index("grp")
    d = lax.axis_index("dp")
    z, c = d // 2, d % 2
    par = g % 2
    first_section = sec == 0

    def dev(sec_=None, g_=None, z_=None, c_=None):
        return (
            sec if sec_ is None else sec_,
            g if g_ is None else g_,
            (z if z_ is None else z_) * 2 + (c if c_ is None else c_),
        )

    sibling = dev(c_=1 - c)
    across = dev(g_=g + 1 - 2 * par)
    other = dev(sec_=1 - sec)

    def rcopy(src, dst, send, recv, to):
        return pltpu.make_async_remote_copy(
            src_ref=src, dst_ref=dst, send_sem=send, recv_sem=recv, device_id=to, device_id_type=MESH
        )

    def shard_row(m, owner, down=DOWN):
        row = jnp.where(m < 8, m * D + owner * rs, down + owner * (4 * rs) + (m - 8) * rs)
        return pl.multiple_of(row, 16)

    barrier = pltpu.get_barrier_semaphore()
    greeted = 0
    for to in [sibling, other]:
        pl.semaphore_signal(barrier, inc=1, device_id=to, device_id_type=MESH)
        greeted += 1
    for k in range(1, groups):
        pl.semaphore_signal(barrier, inc=1, device_id=dev(g_=(g + k) % groups), device_id_type=MESH)
        greeted += 1
    for k in range(1, depth):
        pl.semaphore_signal(barrier, inc=1, device_id=dev(z_=(z + k) % depth), device_id_type=MESH)
        greeted += 1

    own = []
    for k in range(3):
        own.append((wq_in.at[:, pl.ds(k * D, D)], k))
    own.append((wo_in, 3))
    for k in range(4):
        own.append((wu_in.at[:, pl.ds(k * D, D)], 4 + k))
    for src, k in own:
        pltpu.make_async_copy(src, big.at[pl.ds(pl.multiple_of(k * D + d * rs, 16), rs), :], local_sem.at[0]).start()
    pltpu.make_async_copy(
        wd_in, big.at[pl.ds(pl.multiple_of(DOWN + d * 4 * rs, 16), 4 * rs), :], local_sem.at[0]
    ).start()

    vectors = [
        pltpu.make_async_copy(src, dst, local_sem.at[2 + k])
        for k, (src, dst) in enumerate(((bias_in, bias), (gains_in, gains), (head_in, head_w)))
    ]
    for copy in vectors:
        copy.start()

    def have_vectors():
        for copy in vectors:
            copy.wait()

    @pl.when(first_section)
    def _():
        pltpu.make_async_copy(emb, hbuf, local_sem.at[1]).start()

    @pl.when(~first_section)
    def _():
        pltpu.make_async_copy(token_grads, gbuf, local_sem.at[1]).start()

    small[...] = jnp.zeros_like(small)
    pl.semaphore_wait(barrier, greeted)
    pltpu.make_async_copy(
        big.at[pl.ds(0, CHUNKS * rs), :], big.at[pl.ds(0, CHUNKS * rs), :], local_sem.at[0]
    ).wait()

    def region(m, zz, half=None, cc=c):
        cols = slice(None) if half is None else span(half, HALF)
        return big.at[pl.ds(shard_row(m, 2 * zz + cc), rs), cols]

    far = [depth >> (t + 1) for t in range(stages)]
    held = [masks(far[:t]) for t in range(stages + 1)]

    def along(m, zz, t):
        part = region(m, zz, par)
        return rcopy(part, part, g_send.at[0], g_zr.at[m, zz], dev(z_=flip(z, far[t])))

    def over(m, zz, half):
        part = region(m, zz, half)
        return rcopy(part, part, g_send.at[1], g_xr.at[m, zz], across)

    def beside(m, zz, half):
        part = region(m, zz, half)
        return rcopy(part, part, g_send.at[2], g_sr.at[m], sibling)

    def relayed(b, zz, half):
        return dd.at[pl.ds(pl.multiple_of((b * depth + zz) * rs, 16), rs), span(half, HALF)]

    def lend(b):
        return rcopy(
            region(CHUNKS - RELAY + b, z, par), relayed(b, z, par), b_send.at[0], b_own.at[b], other
        )

    def relay_along(b, zz, t):
        part = relayed(b, zz, par)
        return rcopy(part, part, b_send.at[1], b_zr.at[b, zz], dev(z_=flip(z, far[t])))

    def relay_over(b, zz, half):
        part = relayed(b, zz, half)
        return rcopy(part, part, b_send.at[2], b_xr.at[b, zz], across)

    def give_back(b, zz, half):
        return rcopy(
            relayed(b, zz, half), region(CHUNKS - RELAY + b, zz, half), b_send.at[3], b_back.at[b], other
        )

    def relay_own(b):
        lend(b).wait_recv()
        relay_along(b, z, 0).start()

    def relay_arrived(t, b):
        for mask in held[t]:
            zz = flip(z, far[t] ^ mask)
            relay_along(b, zz, t).wait_recv()
            relay_over(b, zz, par).start()
            give_back(b, zz, par).start()
        if t + 1 < stages:
            for mask in held[t + 1]:
                relay_along(b, flip(z, mask), t + 1).start()

    def relay_crossed(t, b):
        for mask in held[t]:
            zz = flip(z, far[t] ^ mask)
            relay_over(b, zz, 1 - par).wait_recv()
            give_back(b, zz, 1 - par).start()

    def take(b):
        got = big.at[pl.ds(0, (depth - 1) * rs), :]
        rcopy(got, got, b_send.at[3], b_back.at[b], other).wait_recv()
        for k in range(1, depth):
            beside(CHUNKS - RELAY + b, (z + k) % depth, None).start()

    def bias_row(start, width=D):
        return bias[:, pl.ds(start, width)]

    low = lax.broadcasted_iota(jnp.int32, (1, 128), 1) < HEAD
    key = lax.broadcasted_iota(jnp.int32, (1, seq), 1)

    def pair_rows(p):
        return span(p, seq)

    def block(k):
        return big[pl.ds(k * D, D), :]

    def project(p, k):
        r = pair_rows(p)
        x = dot(hbuf[r, :], block(k))
        if k != 1:
            x = x + bias_row(0 if k == 0 else D)
        qkv[r, pl.ds(k * D, D)] = x.astype(BF)

    def both_heads(x):
        none = jnp.zeros_like(x)
        return jnp.concatenate([jnp.where(low, x, none), jnp.where(low, none, x)], 0)

    def ahead(make):
        coming = make(0)
        for j in range(HEADS // 2):
            now, coming = coming, make(j + 1) if j + 1 < HEADS // 2 else None
            yield j, now

    def attend(p):
        r = pair_rows(p)
        ok = key < lens[p]

        def scores_of(j):
            q2 = qkv[r, pl.ds(j * 128, 128)] * jnp.asarray(SCALE, BF)
            return dot_t(both_heads(q2), qkv[r, pl.ds((j + 6) * 128, 128)])

        for j, sc in ahead(scores_of):
            sc = jnp.where(ok, sc, -1e30)
            e = jnp.exp(sc - jnp.max(sc, -1, keepdims=True))
            pr = (e * (1.0 / jnp.sum(e, -1, keepdims=True))).astype(BF)
            probs[p * HEADS + 2 * j] = pr[:seq]
            probs[p * HEADS + 2 * j + 1] = pr[seq:]
            o = dot(pr, qkv[r, pl.ds((j + 12) * 128, 128)])
            mixed[r, pl.ds(j * 128, 128)] = jnp.where(low, o[:seq], o[seq:]).astype(BF)

    def join(p):
        r = pair_rows(p)
        n, scale = normed(hbuf[r, :].astype(F32) + dot(mixed[r, :], block(3)) + bias_row(2 * D))
        n1[r, :] = n.astype(BF)
        r1[r, :] = scale
        y = n * gains[0:1, :] + bias_row(4 * D + FF)
        high[r, :] = y
        first_low[r, :] = y.astype(BF)

    def widen(p, k):
        r = pair_rows(p)
        for t in range(3):
            w = big[pl.ds((4 + k) * D, D), pl.ds(t * 256, 256)]
            col = k * D + t * 256
            a, dg = gelu_parts(dot(first_low[r, :], w) + bias_row(3 * D + col, 256))
            act[r, pl.ds(col, 256)] = a.astype(BF)
            gp[r, pl.ds(col, 256)] = dg.astype(BF)

    def narrow(p):
        r = pair_rows(p)
        n, scale = normed(high[r, :] + dot(act[r, :], big[pl.ds(DOWN, FF), :]) + bias_row(3 * D + FF))
        n2[r, :] = n.astype(BF)
        r2[r, :] = scale
        y = n * gains[1:2, :] + bias_row(5 * D + FF)
        outb[r, :] = y.astype(BF)

        @pl.when(~first_section)
        def _():
            small[pl.ds(HEAD_ROW, 1), :] += scores[p] * y[0:1]

    def state_copy(p):
        r = pair_rows(p)
        return rcopy(outb.at[r, :], hbuf.at[r, :], y_send.at[p], y_recv.at[p], other)

    def out_copy(p):
        r = pair_rows(p)
        return pltpu.make_async_copy(outb.at[r, :], out_sec.at[r, :], io_sem.at[p])

    def chunk_ready(m):
        whole = big.at[pl.ds(0, depth * rs), :]
        rcopy(whole, whole, g_send.at[2], g_sr.at[m], sibling).wait_recv()

    def own_step(n):
        if stages:
            along(n, z, 0).start()
        beside(n, z, None).start()

    def arrived(m, t):
        for mask in held[t]:
            zz = flip(z, far[t] ^ mask)
            along(m, zz, t).wait_recv()
            over(m, zz, par).start()
            beside(m, zz, par).start()
        if t + 1 < stages:
            for mask in held[t + 1]:
                along(m, flip(z, mask), t + 1).start()

    def crossed(m, t):
        for mask in held[t]:
            zz = flip(z, far[t] ^ mask)
            over(m, zz, 1 - par).wait_recv()
            beside(m, zz, 1 - par).start()

    def early(step, pieces):
        def run(n):
            @pl.when(first_section & (n == stages + 2 + step))
            def _():
                pieces()

        return run

    def both_pairs(piece):
        @pl.loop(0, pairs)
        def _(p):
            piece(p)

    def early_project(k):
        if k == 0:
            pltpu.make_async_copy(emb, hbuf, local_sem.at[1]).wait()
            have_vectors()
        chunk_ready(k)
        both_pairs(lambda p: project(p, k))

    def early_join():
        chunk_ready(3)
        both_pairs(join)

    def early_widen(k):
        chunk_ready(4 + k)
        both_pairs(lambda p: widen(p, k))

    plan = [early(k, functools.partial(early_project, k)) for k in range(3)]
    plan.append(early(2, lambda: attend(0)))
    plan.append(early(3, lambda: attend(1)))
    plan.append(early(4, early_join))
    plan += [early(4 + k, functools.partial(early_widen, k)) for k in range(4)]

    mine = jnp.where(first_section, CHUNKS - RELAY, CHUNKS)

    @pl.loop(0, mine + stages + 1)
    def _(n):
        pl.when(n < mine)(functools.partial(own_step, n))

        @pl.when(first_section & (n < RELAY))
        def _():
            lend(n).start()
            beside(CHUNKS - RELAY + n, z, None).start()

        relay_stages = [relay_own]
        for t in range(stages):
            relay_stages.append(functools.partial(relay_arrived, t))
        for lag, stage in enumerate(relay_stages):
            b = n - 1 - lag
            pl.when(~first_section & (b >= 0) & (b < RELAY))(functools.partial(stage, b))
        for t in range(stages):
            b = n - 3 - t
            pl.when(~first_section & (b >= 0) & (b < RELAY))(functools.partial(relay_crossed, t, b))
        for t in range(stages):
            m = n - t - 1
            pl.when((m >= 0) & (m < mine))(functools.partial(arrived, m, t))
        for t in range(stages):
            m = n - t - 2
            pl.when((m >= 0) & (m < mine))(functools.partial(crossed, m, t))
        for b in range(RELAY):
            pl.when(first_section & (n == TAKE[b]))(functools.partial(take, b))
        for run in plan:
            run(n)

    @pl.loop(jnp.where(first_section, 8, 0), CHUNKS)
    def _(m):
        chunk_ready(m)

    @pl.when(first_section)
    def _():
        @pl.loop(0, pairs)
        def _(p):
            narrow(p)
            state_copy(p).start()
            out_copy(p).start()

    @pl.when(~first_section)
    def _():
        pltpu.make_async_copy(token_grads, gbuf, local_sem.at[1]).wait()
        have_vectors()

    for is_first, count in ((first_section, CHUNKS - RELAY), (~first_section, CHUNKS)):

        @pl.when(is_first)
        def _(count=count):
            sent = big.at[pl.ds(0, count * (depth - 1) * rs), pl.ds(0, HALF)]
            rcopy(sent, sent, g_send.at[0], g_zr.at[0, 0], across).wait_send()
            rcopy(sent, sent, g_send.at[1], g_xr.at[0, 0], across).wait_send()

    def relay_sent(k, rows, cols):
        sent = big.at[pl.ds(0, rows), pl.ds(0, cols)]
        rcopy(sent, sent, b_send.at[k], b_own.at[0], other).wait_send()

    @pl.when(first_section)
    def _():
        relay_sent(0, RELAY * rs, HALF)

    @pl.when(~first_section)
    def _():
        relay_sent(1, RELAY * (depth - 1) * rs, HALF)
        relay_sent(2, RELAY * (depth - 1) * rs, HALF)
        relay_sent(3, RELAY * (depth - 1) * rs, D)

    sent = big.at[pl.ds(0, CHUNKS * depth * rs), :]
    rcopy(sent, sent, g_send.at[2], g_sr.at[0], sibling).wait_send()

    def add_small(row, x):
        small[pl.ds(row, 1), :] += row_sum(x)

    def outer_norm(p):
        r = pair_rows(p)
        length = jnp.where(first_section, seq, lens[p])
        score = jnp.where(first_section, 0.0, scores[p])
        place = lax.broadcasted_iota(jnp.int32, (seq, 1), 0)
        grad = jnp.where(place < length, gbuf[r, :].astype(F32), 0.0)
        grad = grad + jnp.where(place == 0, score * head_w[...].reshape(1, D), 0.0)
        n = n2[r, :].astype(F32)
        x = norm_back(grad, n, r2[r, :], gains[1:2, :])
        xl = x.astype(BF)
        high[r, :] = x
        dd[r, :] = xl
        add_small(BD, xl.astype(F32))
        add_small(BETA2, grad)
        add_small(GAIN2, grad * n)

    def act_back(p):
        r = pair_rows(p)
        for k in range(4):
            c4 = pl.ds(k * D, D)
            x = (dot_t(dd[r, :], big[pl.ds(DOWN + k * D, D), :]) * gp[r, c4].astype(F32)).astype(BF)
            gp[r, c4] = x
            add_small(BU + k, x.astype(F32))

    def inner_norm(p):
        r = pair_rows(p)
        grad = high[r, :]
        for k in range(4):
            grad = grad + dot_t(gp[r, pl.ds(k * D, D)], block(4 + k))
        n = n1[r, :].astype(F32)
        x = norm_back(grad, n, r1[r, :], gains[0:1, :])
        xl = x.astype(BF)
        high[r, :] = x
        da[r, :] = xl
        add_small(BO, xl.astype(F32))
        add_small(BETA1, grad)
        add_small(GAIN1, grad * n)
        dm[r, :] = dot_t(xl, block(3)).astype(BF)

    def attend_back(p):
        r = pair_rows(p)

        def dprobs_of(j):
            return dot_t(both_heads(dm[r, pl.ds(j * 128, 128)]), qkv[r, pl.ds((j + 12) * 128, 128)])

        for j, dp in ahead(dprobs_of):
            q2 = qkv[r, pl.ds(j * 128, 128)]
            k2 = qkv[r, pl.ds((j + 6) * 128, 128)]
            pr = jnp.concatenate([probs[p * HEADS + 2 * j], probs[p * HEADS + 2 * j + 1]], 0)
            pf = pr.astype(F32)
            t = pf * dp
            ds = (t - pf * jnp.sum(t, -1, keepdims=True)).astype(BF)
            dq = dot(ds, k2)
            dq = (jnp.where(low, dq[:seq], dq[seq:]) * SCALE).astype(BF)
            qt, dt = q2.T, dm[r, pl.ds(j * 128, 128)].T
            dk = jnp.concatenate([dot(qt[:HEAD], ds[:seq]), dot(qt[HEAD:], ds[seq:])], 0)
            dv = jnp.concatenate([dot(dt[:HEAD], pr[:seq]), dot(dt[HEAD:], pr[seq:])], 0)
            dk = (dk * SCALE).astype(BF).T
            dv = dv.astype(BF).T
            dqkv[r, pl.ds(j * 128, 128)] = dq
            dqkv[r, pl.ds((j + 6) * 128, 128)] = dk
            dqkv[r, pl.ds((j + 12) * 128, 128)] = dv
            small[pl.ds(BQ, 1), pl.ds(j * 128, 128)] += row_sum(dq.astype(F32))
            small[pl.ds(BV, 1), pl.ds(j * 128, 128)] += row_sum(dv.astype(F32))

    def hidden_back(p):
        r = pair_rows(p)
        grad = high[r, :]
        for k in range(3):
            grad = grad + dot_t(dqkv[r, pl.ds(k * D, D)], block(k))
        high[r, :] = grad
        outb[r, :] = grad.astype(BF)

    def grad_copy(p):
        r = pair_rows(p)
        return rcopy(outb.at[r, :], gbuf.at[r, :], y_send.at[2 + p], y_recv.at[2 + p], other)

    def weight_grad(left, lcol, right, rcol, row):
        a = left[:, pl.ds(pl.multiple_of(lcol, 256), D)]
        b = right[:, pl.ds(pl.multiple_of(rcol, 256), D)]
        big[pl.ds(pl.multiple_of(row, 256), D), :] = dot_c(a, b).astype(BF)

    def sib_copy(m, zz):
        return rcopy(
            big.at[pl.ds(shard_row(m, 2 * zz + 1 - c, DOWN_GRAD), rs), :],
            s1.at[m, zz], r_send.at[0], r_sib.at[m], sibling,
        )

    def sib_send(m):
        @pl.loop(0, depth)
        def _(zz):
            sib_copy(m, zz).start()

    def half_down(p):
        r = pair_rows(p)

        @pl.loop(0, 4)
        def _(k):
            x = dot_c(act[r, span(k, D)], dd[r, :])
            place = pl.ds(pl.multiple_of(DOWN_GRAD + k * D, 256), D)
            if p > 0:
                x = x + big[place, :].astype(F32)
            big[place, :] = x.astype(BF)

    def make_down():
        half_down(last)

        @pl.loop(8, 12)
        def _(m):
            sib_send(m)

    def make_up(k):
        weight_grad(first_low, 0, gp, k * D, (4 + k) * D)
        sib_send(4 + k)

    def make_attn():
        weight_grad(mixed, 0, da, 0, 3 * D)
        sib_send(3)

    def make_qkv(k):
        weight_grad(hbuf, 0, dqkv, k * D, k * D)
        sib_send(k)

    def pair_sums(m):
        rcopy(s1.at[m], s1.at[m], r_send.at[0], r_sib.at[m], sibling).wait_recv()

        @pl.loop(0, depth)
        def _(zz):
            mine = big[pl.ds(shard_row(m, 2 * zz + c, DOWN_GRAD), rs), :]
            s1[m, zz] = (mine.astype(F32) + s1[m, zz].astype(F32)).astype(BF)

    sides = [masks([2 << k for k in range(t, stages - 1)]) for t in range(stages)]
    slots = [sum(len(side) for side in sides[:t]) for t in range(stages)]

    def line_send(part, landing, m, t, send):
        for k, mask in enumerate(sides[t]):
            rcopy(
                part.at[flip(z, (1 << t) ^ mask)], landing.at[slots[t] + k], send, r_z.at[m, t],
                dev(z_=flip(z, 1 << t)),
            ).start()

    def line_add(part, landing, m, t, send):
        here = landing.at[pl.ds(slots[t], len(sides[t]))]
        rcopy(here, here, send, r_z.at[m, t], dev(z_=flip(z, 1 << t))).wait_recv()
        for k, mask in enumerate(sides[t]):
            zz = flip(z, mask)
            part[zz] = (part[zz].astype(F32) + landing[slots[t] + k].astype(F32)).astype(BF)

    def put_out(m):
        def put(to, row, col):
            for h in range(2):
                rows = pl.ds(pl.multiple_of(row, 16), rs)
                cols = pl.ds(pl.multiple_of(col + h * HALF, 128), HALF)
                pltpu.make_async_copy(fin.at[m, h], to.at[rows, cols], io_sem.at[3]).start()

        pl.when(m >= 8)(lambda: put(out_d, (m - 8) * rs, 0))
        pl.when((m >= 4) & (m < 8))(lambda: put(out_u, 0, (m - 4) * D))
        pl.when(m == 3)(lambda: put(out_o, 0, 0))
        pl.when(m < 3)(lambda: put(out_q, 0, m * D))

    def x_copy(q, m):
        return rcopy(
            s1.at[m, :, :, span(1 - par, HALF)], xr.at[q], r_send.at[1], r_x.at[m], across
        )

    def fin_copy(m):
        return rcopy(fin.at[m, par], fin.at[m, par], r_send.at[4], r_fin.at[m], across)

    lent = X_FIRST[LENT]

    def lent_shard(zz):
        return qkv.at[pl.ds(pl.multiple_of(zz * rs, 16), rs), pl.ds(0, D)]

    def lend_sums():
        for zz in range(depth):
            rcopy(s1.at[lent, zz], lent_shard(zz), k_send.at[0], k_in.at[0], other).start()

    def lent_send(t):
        for k, mask in enumerate(sides[t]):
            rcopy(
                lent_shard(flip(z, (1 << t) ^ mask)), rz.at[slots[t] + k], k_send.at[1], k_z.at[t],
                dev(z_=flip(z, 1 << t)),
            ).start()

    def lent_add(t):
        here = rz.at[pl.ds(slots[t], len(sides[t]))]
        rcopy(here, here, k_send.at[1], k_z.at[t], dev(z_=flip(z, 1 << t))).wait_recv()
        for k, mask in enumerate(sides[t]):
            part = lent_shard(flip(z, mask))
            part[...] = (part[...].astype(F32) + rz[slots[t] + k].astype(F32)).astype(BF)

    def lent_start():
        whole = qkv.at[pl.ds(0, depth * rs), pl.ds(0, D)]
        rcopy(whole, whole, k_send.at[0], k_in.at[0], other).wait_recv()
        lent_send(0)

    def lent_line(ts):
        for t in ts:
            lent_add(t)
            if t + 1 < stages:
                lent_send(t + 1)
        if stages - 1 in ts:
            rg[g] = lent_shard(z)[...]
            for k in range(1, groups):
                rcopy(rg.at[g], rg.at[g], k_send.at[2], k_g.at[g], dev(g_=(g + k) % groups)).start()

    def lent_done():
        for k in range(1, groups):
            gg = (g + k) % groups
            rcopy(rg.at[gg], rg.at[gg], k_send.at[2], k_g.at[gg], across).wait_recv()
        total = rg[0].astype(F32)
        for k in range(1, groups):
            total = total + rg[k].astype(F32)
        qkv[pl.ds(0, rs), pl.ds(D, D)] = total.astype(BF)
        for h in range(2):
            rcopy(
                qkv.at[pl.ds(0, rs), pl.ds(D + h * HALF, HALF)], fin.at[lent, h], k_send.at[3], k_out.at[0], other
            ).start()

    def lent_back():
        rcopy(fin.at[lent], fin.at[lent], k_send.at[3], k_out.at[0], other).wait_recv()
        put_out(jnp.int32(lent))

    def x_start(q, m):
        pair_sums(m)
        lends = first_section & (q == LENT)
        pl.when(lends)(lend_sums)
        pl.when(~lends)(lambda: x_copy(q, m).start())

    def x_halves(q, m):
        x_copy(q, m).wait_recv()

        @pl.loop(0, depth)
        def _(zz):
            mine = s1[m, zz, :, span(par, HALF)]
            xr[q, zz] = (mine.astype(F32) + xr[q, zz].astype(F32)).astype(BF)

        line_send(xr.at[q], zr.at[q], m, 0, r_send.at[2])

    def lines(part, landing, m, ts, send):
        for t in ts:
            line_add(part, landing, m, t, send)
            if t + 1 < stages:
                line_send(part, landing, m, t + 1, send)

    def x_line(ts, q, m):
        lines(xr.at[q], zr.at[q], m, ts, r_send.at[2])
        if stages - 1 not in ts:
            return
        total = xr[q, z]
        if groups > 2:
            teams = groups // 2
            team = g // 2
            peers[q, team] = total
            for k in range(1, teams):
                to = dev(g_=((team + k) % teams) * 2 + par)
                rcopy(peers.at[q, team], peers.at[q, team], r_send.at[5], r_peer.at[m, team], to).start()
            for k in range(1, teams):
                tt = (team + k) % teams
                rcopy(peers.at[q, tt], peers.at[q, tt], r_send.at[5], r_peer.at[m, tt], across).wait_recv()
            total = peers[q, 0].astype(F32)
            for k in range(1, teams):
                total = total + peers[q, k].astype(F32)
            total = total.astype(BF)
        fin[m, par] = total
        fin_copy(m).start()

    def x_finish(q, m):
        rcopy(fin.at[m, 1 - par], fin.at[m, 1 - par], r_send.at[4], r_fin.at[m], across).wait_recv()
        put_out(m)

    def z_start(q, m):
        pair_sums(m)
        line_send(s1.at[m], zw.at[q], m, 0, r_send.at[3])

    def z_line(ts, q, m):
        lines(s1.at[m], zw.at[q], m, ts, r_send.at[3])
        if stages - 1 not in ts:
            return
        xw[q, g] = s1[m, z]
        for k in range(1, groups):
            rcopy(xw.at[q, g], xw.at[q, g], r_send.at[6], r_grp.at[q, g], dev(g_=(g + k) % groups)).start()

    def z_finish(q, m):
        for k in range(1, groups):
            gg = (g + k) % groups
            rcopy(xw.at[q, gg], xw.at[q, gg], r_send.at[6], r_grp.at[q, gg], across).wait_recv()
        total = xw[q, 0].astype(F32)
        for k in range(1, groups):
            total = total + xw[q, k].astype(F32)
        total = total.astype(BF)
        fin[m, 0] = total[:, :HALF]
        fin[m, 1] = total[:, HALF:]
        put_out(m)

    first_line, last_lines = range(0, 1), range(1, stages)
    if stages == 1:
        first_line, last_lines = range(0, 0), range(0, 1)
    x_stages = [
        x_start, x_halves, functools.partial(x_line, first_line), functools.partial(x_line, last_lines), x_finish
    ]
    z_stages = [z_start, functools.partial(z_line, first_line), functools.partial(z_line, last_lines), z_finish]

    last = pairs - 1

    def hidden_step(p):
        out_copy(p).wait()

        @pl.when(first_section)
        def _():
            state_copy(p).wait_send()

        hidden_back(p)

    @pl.loop(0, jnp.where(first_section, last, pairs))
    def _(p):
        @pl.when(~first_section)
        def _():
            state_copy(p).wait_recv()
            for k in range(3):
                project(p, k)
            attend(p)
            join(p)
            for k in range(4):
                widen(p, k)
            narrow(p)
            out_copy(p).start()

        @pl.when(first_section)
        def _():
            grad_copy(p).wait_recv()

        outer_norm(p)
        act_back(p)
        inner_norm(p)
        attend_back(p)
        hidden_step(p)

        @pl.when(~first_section)
        def _():
            grad_copy(p).start()

    def sm_copy(src, dst, recv, to):
        return rcopy(src, dst, sm_send.at[0], recv, to)

    def small_sib():
        sm_copy(small, sm_sib, sm_recv.at[0], sibling).start()

    def small_grp():
        sm_copy(small, sm_sib, sm_recv.at[0], sibling).wait_recv()
        sm_grp[g] = small[...] + sm_sib[...]
        for k in range(1, groups):
            sm_copy(sm_grp.at[g], sm_grp.at[g], sm_recv.at[1 + g], dev(g_=(g + k) % groups)).start()

    def small_dp():
        for k in range(1, groups):
            gg = (g + k) % groups
            sm_copy(sm_grp.at[gg], sm_grp.at[gg], sm_recv.at[1 + gg], across).wait_recv()
        total = sm_grp[0]
        for k in range(1, groups):
            total = total + sm_grp[k]
        sm_dp[z] = total
        for k in range(1, depth):
            sm_copy(sm_dp.at[z], sm_dp.at[z], sm_recv.at[1 + groups + z], dev(z_=(z + k) % depth)).start()

    def head_copy():
        return rcopy(out_small, sm_sec, sm_send.at[1], sm_recv.at[1 + groups + depth], other)

    def small_sec():
        for k in range(1, depth):
            zz = (z + k) % depth
            sm_copy(sm_dp.at[zz], sm_dp.at[zz], sm_recv.at[1 + groups + zz], across).wait_recv()
        total = sm_dp[0]
        for k in range(1, depth):
            total = total + sm_dp[k]
        out_small[...] = total

        @pl.when(~first_section)
        def _():
            head_copy().start()

    def small_head():
        @pl.when(first_section)
        def _():
            head_copy().wait_recv()
            out_small[pl.ds(HEAD_ROW, 1), :] = sm_sec[pl.ds(HEAD_ROW, 1), :]

        @pl.when(~first_section)
        def _():
            head_copy().wait_send()

    def make_inner():
        @pl.loop(0, 4)
        def _(k):
            make_up(k)

    def make_outer():
        make_attn()

        @pl.loop(0, 3)
        def _(k):
            make_qkv(k)

        pltpu.make_async_copy(high, out_gin, io_sem.at[2]).start()

    beside = (
        ("down", make_down, False),
        ("act", act_back, True),
        ("inner", inner_norm, True),
        ("up", make_inner, False),
        ("attend", attend_back, True),
        ("hidden", hidden_step, True),
        ("qkv", make_outer, False),
    )
    lent_parts = (
        lent_start, functools.partial(lent_line, first_line), functools.partial(lent_line, last_lines), lent_done
    )
    smalls = (small_sib, small_grp, small_dp, small_sec, small_head)

    for p in range(last):
        half_down(p)

    @pl.when(first_section)
    def _():
        grad_copy(last).wait_recv()
        outer_norm(last)

    @pl.loop(0, STEPS)
    def _(i):
        for name, part, inside in beside:
            if inside:
                pl.when(first_section & (i == BESIDE[name]))(functools.partial(part, last))
            else:
                pl.when(i == BESIDE[name])(part)
        for step, part in zip(SMALL_STEPS, smalls):
            pl.when(i == step)(part)
        for step, part in zip(LENT_STEPS, lent_parts):
            pl.when(~first_section & (i == step))(part)
        pl.when(first_section & (i == LENT_BACK))(lent_back)
        for name, at in SLOTS:
            chunks, parts = (X_FIRST, x_stages) if name[0] == "x" else (Z_FIRST, z_stages)
            q = jnp.int32(-1)
            for k, step in enumerate(at):
                q = jnp.where(i == step, k, q)

            runs = q >= 0
            if name[0] == "x" and name[1] != "0":
                runs = runs & ~(first_section & (q == LENT))

            @pl.when(runs)
            def _(q=q, chunks=chunks, part=parts[int(name[1])]):
                part(q, pick(q, chunks))

    count = 1 + (groups - 1) + (depth - 1)
    sent = high.at[pl.ds(0, count * SMALL), :]
    rcopy(sent, sent, sm_send.at[0], sm_recv.at[0], other).wait_send()

    @pl.when(~first_section)
    def _():
        for p in range(pairs):
            grad_copy(p).wait_send()

    pltpu.make_async_copy(high, out_gin, io_sem.at[2]).wait()
    pltpu.make_async_copy(fin, fin, io_sem.at[3]).wait()
    rcopy(s1, s1, r_send.at[0], r_sib.at[0], sibling).wait_send()
    for is_here, chunks in ((first_section, len(X_FIRST) - 1), (~first_section, len(X_FIRST))):

        @pl.when(is_here)
        def _(chunks=chunks):
            part = xr.at[pl.ds(0, chunks)]
            rcopy(part, part, r_send.at[1], r_x.at[0], across).wait_send()
            part = zr.at[pl.ds(0, chunks)]
            rcopy(part, part, r_send.at[2], r_z.at[0, 0], across).wait_send()
            part = fin.at[pl.ds(0, chunks), 0]
            rcopy(part, part, r_send.at[4], r_fin.at[0], across).wait_send()
            if groups > 2:
                part = peers.at[pl.ds(0, chunks), pl.ds(0, groups // 2 - 1)]
                rcopy(part, part, r_send.at[5], r_peer.at[0, 0], across).wait_send()

    rcopy(zw, zw, r_send.at[3], r_z.at[0, 0], across).wait_send()

    @pl.when(first_section)
    def _():
        rcopy(s1.at[0], s1.at[0], k_send.at[0], k_in.at[0], other).wait_send()

    @pl.when(~first_section)
    def _():
        rcopy(rz, rz, k_send.at[1], k_z.at[0], across).wait_send()
        part = rg.at[pl.ds(0, groups - 1)]
        rcopy(part, part, k_send.at[2], k_g.at[0], across).wait_send()
        rcopy(fin.at[0], fin.at[0], k_send.at[3], k_out.at[0], other).wait_send()

    part = xw.at[:, pl.ds(0, groups - 1)]
    rcopy(part, part, r_send.at[6], r_grp.at[0, 0], across).wait_send()


def on_device(groups, depth, embedded, lengths, token_grads, score_grads, w_qkv, w_attn_out, w_up, w_down, biases, gains, head_weight):
    micro, _, seq, _ = embedded.shape
    tokens = micro * seq
    rs = w_qkv.shape[1]
    vmem = pl.BlockSpec(memory_space=pltpu.VMEM)
    smem = pl.BlockSpec(memory_space=pltpu.SMEM)
    hbm = pl.BlockSpec(memory_space=pl.ANY)
    teams = max(groups // 2, 1)
    stages = depth.bit_length() - 1
    out_shape = (
        jax.ShapeDtypeStruct((tokens, D), BF),
        jax.ShapeDtypeStruct((tokens, D), F32),
        jax.ShapeDtypeStruct((rs, 3 * D), BF),
        jax.ShapeDtypeStruct((rs, D), BF),
        jax.ShapeDtypeStruct((rs, FF), BF),
        jax.ShapeDtypeStruct((4 * rs, D), BF),
        jax.ShapeDtypeStruct((SMALL, D), F32),
    )
    nx, nz = len(X_FIRST), len(Z_FIRST)
    scratch = [
        pltpu.VMEM((CHUNKS * D + FF, D), BF),
        pltpu.VMEM((CHUNKS, depth, rs, D), BF),
        pltpu.VMEM((nx, depth, rs, HALF), BF),
        pltpu.VMEM((nx, max(depth - 1, 1), rs, HALF), BF),
        pltpu.VMEM((nz, max(depth - 1, 1), rs, D), BF),
        pltpu.VMEM((nz, groups, rs, D), BF),
        pltpu.VMEM((CHUNKS, 2, rs, HALF), BF),
        pltpu.VMEM((nx, teams, rs, HALF) if groups > 2 else (1, 1, 16, 128), BF),
        pltpu.VMEM((max(depth - 1, 1), rs, D), BF),
        pltpu.VMEM((groups, rs, D), BF),
        pltpu.VMEM((tokens, D), BF),
        pltpu.VMEM((tokens, 3 * D), BF),
        pltpu.VMEM((micro * HEADS, seq, seq), BF),
        pltpu.VMEM((tokens, D), BF),
        pltpu.VMEM((tokens, D), BF),
        pltpu.VMEM((tokens, 1), F32),
        pltpu.VMEM((tokens, D), BF),
        pltpu.VMEM((tokens, FF), BF),
        pltpu.VMEM((tokens, FF), BF),
        pltpu.VMEM((tokens, D), BF),
        pltpu.VMEM((tokens, 1), F32),
        pltpu.VMEM((tokens, D), BF),
        pltpu.VMEM((tokens, D), BF),
        pltpu.VMEM((tokens, D), F32),
        pltpu.VMEM((tokens, D), BF),
        pltpu.VMEM((tokens, 3 * D), BF),
        pltpu.VMEM((SMALL, D), F32),
        pltpu.VMEM((SMALL, D), F32),
        pltpu.VMEM((groups, SMALL, D), F32),
        pltpu.VMEM((depth, SMALL, D), F32),
        pltpu.VMEM((SMALL, D), F32),
        pltpu.VMEM(biases.shape, F32),
        pltpu.VMEM(gains.shape[1:], F32),
        pltpu.VMEM(head_weight.shape, F32),
        pltpu.SemaphoreType.DMA((5,)),
        pltpu.SemaphoreType.DMA((4,)),
        pltpu.SemaphoreType.DMA((CHUNKS, depth)),
        pltpu.SemaphoreType.DMA((CHUNKS, depth)),
        pltpu.SemaphoreType.DMA((CHUNKS,)),
        pltpu.SemaphoreType.DMA((3,)),
        pltpu.SemaphoreType.DMA((RELAY,)),
        pltpu.SemaphoreType.DMA((RELAY, depth)),
        pltpu.SemaphoreType.DMA((RELAY, depth)),
        pltpu.SemaphoreType.DMA((RELAY,)),
        pltpu.SemaphoreType.DMA((4,)),
        pltpu.SemaphoreType.DMA((1,)),
        pltpu.SemaphoreType.DMA((max(stages, 1),)),
        pltpu.SemaphoreType.DMA((groups,)),
        pltpu.SemaphoreType.DMA((1,)),
        pltpu.SemaphoreType.DMA((4,)),
        pltpu.SemaphoreType.DMA((4,)),
        pltpu.SemaphoreType.DMA((4,)),
        pltpu.SemaphoreType.DMA((7,)),
        pltpu.SemaphoreType.DMA((CHUNKS,)),
        pltpu.SemaphoreType.DMA((CHUNKS,)),
        pltpu.SemaphoreType.DMA((CHUNKS, max(stages, 1))),
        pltpu.SemaphoreType.DMA((nz, groups)),
        pltpu.SemaphoreType.DMA((CHUNKS,)),
        pltpu.SemaphoreType.DMA((CHUNKS, teams)),
        pltpu.SemaphoreType.DMA((2,)),
        pltpu.SemaphoreType.DMA((2 + groups + depth,)),
    ]
    state, grad_in, *grads, small = pl.pallas_call(
        functools.partial(kernel, (groups, depth, rs, seq)),
        out_shape=out_shape,
        in_specs=[hbm] * 9 + [smem] * 2,
        out_specs=(hbm,) * 6 + (vmem,),
        scratch_shapes=scratch,
        compiler_params=pltpu.CompilerParams(
            collective_id=0, has_side_effects=True, vmem_limit_bytes=65300 * 1024
        ),
    )(
        embedded.reshape(tokens, D),
        token_grads.reshape(tokens, D),
        w_qkv[0],
        w_attn_out[0],
        w_up[0],
        w_down[0],
        biases,
        gains[0],
        head_weight,
        lengths.reshape(micro),
        score_grads.reshape(micro),
    )
    results = pl.pallas_call(
        hand_out,
        out_shape=[jax.ShapeDtypeStruct(x.shape, x.dtype) for x in (state, grad_in)]
        + [jax.ShapeDtypeStruct(x.shape, F32) for x in grads]
        + [jax.ShapeDtypeStruct(x, F32) for x in ((1, 10 * D), (2, D), (D,))],
        in_specs=[vmem] * 7,
        out_specs=[vmem] * 9,
    )(state, grad_in, *grads, small)
    state, grad_in, g_qkv, g_attn, g_up, g_down, g_bias, g_gain, g_head = results
    return (
        state.reshape(1, micro, 1, seq, D),
        grad_in.reshape(1, micro, 1, seq, D),
        g_qkv[None],
        g_attn[None],
        g_up[None],
        g_down[None],
        g_bias,
        g_gain[None],
        g_head,
    )


def hand_out(state, grad_in, gq, go, gu, gd, small, o_state, o_gin, o_q, o_o, o_u, o_d, o_bias, o_gain, o_head):
    for src, dst in ((state, o_state), (grad_in, o_gin), (gq, o_q), (go, o_o), (gu, o_u), (gd, o_d)):
        dst[...] = src[...].astype(dst.dtype)
    for k in range(10):
        o_bias[:, pl.ds(k * D, D)] = small[pl.ds(k, 1), :]
    o_gain[...] = small[pl.ds(GAIN1, 2), :]
    o_head[...] = small[HEAD_ROW, :]


def solution(mesh):
    return jax.shard_map(
        functools.partial(on_device, mesh.shape["grp"], mesh.shape["dp"] // 2),
        mesh=mesh,
        in_specs=(
            P(None, ("grp", "dp"), None, None),
            P(None, ("grp", "dp")),
            P(None, ("grp", "dp"), None, None),
            P(None, ("grp", "dp")),
            P("section", "dp", None),
            P("section", "dp", None),
            P("section", "dp", None),
            P("section", "dp", None),
            P("section", None),
            P("section", None, None),
            P(),
        ),
        out_specs=(
            P("section", None, ("grp", "dp"), None, None),
            P("section", None, ("grp", "dp"), None, None),
            P("section", "dp", None),
            P("section", "dp", None),
            P("section", "dp", None),
            P("section", "dp", None),
            P("section", None),
            P("section", None, None),
            P(),
        ),
        check_vma=False,
    )
```

```python
import functools
import math

import jax
import jax.numpy as jnp
from jax import lax
from jax.experimental import pallas as pl
from jax.experimental.pallas import tpu as pltpu
from jax.sharding import PartitionSpec as P

D = 768
FF = 3072
HEADS = 12
HEAD = 64
EPSILON = 1e-06
CHUNKS = 12
HALF = D // 2
DOWN = 8 * D
DOWN_GRAD = 12 * D
SCALE = 1.0 / math.sqrt(HEAD)
F32 = jnp.float32
BF = jnp.bfloat16
MESH = pl.DeviceIdType.MESH
BQ, BV, BO, BU, BD, BETA1, BETA2, GAIN1, GAIN2, HEAD_ROW = 0, 1, 2, 3, 7, 8, 9, 10, 11, 12
SMALL = 16
RELAY = 1
TAKE = (8,)
X_FIRST = (8, 4, 5, 6, 7, 3, 0, 1, 2)
Z_FIRST = (9, 10, 11)
SLOTS = (
    ("x0", (0, 2, 1, 4, 3, 6, 5, 7, 9)),
    ("z0", (0, 3, 2)),
    ("z3", (14, 15, 17)),
    ("x4", (8, 12, 9, 13, 11, 14, 15, 16, 17)),
    ("x3", (6, 9, 7, 11, 8, 12, 13, 14, 15)),
    ("z2", (4, 11, 13)),
    ("x2", (3, 6, 4, 8, 7, 9, 11, 12, 13)),
    ("z1", (2, 5, 7)),
    ("x1", (1, 3, 2, 5, 4, 7, 8, 10, 11)),
)
BESIDE = {"down": 0, "act": 1, "inner": 1, "up": 1, "attend": 3, "hidden": 4, "qkv": 5}
UP_ORDER = (1, 0, 3, 2)
SMALL_STEPS = (4, 5, 6, 8, 10)
LENT = 4
LENT_STEPS = (7, 9, 11, 13)
LENT_BACK = 17
STEPS = 1 + max(LENT_BACK, max(max(steps) for _, steps in SLOTS))


def dot(a, b):
    return lax.dot_general(a, b, (((1,), (0,)), ((), ())), preferred_element_type=F32)


def dot_t(a, b):
    return lax.dot_general(a, b, (((1,), (1,)), ((), ())), preferred_element_type=F32)


def dot_c(a, b):
    return lax.dot_general(a, b, (((0,), (0,)), ((), ())), preferred_element_type=F32)


def span(i, width):
    return pl.ds(pl.multiple_of(i * width, width), width)


def flip(index, mask):
    bit = 1
    while bit <= mask:
        if mask & bit:
            index = index + bit - 2 * bit * ((index // bit) % 2)
        bit *= 2
    return index


def masks(bits):
    found = [0]
    for bit in bits:
        found = found + [mask ^ bit for mask in found]
    return found


def pick(i, values):
    found = values[-1]
    for k in range(len(values) - 2, -1, -1):
        found = jnp.where(i == k, values[k], found)
    return found


def row_sum(x):
    return jnp.sum(x, 0, keepdims=True)


def gelu_parts(x):
    t = 1.0 / (1.0 + (0.3275911 * math.sqrt(0.5)) * jnp.abs(x))
    e = jnp.exp2((-0.5 * math.log2(math.e)) * (x * x))
    tail = t * (0.127414796 + t * (-0.142248368 + t * (0.7107068705 + t * (-0.7265760135 + t * 0.5307027145)))) * e
    phi = jnp.where(x >= 0, 1.0 - tail, tail)
    return x * phi, phi + x * (e * (1.0 / math.sqrt(2.0 * math.pi)))


def normed(x):
    centred = x - jnp.mean(x, -1, keepdims=True)
    scale = lax.rsqrt(jnp.mean(centred * centred, -1, keepdims=True) + EPSILON)
    return centred * scale, scale


def norm_back(grad, n, scale, gain):
    gg = gain * grad
    return (gg - jnp.mean(gg, -1, keepdims=True) - n * jnp.mean(gg * n, -1, keepdims=True)) * scale


def kernel(sizes, *refs):
    groups, depth, rs, seq = sizes
    (emb, token_grads, wq_in, wo_in, wu_in, wd_in, bias_in, gains_in, head_in, lens, scores,
     out_sec, out_gin, out_q, out_o, out_u, out_d, out_small,
     big, s1, xr, zr, zw, xw, fin, peers, rz, rg,
     hbuf, qkv, probs, mixed, n1, r1, first_low, act, gp, n2, r2, outb, gbuf, high, dd, dqkv,
     small, sm_sib, sm_grp, sm_dp, sm_sec,
     bias, gains, head_w, local_sem, io_sem, g_zr, g_xr, g_sr, g_send, b_own, b_zr, b_xr, b_back, b_send, k_in, k_z, k_g, k_out, k_send, y_send, y_recv,
     r_send, r_sib, r_x, r_z, r_grp, r_fin, r_peer, sm_send, sm_recv) = refs
    stages = depth.bit_length() - 1
    da, dm = n1, n2
    pairs = 2
    sec = lax.axis_index("section")
    g = lax.axis_index("grp")
    d = lax.axis_index("dp")
    z, c = d // 2, d % 2
    par = g % 2
    first_section = sec == 0

    def dev(sec_=None, g_=None, z_=None, c_=None):
        return (
            sec if sec_ is None else sec_,
            g if g_ is None else g_,
            (z if z_ is None else z_) * 2 + (c if c_ is None else c_),
        )

    sibling = dev(c_=1 - c)
    across = dev(g_=g + 1 - 2 * par)
    other = dev(sec_=1 - sec)

    def rcopy(src, dst, send, recv, to):
        return pltpu.make_async_remote_copy(
            src_ref=src, dst_ref=dst, send_sem=send, recv_sem=recv, device_id=to, device_id_type=MESH
        )

    def shard_row(m, owner, down=DOWN):
        row = jnp.where(m < 8, m * D + owner * rs, down + owner * (4 * rs) + (m - 8) * rs)
        return pl.multiple_of(row, 16)

    barrier = pltpu.get_barrier_semaphore()
    greeted = 0
    for to in [sibling, other]:
        pl.semaphore_signal(barrier, inc=1, device_id=to, device_id_type=MESH)
        greeted += 1
    for k in range(1, groups):
        pl.semaphore_signal(barrier, inc=1, device_id=dev(g_=(g + k) % groups), device_id_type=MESH)
        greeted += 1
    for k in range(1, depth):
        pl.semaphore_signal(barrier, inc=1, device_id=dev(z_=(z + k) % depth), device_id_type=MESH)
        greeted += 1

    own = []
    for k in range(3):
        own.append((wq_in.at[:, pl.ds(k * D, D)], k))
    own.append((wo_in, 3))
    for k in range(4):
        own.append((wu_in.at[:, pl.ds(k * D, D)], 4 + k))
    for src, k in own:
        pltpu.make_async_copy(src, big.at[pl.ds(pl.multiple_of(k * D + d * rs, 16), rs), :], local_sem.at[0]).start()
    pltpu.make_async_copy(
        wd_in, big.at[pl.ds(pl.multiple_of(DOWN + d * 4 * rs, 16), 4 * rs), :], local_sem.at[0]
    ).start()

    vectors = [
        pltpu.make_async_copy(src, dst, local_sem.at[2 + k])
        for k, (src, dst) in enumerate(((bias_in, bias), (gains_in, gains), (head_in, head_w)))
    ]
    for copy in vectors:
        copy.start()

    def have_vectors():
        for copy in vectors:
            copy.wait()

    @pl.when(first_section)
    def _():
        pltpu.make_async_copy(emb, hbuf, local_sem.at[1]).start()

    @pl.when(~first_section)
    def _():
        pltpu.make_async_copy(token_grads, gbuf, local_sem.at[1]).start()

    small[...] = jnp.zeros_like(small)
    pl.semaphore_wait(barrier, greeted)
    pltpu.make_async_copy(
        big.at[pl.ds(0, CHUNKS * rs), :], big.at[pl.ds(0, CHUNKS * rs), :], local_sem.at[0]
    ).wait()

    def region(m, zz, half=None, cc=c):
        cols = slice(None) if half is None else span(half, HALF)
        return big.at[pl.ds(shard_row(m, 2 * zz + cc), rs), cols]

    far = [depth >> (t + 1) for t in range(stages)]
    held = [masks(far[:t]) for t in range(stages + 1)]

    def along(m, zz, t):
        part = region(m, zz, par)
        return rcopy(part, part, g_send.at[0], g_zr.at[m, zz], dev(z_=flip(z, far[t])))

    def over(m, zz, half):
        part = region(m, zz, half)
        return rcopy(part, part, g_send.at[1], g_xr.at[m, zz], across)

    def beside(m, zz, half):
        part = region(m, zz, half)
        return rcopy(part, part, g_send.at[2], g_sr.at[m], sibling)

    def relayed(b, zz, half):
        return dd.at[pl.ds(pl.multiple_of((b * depth + zz) * rs, 16), rs), span(half, HALF)]

    def lend(b):
        return rcopy(
            region(CHUNKS - RELAY + b, z, par), relayed(b, z, par), b_send.at[0], b_own.at[b], other
        )

    def relay_along(b, zz, t):
        part = relayed(b, zz, par)
        return rcopy(part, part, b_send.at[1], b_zr.at[b, zz], dev(z_=flip(z, far[t])))

    def relay_over(b, zz, half):
        part = relayed(b, zz, half)
        return rcopy(part, part, b_send.at[2], b_xr.at[b, zz], across)

    def give_back(b, zz, half):
        return rcopy(
            relayed(b, zz, half), region(CHUNKS - RELAY + b, zz, half), b_send.at[3], b_back.at[b], other
        )

    def relay_own(b):
        lend(b).wait_recv()
        relay_along(b, z, 0).start()

    def relay_arrived(t, b):
        for mask in held[t]:
            zz = flip(z, far[t] ^ mask)
            relay_along(b, zz, t).wait_recv()
            relay_over(b, zz, par).start()
            give_back(b, zz, par).start()
        if t + 1 < stages:
            for mask in held[t + 1]:
                relay_along(b, flip(z, mask), t + 1).start()

    def relay_crossed(t, b):
        for mask in held[t]:
            zz = flip(z, far[t] ^ mask)
            relay_over(b, zz, 1 - par).wait_recv()
            give_back(b, zz, 1 - par).start()

    def take(b):
        got = big.at[pl.ds(0, (depth - 1) * rs), :]
        rcopy(got, got, b_send.at[3], b_back.at[b], other).wait_recv()
        for k in range(1, depth):
            beside(CHUNKS - RELAY + b, (z + k) % depth, None).start()

    def bias_row(start, width=D):
        return bias[:, pl.ds(start, width)]

    low = lax.broadcasted_iota(jnp.int32, (1, 128), 1) < HEAD
    key = lax.broadcasted_iota(jnp.int32, (1, seq), 1)

    def pair_rows(p):
        return span(p, seq)

    def block(k):
        return big[pl.ds(k * D, D), :]

    def project(p, k):
        r = pair_rows(p)
        x = dot(hbuf[r, :], block(k))
        if k != 1:
            x = x + bias_row(0 if k == 0 else D)
        qkv[r, pl.ds(k * D, D)] = x.astype(BF)

    def both_heads(x):
        none = jnp.zeros_like(x)
        return jnp.concatenate([jnp.where(low, x, none), jnp.where(low, none, x)], 0)

    def ahead(make):
        coming = make(0)
        for j in range(HEADS // 2):
            now, coming = coming, make(j + 1) if j + 1 < HEADS // 2 else None
            yield j, now

    def attend(p):
        r = pair_rows(p)
        ok = key < lens[p]

        def scores_of(j):
            q2 = qkv[r, pl.ds(j * 128, 128)] * jnp.asarray(SCALE, BF)
            return dot_t(both_heads(q2), qkv[r, pl.ds((j + 6) * 128, 128)])

        for j, sc in ahead(scores_of):
            sc = jnp.where(ok, sc, -1e30)
            e = jnp.exp(sc - jnp.max(sc, -1, keepdims=True))
            pr = (e * (1.0 / jnp.sum(e, -1, keepdims=True))).astype(BF)
            probs[p * HEADS + 2 * j] = pr[:seq]
            probs[p * HEADS + 2 * j + 1] = pr[seq:]
            o = dot(pr, qkv[r, pl.ds((j + 12) * 128, 128)])
            mixed[r, pl.ds(j * 128, 128)] = jnp.where(low, o[:seq], o[seq:]).astype(BF)

    def join(p):
        r = pair_rows(p)
        n, scale = normed(hbuf[r, :].astype(F32) + dot(mixed[r, :], block(3)) + bias_row(2 * D))
        n1[r, :] = n.astype(BF)
        r1[r, :] = scale
        y = n * gains[0:1, :] + bias_row(4 * D + FF)
        high[r, :] = y
        first_low[r, :] = y.astype(BF)

    def widen(p, k):
        r = pair_rows(p)
        for t in range(3):
            w = big[pl.ds((4 + k) * D, D), pl.ds(t * 256, 256)]
            col = k * D + t * 256
            a, dg = gelu_parts(dot(first_low[r, :], w) + bias_row(3 * D + col, 256))
            act[r, pl.ds(col, 256)] = a.astype(BF)
            gp[r, pl.ds(col, 256)] = dg.astype(BF)

    def narrow(p):
        r = pair_rows(p)
        n, scale = normed(high[r, :] + dot(act[r, :], big[pl.ds(DOWN, FF), :]) + bias_row(3 * D + FF))
        n2[r, :] = n.astype(BF)
        r2[r, :] = scale
        y = n * gains[1:2, :] + bias_row(5 * D + FF)
        outb[r, :] = y.astype(BF)

        @pl.when(~first_section)
        def _():
            small[pl.ds(HEAD_ROW, 1), :] += scores[p] * y[0:1]

    def state_copy(p):
        r = pair_rows(p)
        return rcopy(outb.at[r, :], hbuf.at[r, :], y_send.at[p], y_recv.at[p], other)

    def out_copy(p):
        r = pair_rows(p)
        return pltpu.make_async_copy(outb.at[r, :], out_sec.at[r, :], io_sem.at[p])

    def chunk_ready(m):
        whole = big.at[pl.ds(0, depth * rs), :]
        rcopy(whole, whole, g_send.at[2], g_sr.at[m], sibling).wait_recv()

    def own_step(n):
        if stages:
            along(n, z, 0).start()
        beside(n, z, None).start()

    def arrived(m, t):
        for mask in held[t]:
            zz = flip(z, far[t] ^ mask)
            along(m, zz, t).wait_recv()
            over(m, zz, par).start()
            beside(m, zz, par).start()
        if t + 1 < stages:
            for mask in held[t + 1]:
                along(m, flip(z, mask), t + 1).start()

    def crossed(m, t):
        for mask in held[t]:
            zz = flip(z, far[t] ^ mask)
            over(m, zz, 1 - par).wait_recv()
            beside(m, zz, 1 - par).start()

    def early(step, pieces):
        def run(n):
            @pl.when(first_section & (n == stages + 2 + step))
            def _():
                pieces()

        return run

    def both_pairs(piece):
        @pl.loop(0, pairs)
        def _(p):
            piece(p)

    def early_project(k):
        if k == 0:
            pltpu.make_async_copy(emb, hbuf, local_sem.at[1]).wait()
            have_vectors()
        chunk_ready(k)
        both_pairs(lambda p: project(p, k))

    def early_join():
        chunk_ready(3)
        both_pairs(join)

    def early_widen(k):
        chunk_ready(4 + k)
        both_pairs(lambda p: widen(p, k))

    plan = [early(k, functools.partial(early_project, k)) for k in range(3)]
    plan.append(early(2, lambda: attend(0)))
    plan.append(early(3, lambda: attend(1)))
    plan.append(early(4, early_join))
    plan += [early(4 + k, functools.partial(early_widen, k)) for k in range(4)]

    mine = jnp.where(first_section, CHUNKS - RELAY, CHUNKS)

    @pl.loop(0, mine + stages + 1)
    def _(n):
        pl.when(n < mine)(functools.partial(own_step, n))

        @pl.when(first_section & (n < RELAY))
        def _():
            lend(n).start()
            beside(CHUNKS - RELAY + n, z, None).start()

        relay_stages = [relay_own]
        for t in range(stages):
            relay_stages.append(functools.partial(relay_arrived, t))
        for lag, stage in enumerate(relay_stages):
            b = n - 1 - lag
            pl.when(~first_section & (b >= 0) & (b < RELAY))(functools.partial(stage, b))
        for t in range(stages):
            b = n - 3 - t
            pl.when(~first_section & (b >= 0) & (b < RELAY))(functools.partial(relay_crossed, t, b))
        for t in range(stages):
            m = n - t - 1
            pl.when((m >= 0) & (m < mine))(functools.partial(arrived, m, t))
        for t in range(stages):
            m = n - t - 2
            pl.when((m >= 0) & (m < mine))(functools.partial(crossed, m, t))
        for b in range(RELAY):
            pl.when(first_section & (n == TAKE[b]))(functools.partial(take, b))
        for run in plan:
            run(n)

    @pl.loop(jnp.where(first_section, 8, 0), CHUNKS)
    def _(m):
        chunk_ready(m)

    @pl.when(first_section)
    def _():
        @pl.loop(0, pairs)
        def _(p):
            narrow(p)
            state_copy(p).start()
            out_copy(p).start()

    @pl.when(~first_section)
    def _():
        pltpu.make_async_copy(token_grads, gbuf, local_sem.at[1]).wait()
        have_vectors()

    for is_first, count in ((first_section, CHUNKS - RELAY), (~first_section, CHUNKS)):

        @pl.when(is_first)
        def _(count=count):
            sent = big.at[pl.ds(0, count * (depth - 1) * rs), pl.ds(0, HALF)]
            rcopy(sent, sent, g_send.at[0], g_zr.at[0, 0], across).wait_send()
            rcopy(sent, sent, g_send.at[1], g_xr.at[0, 0], across).wait_send()

    def relay_sent(k, rows, cols):
        sent = big.at[pl.ds(0, rows), pl.ds(0, cols)]
        rcopy(sent, sent, b_send.at[k], b_own.at[0], other).wait_send()

    @pl.when(first_section)
    def _():
        relay_sent(0, RELAY * rs, HALF)

    @pl.when(~first_section)
    def _():
        relay_sent(1, RELAY * (depth - 1) * rs, HALF)
        relay_sent(2, RELAY * (depth - 1) * rs, HALF)
        relay_sent(3, RELAY * (depth - 1) * rs, D)

    sent = big.at[pl.ds(0, CHUNKS * depth * rs), :]
    rcopy(sent, sent, g_send.at[2], g_sr.at[0], sibling).wait_send()

    def add_small(row, x):
        small[pl.ds(row, 1), :] += row_sum(x)

    def outer_norm(p):
        r = pair_rows(p)
        length = jnp.where(first_section, seq, lens[p])
        score = jnp.where(first_section, 0.0, scores[p])
        place = lax.broadcasted_iota(jnp.int32, (seq, 1), 0)
        grad = jnp.where(place < length, gbuf[r, :].astype(F32), 0.0)
        grad = grad + jnp.where(place == 0, score * head_w[...].reshape(1, D), 0.0)
        n = n2[r, :].astype(F32)
        x = norm_back(grad, n, r2[r, :], gains[1:2, :])
        xl = x.astype(BF)
        high[r, :] = x
        dd[r, :] = xl
        add_small(BD, xl.astype(F32))
        add_small(BETA2, grad)
        add_small(GAIN2, grad * n)

    def act_back(p):
        r = pair_rows(p)
        for k in range(4):
            c4 = pl.ds(k * D, D)
            x = (dot_t(dd[r, :], big[pl.ds(DOWN + k * D, D), :]) * gp[r, c4].astype(F32)).astype(BF)
            gp[r, c4] = x
            add_small(BU + k, x.astype(F32))

    def inner_norm(p):
        r = pair_rows(p)
        grad = high[r, :]
        for k in range(4):
            grad = grad + dot_t(gp[r, pl.ds(k * D, D)], block(4 + k))
        n = n1[r, :].astype(F32)
        x = norm_back(grad, n, r1[r, :], gains[0:1, :])
        xl = x.astype(BF)
        high[r, :] = x
        da[r, :] = xl
        add_small(BO, xl.astype(F32))
        add_small(BETA1, grad)
        add_small(GAIN1, grad * n)
        dm[r, :] = dot_t(xl, block(3)).astype(BF)

    def attend_back(p):
        r = pair_rows(p)

        def dprobs_of(j):
            return dot_t(both_heads(dm[r, pl.ds(j * 128, 128)]), qkv[r, pl.ds((j + 12) * 128, 128)])

        for j, dp in ahead(dprobs_of):
            q2 = qkv[r, pl.ds(j * 128, 128)]
            k2 = qkv[r, pl.ds((j + 6) * 128, 128)]
            pr = jnp.concatenate([probs[p * HEADS + 2 * j], probs[p * HEADS + 2 * j + 1]], 0)
            pf = pr.astype(F32)
            t = pf * dp
            ds = (t - pf * jnp.sum(t, -1, keepdims=True)).astype(BF)
            dq = dot(ds, k2)
            dq = (jnp.where(low, dq[:seq], dq[seq:]) * SCALE).astype(BF)
            qt, dt = q2.T, dm[r, pl.ds(j * 128, 128)].T
            dk = jnp.concatenate([dot(qt[:HEAD], ds[:seq]), dot(qt[HEAD:], ds[seq:])], 0)
            dv = jnp.concatenate([dot(dt[:HEAD], pr[:seq]), dot(dt[HEAD:], pr[seq:])], 0)
            dk = (dk * SCALE).astype(BF).T
            dv = dv.astype(BF).T
            dqkv[r, pl.ds(j * 128, 128)] = dq
            dqkv[r, pl.ds((j + 6) * 128, 128)] = dk
            dqkv[r, pl.ds((j + 12) * 128, 128)] = dv
            small[pl.ds(BQ, 1), pl.ds(j * 128, 128)] += row_sum(dq.astype(F32))
            small[pl.ds(BV, 1), pl.ds(j * 128, 128)] += row_sum(dv.astype(F32))

    def hidden_back(p):
        r = pair_rows(p)
        grad = high[r, :]
        for k in range(3):
            grad = grad + dot_t(dqkv[r, pl.ds(k * D, D)], block(k))
        high[r, :] = grad
        outb[r, :] = grad.astype(BF)

    def grad_copy(p):
        r = pair_rows(p)
        return rcopy(outb.at[r, :], gbuf.at[r, :], y_send.at[2 + p], y_recv.at[2 + p], other)

    def weight_grad(left, lcol, right, rcol, row):
        a = left[:, pl.ds(pl.multiple_of(lcol, 256), D)]
        b = right[:, pl.ds(pl.multiple_of(rcol, 256), D)]
        big[pl.ds(pl.multiple_of(row, 256), D), :] = dot_c(a, b).astype(BF)

    def sib_copy(m, zz):
        return rcopy(
            big.at[pl.ds(shard_row(m, 2 * zz + 1 - c, DOWN_GRAD), rs), :],
            s1.at[m, zz], r_send.at[0], r_sib.at[m], sibling,
        )

    def sib_send(m):
        @pl.loop(0, depth)
        def _(zz):
            sib_copy(m, zz).start()

    def half_down(p):
        r = pair_rows(p)

        @pl.loop(0, 4)
        def _(k):
            x = dot_c(act[r, span(k, D)], dd[r, :])
            place = pl.ds(pl.multiple_of(DOWN_GRAD + k * D, 256), D)
            if p > 0:
                x = x + big[place, :].astype(F32)
            big[place, :] = x.astype(BF)

    def make_down():
        half_down(last)

        @pl.loop(8, 12)
        def _(m):
            sib_send(m)

    def make_up(k):
        weight_grad(first_low, 0, gp, k * D, (4 + k) * D)
        sib_send(4 + k)

    def make_attn():
        weight_grad(mixed, 0, da, 0, 3 * D)
        sib_send(3)

    def make_qkv(k):
        weight_grad(hbuf, 0, dqkv, k * D, k * D)
        sib_send(k)

    def pair_sums(m):
        rcopy(s1.at[m], s1.at[m], r_send.at[0], r_sib.at[m], sibling).wait_recv()

        @pl.loop(0, depth)
        def _(zz):
            mine = big[pl.ds(shard_row(m, 2 * zz + c, DOWN_GRAD), rs), :]
            s1[m, zz] = (mine.astype(F32) + s1[m, zz].astype(F32)).astype(BF)

    sides = [masks([2 << k for k in range(t, stages - 1)]) for t in range(stages)]
    slots = [sum(len(side) for side in sides[:t]) for t in range(stages)]

    def line_send(part, landing, m, t, send):
        for k, mask in enumerate(sides[t]):
            rcopy(
                part.at[flip(z, (1 << t) ^ mask)], landing.at[slots[t] + k], send, r_z.at[m, t],
                dev(z_=flip(z, 1 << t)),
            ).start()

    def line_add(part, landing, m, t, send):
        here = landing.at[pl.ds(slots[t], len(sides[t]))]
        rcopy(here, here, send, r_z.at[m, t], dev(z_=flip(z, 1 << t))).wait_recv()
        for k, mask in enumerate(sides[t]):
            zz = flip(z, mask)
            part[zz] = (part[zz].astype(F32) + landing[slots[t] + k].astype(F32)).astype(BF)

    def put_out(m):
        def put(to, row, col):
            for h in range(2):
                rows = pl.ds(pl.multiple_of(row, 16), rs)
                cols = pl.ds(pl.multiple_of(col + h * HALF, 128), HALF)
                pltpu.make_async_copy(fin.at[m, h], to.at[rows, cols], io_sem.at[3]).start()

        pl.when(m >= 8)(lambda: put(out_d, (m - 8) * rs, 0))
        pl.when((m >= 4) & (m < 8))(lambda: put(out_u, 0, (m - 4) * D))
        pl.when(m == 3)(lambda: put(out_o, 0, 0))
        pl.when(m < 3)(lambda: put(out_q, 0, m * D))

    def x_copy(q, m):
        return rcopy(
            s1.at[m, :, :, span(1 - par, HALF)], xr.at[q], r_send.at[1], r_x.at[m], across
        )

    def fin_copy(m):
        return rcopy(fin.at[m, par], fin.at[m, par], r_send.at[4], r_fin.at[m], across)

    lent = X_FIRST[LENT]

    def lent_shard(zz):
        return qkv.at[pl.ds(pl.multiple_of(zz * rs, 16), rs), pl.ds(0, D)]

    def lend_sums():
        for zz in range(depth):
            rcopy(s1.at[lent, zz], lent_shard(zz), k_send.at[0], k_in.at[0], other).start()

    def lent_send(t):
        for k, mask in enumerate(sides[t]):
            rcopy(
                lent_shard(flip(z, (1 << t) ^ mask)), rz.at[slots[t] + k], k_send.at[1], k_z.at[t],
                dev(z_=flip(z, 1 << t)),
            ).start()

    def lent_add(t):
        here = rz.at[pl.ds(slots[t], len(sides[t]))]
        rcopy(here, here, k_send.at[1], k_z.at[t], dev(z_=flip(z, 1 << t))).wait_recv()
        for k, mask in enumerate(sides[t]):
            part = lent_shard(flip(z, mask))
            part[...] = (part[...].astype(F32) + rz[slots[t] + k].astype(F32)).astype(BF)

    def lent_start():
        whole = qkv.at[pl.ds(0, depth * rs), pl.ds(0, D)]
        rcopy(whole, whole, k_send.at[0], k_in.at[0], other).wait_recv()
        lent_send(0)

    def lent_line(ts):
        for t in ts:
            lent_add(t)
            if t + 1 < stages:
                lent_send(t + 1)
        if stages - 1 in ts:
            rg[g] = lent_shard(z)[...]
            for k in range(1, groups):
                rcopy(rg.at[g], rg.at[g], k_send.at[2], k_g.at[g], dev(g_=(g + k) % groups)).start()

    def lent_done():
        for k in range(1, groups):
            gg = (g + k) % groups
            rcopy(rg.at[gg], rg.at[gg], k_send.at[2], k_g.at[gg], across).wait_recv()
        total = rg[0].astype(F32)
        for k in range(1, groups):
            total = total + rg[k].astype(F32)
        qkv[pl.ds(0, rs), pl.ds(D, D)] = total.astype(BF)
        for h in range(2):
            rcopy(
                qkv.at[pl.ds(0, rs), pl.ds(D + h * HALF, HALF)], fin.at[lent, h], k_send.at[3], k_out.at[0], other
            ).start()

    def lent_back():
        rcopy(fin.at[lent], fin.at[lent], k_send.at[3], k_out.at[0], other).wait_recv()
        put_out(jnp.int32(lent))

    def x_start(q, m):
        pair_sums(m)
        lends = first_section & (q == LENT)
        pl.when(lends)(lend_sums)
        pl.when(~lends)(lambda: x_copy(q, m).start())

    def x_halves(q, m):
        x_copy(q, m).wait_recv()

        @pl.loop(0, depth)
        def _(zz):
            mine = s1[m, zz, :, span(par, HALF)]
            xr[q, zz] = (mine.astype(F32) + xr[q, zz].astype(F32)).astype(BF)

        line_send(xr.at[q], zr.at[q], m, 0, r_send.at[2])

    def lines(part, landing, m, ts, send):
        for t in ts:
            line_add(part, landing, m, t, send)
            if t + 1 < stages:
                line_send(part, landing, m, t + 1, send)

    def x_line(ts, q, m):
        lines(xr.at[q], zr.at[q], m, ts, r_send.at[2])
        if stages - 1 not in ts:
            return
        total = xr[q, z]
        if groups > 2:
            teams = groups // 2
            team = g // 2
            peers[q, team] = total
            for k in range(1, teams):
                to = dev(g_=((team + k) % teams) * 2 + par)
                rcopy(peers.at[q, team], peers.at[q, team], r_send.at[5], r_peer.at[m, team], to).start()
            for k in range(1, teams):
                tt = (team + k) % teams
                rcopy(peers.at[q, tt], peers.at[q, tt], r_send.at[5], r_peer.at[m, tt], across).wait_recv()
            total = peers[q, 0].astype(F32)
            for k in range(1, teams):
                total = total + peers[q, k].astype(F32)
            total = total.astype(BF)
        fin[m, par] = total
        fin_copy(m).start()

    def x_finish(q, m):
        rcopy(fin.at[m, 1 - par], fin.at[m, 1 - par], r_send.at[4], r_fin.at[m], across).wait_recv()
        put_out(m)

    def z_start(q, m):
        pair_sums(m)
        line_send(s1.at[m], zw.at[q], m, 0, r_send.at[3])

    def z_line(ts, q, m):
        lines(s1.at[m], zw.at[q], m, ts, r_send.at[3])
        if stages - 1 not in ts:
            return
        xw[q, g] = s1[m, z]
        for k in range(1, groups):
            rcopy(xw.at[q, g], xw.at[q, g], r_send.at[6], r_grp.at[q, g], dev(g_=(g + k) % groups)).start()

    def z_finish(q, m):
        for k in range(1, groups):
            gg = (g + k) % groups
            rcopy(xw.at[q, gg], xw.at[q, gg], r_send.at[6], r_grp.at[q, gg], across).wait_recv()
        total = xw[q, 0].astype(F32)
        for k in range(1, groups):
            total = total + xw[q, k].astype(F32)
        total = total.astype(BF)
        fin[m, 0] = total[:, :HALF]
        fin[m, 1] = total[:, HALF:]
        put_out(m)

    first_line, last_lines = range(0, 1), range(1, stages)
    if stages == 1:
        first_line, last_lines = range(0, 0), range(0, 1)
    x_stages = [
        x_start, x_halves, functools.partial(x_line, first_line), functools.partial(x_line, last_lines), x_finish
    ]
    z_stages = [z_start, functools.partial(z_line, first_line), functools.partial(z_line, last_lines), z_finish]

    last = pairs - 1

    def hidden_step(p):
        out_copy(p).wait()

        @pl.when(first_section)
        def _():
            state_copy(p).wait_send()

        hidden_back(p)

    @pl.loop(0, jnp.where(first_section, last, pairs))
    def _(p):
        @pl.when(~first_section)
        def _():
            state_copy(p).wait_recv()
            for k in range(3):
                project(p, k)
            attend(p)
            join(p)
            for k in range(4):
                widen(p, k)
            narrow(p)
            out_copy(p).start()

        @pl.when(first_section)
        def _():
            grad_copy(p).wait_recv()

        outer_norm(p)
        act_back(p)
        inner_norm(p)
        attend_back(p)
        hidden_step(p)

        @pl.when(~first_section)
        def _():
            grad_copy(p).start()

    def sm_copy(src, dst, recv, to):
        return rcopy(src, dst, sm_send.at[0], recv, to)

    def small_sib():
        sm_copy(small, sm_sib, sm_recv.at[0], sibling).start()

    def small_grp():
        sm_copy(small, sm_sib, sm_recv.at[0], sibling).wait_recv()
        sm_grp[g] = small[...] + sm_sib[...]
        for k in range(1, groups):
            sm_copy(sm_grp.at[g], sm_grp.at[g], sm_recv.at[1 + g], dev(g_=(g + k) % groups)).start()

    def small_dp():
        for k in range(1, groups):
            gg = (g + k) % groups
            sm_copy(sm_grp.at[gg], sm_grp.at[gg], sm_recv.at[1 + gg], across).wait_recv()
        total = sm_grp[0]
        for k in range(1, groups):
            total = total + sm_grp[k]
        sm_dp[z] = total
        for k in range(1, depth):
            sm_copy(sm_dp.at[z], sm_dp.at[z], sm_recv.at[1 + groups + z], dev(z_=(z + k) % depth)).start()

    def head_copy():
        return rcopy(out_small, sm_sec, sm_send.at[1], sm_recv.at[1 + groups + depth], other)

    def small_sec():
        for k in range(1, depth):
            zz = (z + k) % depth
            sm_copy(sm_dp.at[zz], sm_dp.at[zz], sm_recv.at[1 + groups + zz], across).wait_recv()
        total = sm_dp[0]
        for k in range(1, depth):
            total = total + sm_dp[k]
        out_small[...] = total

        @pl.when(~first_section)
        def _():
            head_copy().start()

    def small_head():
        @pl.when(first_section)
        def _():
            head_copy().wait_recv()
            out_small[pl.ds(HEAD_ROW, 1), :] = sm_sec[pl.ds(HEAD_ROW, 1), :]

        @pl.when(~first_section)
        def _():
            head_copy().wait_send()

    def make_inner(i):
        make_up(pick(i - BESIDE["up"], UP_ORDER))

    def make_outer(i):
        at = i - BESIDE["qkv"]
        pl.when(at == 1)(make_attn)

        @pl.when(at != 1)
        def _():
            make_qkv(jnp.where(at == 0, 0, at - 1))

        @pl.when(at == 0)
        def _():
            pltpu.make_async_copy(high, out_gin, io_sem.at[2]).start()

    beside = (
        ("down", make_down, False),
        ("act", act_back, True),
        ("inner", inner_norm, True),
        ("up", make_inner, False),
        ("attend", attend_back, True),
        ("hidden", hidden_step, True),
        ("qkv", make_outer, False),
    )
    lent_parts = (
        lent_start, functools.partial(lent_line, first_line), functools.partial(lent_line, last_lines), lent_done
    )
    smalls = (small_sib, small_grp, small_dp, small_sec, small_head)

    for p in range(last):
        half_down(p)

    @pl.when(first_section)
    def _():
        grad_copy(last).wait_recv()
        outer_norm(last)

    @pl.loop(0, STEPS)
    def _(i):
        for name, part, inside in beside:
            if inside:
                pl.when(first_section & (i == BESIDE[name]))(functools.partial(part, last))
            elif name == "down":
                pl.when(i == BESIDE[name])(part)
            else:
                pl.when((i >= BESIDE[name]) & (i < BESIDE[name] + 4))(functools.partial(part, i))
        for step, part in zip(SMALL_STEPS, smalls):
            pl.when(i == step)(part)
        for step, part in zip(LENT_STEPS, lent_parts):
            pl.when(~first_section & (i == step))(part)
        pl.when(first_section & (i == LENT_BACK))(lent_back)
        for name, at in SLOTS:
            chunks, parts = (X_FIRST, x_stages) if name[0] == "x" else (Z_FIRST, z_stages)
            q = jnp.int32(-1)
            for k, step in enumerate(at):
                q = jnp.where(i == step, k, q)

            runs = q >= 0
            if name[0] == "x" and name[1] != "0":
                runs = runs & ~(first_section & (q == LENT))

            @pl.when(runs)
            def _(q=q, chunks=chunks, part=parts[int(name[1])]):
                part(q, pick(q, chunks))

    count = 1 + (groups - 1) + (depth - 1)
    sent = high.at[pl.ds(0, count * SMALL), :]
    rcopy(sent, sent, sm_send.at[0], sm_recv.at[0], other).wait_send()

    @pl.when(~first_section)
    def _():
        for p in range(pairs):
            grad_copy(p).wait_send()

    pltpu.make_async_copy(high, out_gin, io_sem.at[2]).wait()
    pltpu.make_async_copy(fin, fin, io_sem.at[3]).wait()
    rcopy(s1, s1, r_send.at[0], r_sib.at[0], sibling).wait_send()
    for is_here, chunks in ((first_section, len(X_FIRST) - 1), (~first_section, len(X_FIRST))):

        @pl.when(is_here)
        def _(chunks=chunks):
            part = xr.at[pl.ds(0, chunks)]
            rcopy(part, part, r_send.at[1], r_x.at[0], across).wait_send()
            part = zr.at[pl.ds(0, chunks)]
            rcopy(part, part, r_send.at[2], r_z.at[0, 0], across).wait_send()
            part = fin.at[pl.ds(0, chunks), 0]
            rcopy(part, part, r_send.at[4], r_fin.at[0], across).wait_send()
            if groups > 2:
                part = peers.at[pl.ds(0, chunks), pl.ds(0, groups // 2 - 1)]
                rcopy(part, part, r_send.at[5], r_peer.at[0, 0], across).wait_send()

    rcopy(zw, zw, r_send.at[3], r_z.at[0, 0], across).wait_send()

    @pl.when(first_section)
    def _():
        rcopy(s1.at[0], s1.at[0], k_send.at[0], k_in.at[0], other).wait_send()

    @pl.when(~first_section)
    def _():
        rcopy(rz, rz, k_send.at[1], k_z.at[0], across).wait_send()
        part = rg.at[pl.ds(0, groups - 1)]
        rcopy(part, part, k_send.at[2], k_g.at[0], across).wait_send()
        rcopy(fin.at[0], fin.at[0], k_send.at[3], k_out.at[0], other).wait_send()

    part = xw.at[:, pl.ds(0, groups - 1)]
    rcopy(part, part, r_send.at[6], r_grp.at[0, 0], across).wait_send()


def on_device(groups, depth, embedded, lengths, token_grads, score_grads, w_qkv, w_attn_out, w_up, w_down, biases, gains, head_weight):
    micro, _, seq, _ = embedded.shape
    tokens = micro * seq
    rs = w_qkv.shape[1]
    vmem = pl.BlockSpec(memory_space=pltpu.VMEM)
    smem = pl.BlockSpec(memory_space=pltpu.SMEM)
    hbm = pl.BlockSpec(memory_space=pl.ANY)
    teams = max(groups // 2, 1)
    stages = depth.bit_length() - 1
    out_shape = (
        jax.ShapeDtypeStruct((tokens, D), BF),
        jax.ShapeDtypeStruct((tokens, D), F32),
        jax.ShapeDtypeStruct((rs, 3 * D), BF),
        jax.ShapeDtypeStruct((rs, D), BF),
        jax.ShapeDtypeStruct((rs, FF), BF),
        jax.ShapeDtypeStruct((4 * rs, D), BF),
        jax.ShapeDtypeStruct((SMALL, D), F32),
    )
    nx, nz = len(X_FIRST), len(Z_FIRST)
    scratch = [
        pltpu.VMEM((CHUNKS * D + FF, D), BF),
        pltpu.VMEM((CHUNKS, depth, rs, D), BF),
        pltpu.VMEM((nx, depth, rs, HALF), BF),
        pltpu.VMEM((nx, max(depth - 1, 1), rs, HALF), BF),
        pltpu.VMEM((nz, max(depth - 1, 1), rs, D), BF),
        pltpu.VMEM((nz, groups, rs, D), BF),
        pltpu.VMEM((CHUNKS, 2, rs, HALF), BF),
        pltpu.VMEM((nx, teams, rs, HALF) if groups > 2 else (1, 1, 16, 128), BF),
        pltpu.VMEM((max(depth - 1, 1), rs, D), BF),
        pltpu.VMEM((groups, rs, D), BF),
        pltpu.VMEM((tokens, D), BF),
        pltpu.VMEM((tokens, 3 * D), BF),
        pltpu.VMEM((micro * HEADS, seq, seq), BF),
        pltpu.VMEM((tokens, D), BF),
        pltpu.VMEM((tokens, D), BF),
        pltpu.VMEM((tokens, 1), F32),
        pltpu.VMEM((tokens, D), BF),
        pltpu.VMEM((tokens, FF), BF),
        pltpu.VMEM((tokens, FF), BF),
        pltpu.VMEM((tokens, D), BF),
        pltpu.VMEM((tokens, 1), F32),
        pltpu.VMEM((tokens, D), BF),
        pltpu.VMEM((tokens, D), BF),
        pltpu.VMEM((tokens, D), F32),
        pltpu.VMEM((tokens, D), BF),
        pltpu.VMEM((tokens, 3 * D), BF),
        pltpu.VMEM((SMALL, D), F32),
        pltpu.VMEM((SMALL, D), F32),
        pltpu.VMEM((groups, SMALL, D), F32),
        pltpu.VMEM((depth, SMALL, D), F32),
        pltpu.VMEM((SMALL, D), F32),
        pltpu.VMEM(biases.shape, F32),
        pltpu.VMEM(gains.shape[1:], F32),
        pltpu.VMEM(head_weight.shape, F32),
        pltpu.SemaphoreType.DMA((5,)),
        pltpu.SemaphoreType.DMA((4,)),
        pltpu.SemaphoreType.DMA((CHUNKS, depth)),
        pltpu.SemaphoreType.DMA((CHUNKS, depth)),
        pltpu.SemaphoreType.DMA((CHUNKS,)),
        pltpu.SemaphoreType.DMA((3,)),
        pltpu.SemaphoreType.DMA((RELAY,)),
        pltpu.SemaphoreType.DMA((RELAY, depth)),
        pltpu.SemaphoreType.DMA((RELAY, depth)),
        pltpu.SemaphoreType.DMA((RELAY,)),
        pltpu.SemaphoreType.DMA((4,)),
        pltpu.SemaphoreType.DMA((1,)),
        pltpu.SemaphoreType.DMA((max(stages, 1),)),
        pltpu.SemaphoreType.DMA((groups,)),
        pltpu.SemaphoreType.DMA((1,)),
        pltpu.SemaphoreType.DMA((4,)),
        pltpu.SemaphoreType.DMA((4,)),
        pltpu.SemaphoreType.DMA((4,)),
        pltpu.SemaphoreType.DMA((7,)),
        pltpu.SemaphoreType.DMA((CHUNKS,)),
        pltpu.SemaphoreType.DMA((CHUNKS,)),
        pltpu.SemaphoreType.DMA((CHUNKS, max(stages, 1))),
        pltpu.SemaphoreType.DMA((nz, groups)),
        pltpu.SemaphoreType.DMA((CHUNKS,)),
        pltpu.SemaphoreType.DMA((CHUNKS, teams)),
        pltpu.SemaphoreType.DMA((2,)),
        pltpu.SemaphoreType.DMA((2 + groups + depth,)),
    ]
    state, grad_in, *grads, small = pl.pallas_call(
        functools.partial(kernel, (groups, depth, rs, seq)),
        out_shape=out_shape,
        in_specs=[hbm] * 9 + [smem] * 2,
        out_specs=(hbm,) * 6 + (vmem,),
        scratch_shapes=scratch,
        compiler_params=pltpu.CompilerParams(
            collective_id=0, has_side_effects=True, vmem_limit_bytes=65300 * 1024
        ),
    )(
        embedded.reshape(tokens, D),
        token_grads.reshape(tokens, D),
        w_qkv[0],
        w_attn_out[0],
        w_up[0],
        w_down[0],
        biases,
        gains[0],
        head_weight,
        lengths.reshape(micro),
        score_grads.reshape(micro),
    )
    results = pl.pallas_call(
        hand_out,
        out_shape=[jax.ShapeDtypeStruct(x.shape, x.dtype) for x in (state, grad_in)]
        + [jax.ShapeDtypeStruct(x.shape, F32) for x in grads]
        + [jax.ShapeDtypeStruct(x, F32) for x in ((1, 10 * D), (2, D), (D,))],
        in_specs=[vmem] * 7,
        out_specs=[vmem] * 9,
    )(state, grad_in, *grads, small)
    state, grad_in, g_qkv, g_attn, g_up, g_down, g_bias, g_gain, g_head = results
    return (
        state.reshape(1, micro, 1, seq, D),
        grad_in.reshape(1, micro, 1, seq, D),
        g_qkv[None],
        g_attn[None],
        g_up[None],
        g_down[None],
        g_bias,
        g_gain[None],
        g_head,
    )


def hand_out(state, grad_in, gq, go, gu, gd, small, o_state, o_gin, o_q, o_o, o_u, o_d, o_bias, o_gain, o_head):
    for src, dst in ((state, o_state), (grad_in, o_gin), (gq, o_q), (go, o_o), (gu, o_u), (gd, o_d)):
        dst[...] = src[...].astype(dst.dtype)
    for k in range(10):
        o_bias[:, pl.ds(k * D, D)] = small[pl.ds(k, 1), :]
    o_gain[...] = small[pl.ds(GAIN1, 2), :]
    o_head[...] = small[HEAD_ROW, :]


def solution(mesh):
    return jax.shard_map(
        functools.partial(on_device, mesh.shape["grp"], mesh.shape["dp"] // 2),
        mesh=mesh,
        in_specs=(
            P(None, ("grp", "dp"), None, None),
            P(None, ("grp", "dp")),
            P(None, ("grp", "dp"), None, None),
            P(None, ("grp", "dp")),
            P("section", "dp", None),
            P("section", "dp", None),
            P("section", "dp", None),
            P("section", "dp", None),
            P("section", None),
            P("section", None, None),
            P(),
        ),
        out_specs=(
            P("section", None, ("grp", "dp"), None, None),
            P("section", None, ("grp", "dp"), None, None),
            P("section", "dp", None),
            P("section", "dp", None),
            P("section", "dp", None),
            P("section", "dp", None),
            P("section", None),
            P("section", None, None),
            P(),
        ),
        check_vma=False,
    )
```
